512 devices in a mesh: dom: 128 (over y_hi, x, z), rep: 4 (over y_lo, core).
Axes of the slice: x: 4, y: 8 (y_hi: 4, y_lo: 2; y = y_hi * 2 + y_lo), z: 8, core: 2. Of those that a mesh axis runs over, the one named last changes fastest.
Arguments:
- features: bfloat16 [256, 131072], P('rep', 'dom'), may hold values from -6 to 6
- hub_weight: bfloat16 [128, 128, 64, 128], P('dom'), may hold values from -0.25 to 0.25
- hub_block: int32 [128, 128], P('dom'), may hold values from 0 to 7
- hub_mask: int32 [128, 128], P('dom'), may hold values from 0 to 1, as said below
- tail_rows: int32 [128, 128, 32], P('dom'), may hold values from 0 to 1023
- tail_count: int32 [128, 128], P('dom'), may hold values from 1 to 32, as said below
- tail_target: int32 [128, 128, 32], P('dom'), may hold values from 0 to 1023
- degree: int32 [131072], P('dom'), may hold values from 1 to 8
- w_self: bfloat16 [256, 256], P(None, 'rep'), may hold values from -0.375 to 0.375
- w_neigh: bfloat16 [256, 256], P(None, 'rep'), may hold values from -0.375 to 0.375
- out_bias: float32 [256], P('rep'), may hold values from -3 to 3
- cotangent: bfloat16 [256, 131072], P('rep', 'dom'), may hold values from -6 to 6
Outputs:
- output: bfloat16 [256, 131072], P('rep', 'dom')
- grad_features: float32 [256, 131072], P('rep', 'dom')
- grad_w_self: float32 [256, 256], P(None, 'rep')
- grad_w_neigh: float32 [256, 256], P(None, 'rep')
- grad_bias: float32 [256], P('rep')
The draws below stay inside these ranges and needn't reach their ends.
Inputs may be any that keep to these rules, and one draw needn't show every extreme that they name: `hub_mask`: 1 where the pair's hub tile holds edges, else 0. `tail_count`: every partition sends 32 live rows to some partition, and some partition receives 32 live rows from every partition; slots at or past the count are padding.
All inputs are finite; a program needn't handle non-finite values.
Results may differ from the reference program's by a relative error of at most 0.007.
Values may be sent and summed in bfloat16 or wider, within the bound.
No kernel may reach another device: no remote copies, remote signals or barrier semaphores. Data moves between devices by JAX's collectives and lax.ppermute only.
A program may use at most 64 MiB of HBM per device.

```python
import jax
import jax.numpy as jnp
from jax import lax

F = 256
NP = 1024
HUB = 64
TB = 128
S = 32
NODES = 131072
N_DOM = 128


def draw_hub_mask(key, part):
    key = jax.random.fold_in(key, 11)
    level_key, pick_key = jax.random.split(key)
    levels = jax.random.randint(level_key, (N_DOM, 1), 1, 9)
    picks = jax.random.randint(pick_key, (N_DOM, N_DOM), 0, 8)
    return (picks < levels).astype(jnp.int32)


def draw_tail_count(key, part):
    key = jax.random.fold_in(key, 23)
    key_list = jax.random.split(key, 4)
    levels = jax.random.randint(key_list[0], (1, N_DOM), max(1, S // 4), S + 1)
    draws_raw = jax.random.randint(key_list[1], (N_DOM, N_DOM), 0, 1048576)
    counts = 1 + draws_raw % levels
    full_column = jax.random.randint(key_list[2], (), 0, N_DOM)
    full_slot = jax.random.randint(key_list[3], (N_DOM, 1), 0, N_DOM)
    columns = jnp.arange(N_DOM, dtype=jnp.int32)[None, :]
    counts = jnp.where((columns == full_column) | (columns == full_slot), S, counts)
    return counts.astype(jnp.int32)


def touch_ends(values, stream_key, low, largest):
    extent = values.shape
    spot = [jax.random.randint(jax.random.fold_in(stream_key, axis), (), 0, extent[axis]) for axis in range(len(extent))]
    values = values.at[tuple(spot)].set(low)
    longest = extent.index(max(extent))
    spot[longest] = (spot[longest] + 1) % extent[longest]
    return values.at[tuple(spot)].set(largest)


def level_of(stream_key, extent, pieces, smallest, largest):
    level, own = 1.0, jax.random.fold_in(stream_key, 6)
    for position, parts in pieces:
        heights = jnp.exp(jax.random.uniform(jax.random.fold_in(own, position), (parts,), jnp.float32, smallest / len(pieces), largest / len(pieces)))
        level = level * jnp.repeat(heights, extent[position] // parts).reshape([-1 if axis == position else 1 for axis in range(len(extent))])
    return level


def noise(own_key, shape, scale, bound, shards=(), kind=jnp.bfloat16):
    array = jax.random.normal(own_key, shape, jnp.float32) * scale
    if len(shards) > 0:
        array = level_of(own_key, shape, shards, -0.22, 0.18) * array
    return jnp.clip(array, min=-bound, max=bound).astype(kind)


def setup_inputs(seed: int = 0) -> dict:
    splits = jax.random.split(jax.random.key(seed), 13)
    return {
        "features": noise(splits[0], (F, NODES), 1.0, 6.0, ((0, 4), (1, 128))),
        "hub_weight": noise(splits[1], (N_DOM, N_DOM, HUB, TB), (max(HUB, N_DOM * HUB * TB // (2 * NP))) ** -0.5, 0.25, ((0, 128),)),
        "hub_block": touch_ends(jax.random.randint(splits[2], (N_DOM, N_DOM), 0, NP // TB), jax.random.fold_in(splits[2], 1), 0, (NP // TB) - 1).astype(jnp.int32),
        "hub_mask": draw_hub_mask(jax.random.fold_in(splits[12], 71), 0),
        "tail_rows": touch_ends(jax.random.randint(splits[4], (N_DOM, N_DOM, S), 0, NP), jax.random.fold_in(splits[4], 1), 0, NP - 1).astype(jnp.int32),
        "tail_count": draw_tail_count(jax.random.fold_in(splits[12], 71), 0),
        "tail_target": touch_ends(jax.random.randint(splits[6], (N_DOM, N_DOM, S), 0, NP), jax.random.fold_in(splits[6], 1), 0, NP - 1).astype(jnp.int32),
        "degree": touch_ends(jax.random.randint(splits[7], (NODES,), 1, 9), jax.random.fold_in(splits[7], 1), 1, 8).astype(jnp.int32),
        "w_self": noise(splits[8], (F, F), F ** -0.5, 0.375, ((1, 4),)),
        "w_neigh": noise(splits[9], (F, F), F ** -0.5, 0.375, ((1, 4),)),
        "out_bias": noise(splits[10], (F,), 0.5, 3.0, ((0, 4),), jnp.float32),
        "cotangent": noise(splits[11], (F, NODES), 1.0, 6.0, ((0, 4), (1, 128))),
    }


def silu_slope(pre):
    sigma = jax.nn.sigmoid(pre)
    return sigma * (1.0 + pre * (1.0 - sigma))


def reference(features, hub_weight, hub_block, hub_mask, tail_rows, tail_count, tail_target, degree, w_self, w_neigh, out_bias, cotangent):
    width = features.shape[0]
    highest = lax.Precision.HIGHEST
    parts_f = features.reshape(width, N_DOM, NP).transpose(1, 0, 2).astype(jnp.float32)
    hub_feats = parts_f[:, :, :HUB]
    block_ids = jnp.arange(NP // TB, dtype=jnp.int32)

    def hub_into(args):
        tile_set, rows_of, live_of = args
        products = jnp.einsum("qfj,qjt->qft", hub_feats, tile_set.astype(jnp.float32), precision=highest)
        placing = ((rows_of[:, None] == block_ids[None, :]) & (live_of[:, None] > 0)).astype(jnp.float32)
        return jnp.einsum("qft,qb->fbt", products, placing, precision=highest).reshape(width, NP)

    hub_sum = lax.map(hub_into, (hub_weight, hub_block, hub_mask))
    slot_ids = jnp.arange(S, dtype=jnp.int32)
    live_all = slot_ids[None, None, :] < tail_count[:, :, None]

    def tail_into(args):
        rows_from, live_from, targets = args
        index_full = jnp.broadcast_to(rows_from[:, None, :], (N_DOM, width, S)).astype(jnp.int32)
        values = jnp.take_along_axis(parts_f, index_full, axis=2)
        values = jnp.where(live_from[:, None, :], values, 0.0)
        flat = values.transpose(1, 0, 2).reshape(width, N_DOM * S)
        return jnp.zeros((width, NP), jnp.float32).at[:, targets.reshape(-1)].add(flat)

    tail_sum = lax.map(tail_into, (tail_rows.transpose(1, 0, 2), live_all.transpose(1, 0, 2), tail_target))
    degrees = degree.reshape(N_DOM, NP).astype(jnp.float32)
    mixed = (hub_sum + tail_sum / degrees[:, None, :]).astype(jnp.bfloat16)
    mixed_all = mixed.transpose(1, 0, 2).reshape(width, N_DOM * NP)
    pre = jnp.dot(w_self.T, features, preferred_element_type=jnp.float32) + jnp.dot(w_neigh.T, mixed_all, preferred_element_type=jnp.float32) + out_bias[:, None]
    output = jax.nn.silu(pre).astype(jnp.bfloat16)
    d_pre = (cotangent.astype(jnp.float32) * silu_slope(pre)).astype(jnp.bfloat16)
    grad_w_self = jnp.dot(features, d_pre.T, preferred_element_type=jnp.float32)
    grad_w_neigh = jnp.dot(mixed_all, d_pre.T, preferred_element_type=jnp.float32)
    grad_bias = jnp.sum(d_pre.astype(jnp.float32), axis=1)
    direct = jnp.dot(w_self, d_pre, preferred_element_type=jnp.float32)
    mixed_grad = jnp.dot(w_neigh, d_pre, preferred_element_type=jnp.float32).astype(jnp.bfloat16)
    grad_parts = mixed_grad.reshape(width, N_DOM, NP).transpose(1, 0, 2).astype(jnp.float32)

    def tail_back(args):
        targets_to, live_to, rows_of = args
        index_full = jnp.broadcast_to(targets_to[:, None, :], (N_DOM, width, S)).astype(jnp.int32)
        picked = jnp.take_along_axis(grad_parts, index_full, axis=2)
        slot_degree = jnp.take_along_axis(degrees, targets_to.astype(jnp.int32), axis=1)
        values = jnp.where(live_to[:, None, :], picked / slot_degree[:, None, :], 0.0)
        flat = values.transpose(1, 0, 2).reshape(width, N_DOM * S)
        return jnp.zeros((width, NP), jnp.float32).at[:, rows_of.reshape(-1)].add(flat)

    tail_grad = lax.map(tail_back, (tail_target.transpose(1, 0, 2), live_all, tail_rows))
    grad_blocks = grad_parts.reshape(N_DOM, width, NP // TB, TB)

    def hub_back(args):
        tile_set, rows_of, live_of = args
        index_full = jnp.broadcast_to(rows_of[:, None, None, None], (N_DOM, width, 1, TB)).astype(jnp.int32)
        chosen = jnp.take_along_axis(grad_blocks, index_full, axis=2)[:, :, 0, :]
        chosen = chosen * live_of.astype(jnp.float32)[:, None, None]
        return jnp.einsum("pft,pjt->fj", chosen, tile_set.astype(jnp.float32), precision=highest)

    hub_grad = lax.map(hub_back, (hub_weight.transpose(1, 0, 2, 3), hub_block.T, hub_mask.T))
    total_parts = direct.reshape(width, N_DOM, NP).transpose(1, 0, 2) + tail_grad + jnp.pad(hub_grad, ((0, 0), (0, 0), (0, NP - HUB)))
    grad_features = total_parts.transpose(1, 0, 2).reshape(width, N_DOM * NP)
    return output, grad_features, grad_w_self, grad_w_neigh, grad_bias
```

```python
import jax
import jax.numpy as jnp
from jax import lax
from jax.sharding import PartitionSpec as P

BF = jnp.bfloat16
F32 = jnp.float32
BOTH_ROWS = (((0,), (0,)), ((), ()))
BOTH_COLS = (((1,), (1,)), ((), ()))


def mm(a, b, dims):
    return lax.dot_general(a, b, dims, preferred_element_type=F32)


def swap(pieces, axis):
    return lax.all_to_all(pieces, axis, split_axis=0, concat_axis=0, tiled=True)


def high_low(values):
    high = lax.reduce_precision(values, 8, 7)
    return jnp.concatenate([high.astype(BF), (values - high).astype(BF)], axis=1)


def one_hot_rows(index, total):
    return (index[:, None] == lax.broadcasted_iota(jnp.int32, (1, total), 1)).astype(BF)


def slot_groups(index, groups):
    parts, slots = index.shape
    part_len = slots // groups
    return [index[:, g * part_len : (g + 1) * part_len].reshape(-1) for g in range(groups)]


def gather_slots(source, index_groups, parts):
    pieces = [
        mm(one_hot_rows(index, source.shape[1]), source, BOTH_COLS).astype(BF)
        for index in index_groups
    ]
    return jnp.concatenate(pieces, axis=1).reshape(parts, -1, 128)


def spread_slots(arrived, index_groups, width, nodes):
    flat = arrived.reshape(-1, 128)
    total = 0.0
    for g, index in enumerate(index_groups):
        total = total + mm(flat[:, g * width : (g + 1) * width], one_hot_rows(index, nodes), BOTH_ROWS)
    return total


def local(
    features,
    hub_weight,
    hub_block,
    hub_mask,
    tail_rows,
    tail_count,
    tail_target,
    degree,
    w_self,
    w_neigh,
    out_bias,
    cotangent,
):
    width, nodes = features.shape
    tiles = hub_weight[0]
    parts, hubs, tile_len = tiles.shape
    slots = tail_rows.shape[2]
    groups = 128 // width
    hub_len = hubs // groups
    blocks = nodes // tile_len
    full_width = w_self.shape[0]
    my_rep = lax.axis_index("rep")

    hub_t = features[:, :hubs].T
    hub_piece = jnp.concatenate(
        [hub_t[g * hub_len : (g + 1) * hub_len] for g in range(groups)], axis=1
    )
    hub_all = swap(jnp.broadcast_to(hub_piece[None], (parts, hub_len, 128)), "dom")

    slot_live = jnp.arange(slots, dtype=jnp.int32)[None, :] < tail_count[0][:, None]
    send_groups = slot_groups(jnp.where(slot_live, tail_rows[0], -1), groups)
    recv_groups = slot_groups(tail_target[0], groups)
    arrived = swap(gather_slots(features, send_groups, parts), "dom")

    early = lax.all_gather(
        jnp.concatenate([features, w_self.T, w_neigh.T], axis=1), "rep", axis=0, tiled=True
    )
    full_feat = early[:, :nodes]
    own_rows = my_rep * width
    w_self_rows = lax.dynamic_slice_in_dim(early[:, nodes : nodes + full_width], own_rows, width, 1)
    w_neigh_rows = lax.dynamic_slice_in_dim(early[:, nodes + full_width :], own_rows, width, 1)
    pre_self = mm(w_self, full_feat, BOTH_ROWS) + out_bias[:, None]

    live = hub_mask[0] > 0
    in_block = (hub_block[0][:, None] == jnp.arange(blocks, dtype=jnp.int32)[None, :]) & live[:, None]
    hub_out = 0.0
    for g in range(groups):
        rows = hub_all[:, :, g * width : (g + 1) * width]
        placed = jnp.where(in_block[:, None, :, None], rows[:, :, None, :], jnp.zeros((), BF))
        hub_out = hub_out + mm(
            placed.reshape(parts * hub_len, blocks * width),
            tiles[:, g * hub_len : (g + 1) * hub_len, :].reshape(parts * hub_len, tile_len),
            BOTH_ROWS,
        )
    hub_sum = jnp.concatenate([hub_out[b * width : (b + 1) * width] for b in range(blocks)], axis=1)
    tail_sum = spread_slots(arrived, recv_groups, width, nodes)
    degree_float = degree.astype(F32)[None, :]
    mixed = (hub_sum + tail_sum / degree_float).astype(BF)

    full_mixed = lax.all_gather(mixed, "rep", axis=0, tiled=True)
    pre = pre_self + mm(w_neigh, full_mixed, BOTH_ROWS)
    sigma = jax.nn.sigmoid(pre)
    output = (pre * sigma).astype(BF)
    d_pre = (cotangent.astype(F32) * (sigma * (1.0 + pre * (1.0 - sigma)))).astype(BF)

    full_d = lax.all_gather(d_pre, "rep", axis=0, tiled=True)
    mixed_grad = mm(w_neigh_rows, full_d, BOTH_ROWS).astype(BF)
    direct = mm(w_self_rows, full_d, BOTH_ROWS)

    half = full_width // groups
    grads = []
    for source in (full_feat, full_mixed):
        grad = mm(source, d_pre, BOTH_COLS)
        grads += [
            jnp.concatenate([grad[g * half : (g + 1) * half] for g in range(groups)], axis=1)
        ]
    bias_part = jnp.sum(d_pre.astype(F32), axis=1)
    bias_rows = jnp.broadcast_to(jnp.tile(bias_part, groups)[None, None], (parts, 2, 128))
    grad_rows = jnp.concatenate([g.reshape(parts, -1, 128) for g in grads] + [bias_rows], axis=1)
    kinds = grad_rows.shape[1]

    scaled = (mixed_grad.astype(F32) / degree_float).astype(BF)
    tail_send = gather_slots(scaled, recv_groups, parts)
    tail_len = tail_send.shape[1]
    first = swap(jnp.concatenate([tail_send, high_low(grad_rows)], axis=1), "dom")

    by_block = mixed_grad.reshape(width, blocks, tile_len).transpose(1, 0, 2)
    chosen = jnp.take(by_block, hub_block[0], axis=0) * live.astype(BF)[:, None, None]
    hub_terms = jnp.einsum("qjt,qft->qjf", tiles, chosen, preferred_element_type=F32).astype(BF)
    hub_send = jnp.concatenate(
        [hub_terms[:, g * hub_len : (g + 1) * hub_len] for g in range(groups)], axis=2
    )
    sums = jnp.sum(first[:, tail_len:].astype(F32), axis=0)
    sums = sums[:kinds] + sums[kinds:]
    grad_bias = sums[kinds - 1, :width]
    sum_rows = jnp.broadcast_to(high_low(sums[None]), (parts, 2 * kinds, 128))
    second = swap(jnp.concatenate([hub_send, sum_rows], axis=1), "dom")

    tail_grad = spread_slots(first[:, :tail_len], send_groups, width, nodes)
    all_sums = second[:, hub_len:].astype(F32)
    all_sums = all_sums[:, : kinds - 2] + all_sums[:, kinds : 2 * kinds - 2]
    grad_w_self, grad_w_neigh = [
        jnp.concatenate([rows[:, g * width : (g + 1) * width] for g in range(groups)], axis=0)
        for rows in jnp.split(all_sums, 2, axis=1)
        for rows in [rows.reshape(half, 128)]
    ]
    hub_back = jnp.sum(second[:, :hub_len].astype(F32), axis=0)
    hub_grad = jnp.concatenate(
        [hub_back[:, g * width : (g + 1) * width] for g in range(groups)], axis=0
    ).T
    grad_features = direct + tail_grad + jnp.pad(hub_grad, ((0, 0), (0, nodes - hubs)))
    return (output, grad_features, grad_w_self, grad_w_neigh, grad_bias)


def solution(mesh):
    in_specs = (
        P("rep", "dom"),
        P("dom", None, None, None),
        P("dom", None),
        P("dom", None),
        P("dom", None, None),
        P("dom", None),
        P("dom", None, None),
        P("dom"),
        P(None, "rep"),
        P(None, "rep"),
        P("rep"),
        P("rep", "dom"),
    )
    out_specs = (P("rep", "dom"), P("rep", "dom"), P(None, "rep"), P(None, "rep"), P("rep"))
    return jax.shard_map(local, mesh=mesh, in_specs=in_specs, out_specs=out_specs, check_vma=False)
```

```python
from functools import partial

import jax
import jax.numpy as jnp
from jax import lax
from jax.experimental import pallas as pl
from jax.experimental.pallas import tpu as pltpu
from jax.sharding import Mesh
from jax.sharding import PartitionSpec as P

BF = jnp.bfloat16
F32 = jnp.float32
BOTH_ROWS = (((0,), (0,)), ((), ()))
BOTH_COLS = (((1,), (1,)), ((), ()))
DOM = ("yh", "x", "z")
PLANE = ("yh", "z")
REP = ("yl", "core")


def mm(a, b, dims):
    return lax.dot_general(a, b, dims, preferred_element_type=F32)


def swap(pieces, axis):
    return lax.all_to_all(pieces, axis, split_axis=0, concat_axis=0, tiled=True)


def high_low(values):
    high = lax.reduce_precision(values, 8, 7)
    return jnp.concatenate([high.astype(BF), (values - high).astype(BF)], axis=1)


def shift(values, axis, step):
    size = lax.axis_size(axis)
    return lax.ppermute(values, axis, [(i, (i + step) % size) for i in range(size)])


def gather_rep(values):
    first = lax.axis_index("yl") == 0
    other = shift(values, "yl", 1)
    mine = jnp.stack([jnp.where(first, values, other), jnp.where(first, other, values)])
    theirs = shift(mine, "core", 1)
    first = lax.axis_index("core") == 0
    both = jnp.stack([jnp.where(first, mine, theirs), jnp.where(first, theirs, mine)], axis=1)
    return both.reshape(-1, values.shape[1])


def tile_index(x_ref, k, sizes, yh, z, sign):
    x_size, z_size = sizes
    x = lax.rem(x_ref[0] + (sign * k) % x_size, x_size)
    return (yh * x_size + x) * z_size + z


def fold_kernel(sizes, x_ref, dest_ref, *refs):
    *hub_refs, tile_ref, out_ref, total = refs
    half = hub_refs[0].shape[1]
    lanes = lax.broadcasted_iota(jnp.int32, (half, 128), 1)
    first = (lanes < 64).astype(F32).astype(BF)
    second = (lanes >= 64).astype(F32).astype(BF)
    total[...] = jnp.zeros_like(total)
    x_size, z_size = sizes
    for k, hub_ref in enumerate(hub_refs):

        @pl.loop(0, hub_ref.shape[0] // z_size)
        def _(yh):
            for z in range(z_size):
                tile = tile_index(x_ref, k, sizes, yh, z, -1)
                rows = hub_ref[yh * z_size + z]
                weights = tile_ref[tile]
                product = jnp.dot(
                    jnp.concatenate([rows * first, rows * second], axis=0),
                    jnp.concatenate([weights, weights], axis=0),
                    preferred_element_type=F32,
                )
                dest = dest_ref[tile]
                total[dest] = total[dest] + product

    for b in range(total.shape[0] - 1):
        out_ref[:, b * 128 : (b + 1) * 128] = total[b]


def fold_hubs(x_index, dest, hubs, tiles, sizes, blocks):
    width = 2 * hubs[0].shape[1]
    smem = pl.BlockSpec(memory_space=pltpu.SMEM)
    vmem = pl.BlockSpec(memory_space=pltpu.VMEM)
    return pl.pallas_call(
        partial(fold_kernel, sizes),
        out_shape=jax.ShapeDtypeStruct((width, blocks * 128), F32),
        in_specs=[smem, smem] + [vmem] * (len(hubs) + 1),
        out_specs=vmem,
        scratch_shapes=[pltpu.VMEM((blocks + 1, width, 128), F32)],
        compiler_params=pltpu.CompilerParams(vmem_limit_bytes=24 * 1024 * 1024),
        cost_estimate=pl.CostEstimate(
            flops=4 * tiles.size * width, bytes_accessed=8 * 1024 * 1024, transcendentals=0
        ),
        name="hub_sums",
    )(x_index, dest, *hubs, tiles)


def hub_grad_kernel(sizes, x_ref, dest_ref, grad_ref, tile_ref, out_ref, blocked):
    blocks = blocked.shape[0] - 1
    for b in range(blocks):
        blocked[b] = grad_ref[:, b * 128 : (b + 1) * 128]
    blocked[blocks] = jnp.zeros_like(blocked[blocks])
    half = out_ref.shape[2]
    first = lax.broadcasted_iota(jnp.int32, (half, 128), 1) < 64
    x_size, z_size = sizes
    for k in range(x_size):

        @pl.loop(0, out_ref.shape[1] // z_size)
        def _(yh):
            for z in range(z_size):
                tile = tile_index(x_ref, k, sizes, yh, z, 1)
                weights = tile_ref[tile]
                product = mm(
                    blocked[dest_ref[tile]],
                    jnp.concatenate([weights, weights], axis=0),
                    BOTH_COLS,
                )
                out_ref[k, yh * z_size + z] = jnp.where(
                    first, product[:half], product[half:]
                ).astype(BF)


def hub_grad_terms(x_index, dest, grad, tiles, sizes, blocks):
    width = grad.shape[0]
    parts = tiles.shape[0]
    smem = pl.BlockSpec(memory_space=pltpu.SMEM)
    vmem = pl.BlockSpec(memory_space=pltpu.VMEM)
    return pl.pallas_call(
        partial(hub_grad_kernel, sizes),
        out_shape=jax.ShapeDtypeStruct((sizes[0], parts // sizes[0], width // 2, 128), BF),
        in_specs=[smem, smem, vmem, vmem],
        out_specs=vmem,
        scratch_shapes=[pltpu.VMEM((blocks + 1, width, 128), BF)],
        compiler_params=pltpu.CompilerParams(vmem_limit_bytes=24 * 1024 * 1024),
        cost_estimate=pl.CostEstimate(
            flops=4 * tiles.size * width, bytes_accessed=8 * 1024 * 1024, transcendentals=0
        ),
        name="hub_grad_terms",
    )(x_index, dest, grad, tiles)


def one_hot_rows(index, total):
    return (index[:, None] == lax.broadcasted_iota(jnp.int32, (1, total), 1)).astype(BF)


def slot_groups(index, groups):
    parts, slots = index.shape
    part_len = slots // groups
    return [index[:, g * part_len : (g + 1) * part_len].reshape(-1) for g in range(groups)]


def gather_slots(source, index_groups, parts):
    pieces = [
        mm(one_hot_rows(index, source.shape[1]), source, BOTH_COLS).astype(BF)
        for index in index_groups
    ]
    return jnp.concatenate(pieces, axis=1).reshape(parts, -1, 128)


def spread_slots(arrived, index_groups, width, nodes):
    flat = arrived.reshape(-1, 128)
    total = 0.0
    for g, index in enumerate(index_groups):
        total = total + mm(flat[:, g * width : (g + 1) * width], one_hot_rows(index, nodes), BOTH_ROWS)
    return total


def local(
    features,
    hub_weight,
    hub_block,
    hub_mask,
    tail_rows,
    tail_count,
    tail_target,
    degree,
    w_self,
    w_neigh,
    out_bias,
    cotangent,
):
    width, nodes = features.shape
    tiles = hub_weight[0]
    parts, hubs, tile_len = tiles.shape
    slots = tail_rows.shape[2]
    groups = 128 // width
    half_width = width // 2
    blocks = nodes // tile_len
    full_width = w_self.shape[0]
    x_size, z_size = lax.axis_size("x"), lax.axis_size("z")
    sizes = (x_size, z_size)
    plane = parts // x_size
    x_index = lax.axis_index("x")[None]
    hub_dest = jnp.where(hub_mask[0] > 0, hub_block[0], blocks)

    hub_piece = jnp.concatenate([features[:half_width, :hubs], features[half_width:, :hubs]], axis=1)
    hub_plane = swap(jnp.broadcast_to(hub_piece[None], (plane, half_width, 128)), PLANE)
    hub_all = [hub_plane] + [shift(hub_plane, "x", k) for k in range(1, x_size)]

    slot_live = jnp.arange(slots, dtype=jnp.int32)[None, :] < tail_count[0][:, None]
    send_groups = slot_groups(jnp.where(slot_live, tail_rows[0], -1), groups)
    recv_groups = slot_groups(tail_target[0], groups)
    arrived = swap(gather_slots(features, send_groups, parts), DOM)

    early = gather_rep(jnp.concatenate([features, w_self.T, w_neigh.T], axis=1))
    full_feat = early[:, :nodes]
    own_rows = lax.axis_index(REP) * width
    w_self_rows = lax.dynamic_slice_in_dim(early[:, nodes : nodes + full_width], own_rows, width, 1)
    w_neigh_rows = lax.dynamic_slice_in_dim(early[:, nodes + full_width :], own_rows, width, 1)
    pre_self = mm(w_self, full_feat, BOTH_ROWS) + out_bias[:, None]

    hub_sum = fold_hubs(x_index, hub_dest, hub_all, tiles, sizes, blocks)
    tail_sum = spread_slots(arrived, recv_groups, width, nodes)
    degree_float = degree.astype(F32)[None, :]
    mixed = (hub_sum + tail_sum / degree_float).astype(BF)

    full_mixed = lax.all_gather(mixed, REP, axis=0, tiled=True)
    pre = pre_self + mm(w_neigh, full_mixed, BOTH_ROWS)
    sigma = jax.nn.sigmoid(pre)
    output = (pre * sigma).astype(BF)
    d_pre = (cotangent.astype(F32) * (sigma * (1.0 + pre * (1.0 - sigma)))).astype(BF)

    full_d = lax.all_gather(d_pre, REP, axis=0, tiled=True)
    mixed_grad = mm(w_neigh_rows, full_d, BOTH_ROWS).astype(BF)
    direct = mm(w_self_rows, full_d, BOTH_ROWS)

    half = full_width // groups
    grads = []
    for source in (full_feat, full_mixed):
        grad = mm(source, d_pre, BOTH_COLS)
        grads += [
            jnp.concatenate([grad[g * half : (g + 1) * half] for g in range(groups)], axis=1)
        ]
    bias_part = jnp.sum(d_pre.astype(F32), axis=1)
    bias_rows = jnp.broadcast_to(jnp.tile(bias_part, groups)[None, None], (parts, 2, 128))
    grad_rows = jnp.concatenate([g.reshape(parts, -1, 128) for g in grads] + [bias_rows], axis=1)
    kinds = grad_rows.shape[1]

    scaled = (mixed_grad.astype(F32) / degree_float).astype(BF)
    tail_send = gather_slots(scaled, recv_groups, parts)
    tail_len = tail_send.shape[1]
    first = swap(jnp.concatenate([tail_send, high_low(grad_rows)], axis=1), DOM)

    hub_terms = hub_grad_terms(x_index, hub_dest, mixed_grad, tiles, sizes, blocks)
    hub_x = hub_terms[0].astype(F32)
    for k in range(1, x_size):
        hub_x = hub_x + shift(hub_terms[k], "x", k).astype(F32)
    sums = jnp.sum(first[:, tail_len:].astype(F32), axis=0)
    sums = sums[:kinds] + sums[kinds:]
    grad_bias = sums[kinds - 1, :width]
    sum_rows = jnp.broadcast_to(high_low(sums[None]), (plane, 2 * kinds, 128))
    second = swap(jnp.concatenate([hub_x.astype(BF), sum_rows], axis=1), PLANE)

    tail_grad = spread_slots(first[:, :tail_len], send_groups, width, nodes)
    own_sums = second[:, half_width:].astype(F32)
    own_sums = own_sums[:, : kinds - 2] + own_sums[:, kinds : 2 * kinds - 2]
    far_sums = jnp.stack([own_sums] + [shift(own_sums, "x", k) for k in range(1, x_size)])
    order = lax.rem(x_index[0] + x_size - jnp.arange(x_size, dtype=jnp.int32), x_size)
    all_sums = jnp.take(far_sums, order, axis=0).reshape(x_size, -1, z_size, kinds - 2, 128)
    all_sums = all_sums.transpose(1, 0, 2, 3, 4).reshape(parts, kinds - 2, 128)
    grad_w_self, grad_w_neigh = [
        jnp.concatenate([rows[:, g * width : (g + 1) * width] for g in range(groups)], axis=0)
        for rows in jnp.split(all_sums, 2, axis=1)
        for rows in [rows.reshape(half, 128)]
    ]
    hub_back = jnp.sum(second[:, :half_width].astype(F32), axis=0)
    hub_grad = jnp.concatenate([hub_back[:, :hubs], hub_back[:, hubs:]], axis=0)
    grad_features = direct + tail_grad + jnp.pad(hub_grad, ((0, 0), (0, nodes - hubs)))
    return (output, grad_features, grad_w_self, grad_w_neigh, grad_bias)


def solution(mesh):
    grid = (4, 4, mesh.shape["dom"] // 16, 2, 2)
    parted = Mesh(mesh.devices.reshape(grid), DOM + REP)
    in_specs = (
        P(REP, DOM),
        P(DOM, None, None, None),
        P(DOM, None),
        P(DOM, None),
        P(DOM, None, None),
        P(DOM, None),
        P(DOM, None, None),
        P(DOM),
        P(None, REP),
        P(None, REP),
        P(REP),
        P(REP, DOM),
    )
    out_specs = (P(REP, DOM), P(REP, DOM), P(None, REP), P(None, REP), P(REP))
    return jax.shard_map(local, mesh=parted, in_specs=in_specs, out_specs=out_specs, check_vma=False)
```

```python
from functools import partial

import jax
import jax.numpy as jnp
from jax import lax
from jax.experimental import pallas as pl
from jax.experimental.pallas import tpu as pltpu
from jax.sharding import Mesh
from jax.sharding import PartitionSpec as P

BF = jnp.bfloat16
F32 = jnp.float32
BOTH_ROWS = (((0,), (0,)), ((), ()))
BOTH_COLS = (((1,), (1,)), ((), ()))
DOM = ("yh", "x", "z")
PLANE = ("yh", "z")
REP = ("yl", "core")
SMEM = pl.BlockSpec(memory_space=pltpu.SMEM)
VMEM = pl.BlockSpec(memory_space=pltpu.VMEM)
MIB = 1024 * 1024


def mm(a, b, dims):
    return lax.dot_general(a, b, dims, preferred_element_type=F32)


def swap(pieces, axis):
    return lax.all_to_all(pieces, axis, split_axis=0, concat_axis=0, tiled=True)


def shift(values, axis, step):
    size = lax.axis_size(axis)
    return lax.ppermute(values, axis, [(i, (i + step) % size) for i in range(size)])


def gather_rep(values):
    first = lax.axis_index("yl") == 0
    other = shift(values, "yl", 1)
    mine = jnp.stack([jnp.where(first, values, other), jnp.where(first, other, values)])
    theirs = shift(mine, "core", 1)
    first = lax.axis_index("core") == 0
    both = jnp.stack([jnp.where(first, mine, theirs), jnp.where(first, theirs, mine)], axis=1)
    return both.reshape(-1, values.shape[1])


def call(kernel, out_shape, in_specs, scratch, name, flops, mib):
    outs = VMEM if isinstance(out_shape, jax.ShapeDtypeStruct) else [VMEM] * len(out_shape)
    return pl.pallas_call(
        kernel,
        out_shape=out_shape,
        in_specs=in_specs,
        out_specs=outs,
        scratch_shapes=scratch,
        compiler_params=pltpu.CompilerParams(vmem_limit_bytes=32 * MIB),
        cost_estimate=pl.CostEstimate(flops=flops, bytes_accessed=mib * MIB, transcendentals=0),
        name=name,
    )


def high_low(values, axis):
    high = lax.reduce_precision(values, 8, 7)
    return jnp.concatenate([high.astype(BF), (values - high).astype(BF)], axis=axis)


def slot_rows(index):
    parts, slots = index.shape
    return index.reshape(parts, 2, slots // 2).transpose(1, 0, 2).reshape(2, -1)


def pick_slots(index_ref, source, out_ref):
    width, nodes = source.shape
    low_size = 256
    high_size = nodes // low_size
    split = jnp.concatenate(
        [source[:, i * low_size : (i + 1) * low_size] for i in range(high_size)], axis=0
    )
    step = 256
    rows = out_ref.shape[1]
    low_ids = lax.broadcasted_iota(jnp.int32, (low_size, step), 0)
    for start in range(0, index_ref.shape[1], step):
        halves = []
        for h in range(2):
            index = index_ref[h : h + 1, start : start + step]
            hits = jnp.where(low_ids == (index & (low_size - 1)), 1.0, 0.0).astype(BF)
            found = jnp.dot(split, hits, preferred_element_type=F32)
            high = jnp.broadcast_to(index >> 8, (width, step))
            kept = jnp.zeros((width, step), F32)
            for i in range(high_size):
                kept = jnp.where(high == i, found[i * width : (i + 1) * width], kept)
            halves.append(kept)
        block = jnp.concatenate(halves, axis=0).T
        first = start // rows
        out_ref[first : first + step // rows] = block.reshape(step // rows, rows, 128).astype(BF)


def gather_kernel(index_ref, source_ref, out_ref):
    pick_slots(index_ref, source_ref[...], out_ref)


def gather_slots(index, source, parts, slots):
    return call(
        gather_kernel,
        jax.ShapeDtypeStruct((parts, slots // 2, 128), BF),
        [VMEM, VMEM],
        [],
        "tail_rows_out",
        2 * parts * slots * 256 * 256,
        2,
    )(index, source)


def back_kernel(index_ref, weight_ref, d_ref, degree_ref, grad_ref, out_ref):
    grad = jnp.dot(weight_ref[...], d_ref[...], preferred_element_type=F32).astype(BF)
    grad_ref[...] = grad
    scaled = (grad.astype(F32) / degree_ref[...].astype(F32)).astype(BF)
    pick_slots(index_ref, scaled, out_ref)


def back_gather(index, weight, d_full, degree, parts, slots):
    width, nodes = weight.shape[0], d_full.shape[1]
    return call(
        back_kernel,
        [
            jax.ShapeDtypeStruct((width, nodes), BF),
            jax.ShapeDtypeStruct((parts, slots // 2, 128), BF),
        ],
        [VMEM] * 4,
        [],
        "mixed_grad_rows_out",
        2 * parts * slots * 256 * 256,
        2,
    )(index, weight, d_full, degree)


def sum_slots(index_ref, arrived_ref, rows, start, size):
    parts = arrived_ref.shape[0]
    flat = arrived_ref[:, :rows, :].reshape(parts * rows, 128)
    ids = lax.broadcasted_iota(jnp.int32, (size, parts * rows), 0) + start
    sums = []
    for h in range(2):
        hits = jnp.where(ids == index_ref[h : h + 1, :], 1.0, 0.0).astype(BF)
        sums.append(jnp.dot(hits, flat, preferred_element_type=F32))
    return sums[0].T[:64] + sums[1].T[64:]


def mixed_kernel(rows, index_ref, arrived_ref, hub_ref, degree_ref, out_ref):
    size = 256
    for start in range(0, out_ref.shape[1], size):
        at = slice(start, start + size)
        tail = sum_slots(index_ref, arrived_ref, rows, start, size)
        out_ref[:, at] = (hub_ref[:, at] + tail / degree_ref[:, at].astype(F32)).astype(BF)


def mixed_sums(index, arrived, hub_sum, degree):
    parts, rows, _ = arrived.shape
    width, nodes = hub_sum.shape
    return call(
        partial(mixed_kernel, rows),
        jax.ShapeDtypeStruct((width, nodes), BF),
        [VMEM] * 4,
        [],
        "mixed",
        4 * parts * rows * nodes * 128,
        2,
    )(index, arrived, hub_sum, degree)


def tail_grad_kernel(rows, index_ref, arrived_ref, direct_ref, out_ref):
    size = 256
    for start in range(0, out_ref.shape[1], size):
        at = slice(start, start + size)
        tail = sum_slots(index_ref, arrived_ref, rows, start, size)
        out_ref[:, at] = direct_ref[:, at] + tail


def tail_grads(index, arrived, direct, rows):
    parts = arrived.shape[0]
    width, nodes = direct.shape
    return call(
        partial(tail_grad_kernel, rows),
        jax.ShapeDtypeStruct((width, nodes), F32),
        [VMEM] * 3,
        [],
        "tail_grads",
        4 * parts * rows * nodes * 128,
        2,
    )(index, arrived, direct)


def weight_kernel(feat_ref, mixed_ref, d_ref, out_ref):
    d_pre = d_ref[...]
    full = feat_ref.shape[0]
    half = full // 2
    grads = []
    for ref in (feat_ref, mixed_ref):
        grad = mm(ref[...], d_pre, BOTH_COLS)
        grads.append(jnp.concatenate([grad[:half], grad[half:]], axis=1))
    grads = jnp.concatenate(grads, axis=0)
    ones = jnp.ones((8, d_pre.shape[1]), BF)
    bias = mm(ones, d_pre, BOTH_COLS)
    bias = jnp.concatenate([bias, bias], axis=1)
    high = grads.astype(BF).astype(F32)
    low = (grads - high).reshape(-1, 8, 128)
    high = high.reshape(-1, 8, 128)
    bias_high = bias.astype(BF).astype(F32)
    place = lax.broadcasted_iota(jnp.int32, low.shape, 1)
    rest = jnp.where(place == 4, bias_high[None], (bias - bias_high)[None])
    made = []
    for j in range(4):
        up = high if j == 0 else pltpu.roll(high, 8 - 2 * j, 1)
        down = low if j == 1 else pltpu.roll(low, (10 - 2 * j) % 8, 1)
        made.append(jnp.where(place < 2, up, jnp.where(place < 4, down, rest)))
    out_ref[:, 0] = jnp.concatenate(made[:2], axis=1).astype(BF)
    out_ref[:, 1] = jnp.concatenate(made[2:], axis=1).astype(BF)


def weight_rows(full_feat, full_mixed, d_pre, parts):
    full = full_feat.shape[0]
    made = call(
        weight_kernel,
        jax.ShapeDtypeStruct((full // 8, 2, 16, 128), BF),
        [VMEM] * 3,
        [],
        "weight_grad_rows",
        4 * full_feat.size * d_pre.shape[0],
        2,
    )(full_feat, full_mixed, d_pre)
    return made.reshape(full // 2, 8, 128)


def tile_index(x_ref, k, sizes, yh, z, sign):
    x_size, z_size = sizes
    x = lax.rem(x_ref[0] + (sign * k) % x_size, x_size)
    return (yh * x_size + x) * z_size + z


def fold_kernel(steps, sizes, has_base, x_ref, dest_ref, *refs):
    hub_refs, (tile_ref, *base_ref, out_ref, total) = refs[: len(steps)], refs[len(steps) :]
    blocks = total.shape[0] - 1
    half = hub_refs[0].shape[1]
    lanes = lax.broadcasted_iota(jnp.int32, (half, 128), 1)
    first = (lanes < 64).astype(F32).astype(BF)
    second = (lanes >= 64).astype(F32).astype(BF)
    for b in range(blocks):
        at = slice(b * 128, (b + 1) * 128)
        total[b] = base_ref[0][:, at] if has_base else jnp.zeros_like(total[b])
    total[blocks] = jnp.zeros_like(total[blocks])
    z_size = sizes[1]
    for k, hub_ref in zip(steps, hub_refs):

        @pl.loop(0, hub_ref.shape[0] // z_size)
        def _(yh):
            for z in range(z_size):
                tile = tile_index(x_ref, k, sizes, yh, z, -1)
                rows = hub_ref[yh * z_size + z]
                weights = tile_ref[tile]
                product = jnp.dot(
                    jnp.concatenate([rows * first, rows * second], axis=0),
                    jnp.concatenate([weights, weights], axis=0),
                    preferred_element_type=F32,
                )
                dest = dest_ref[tile]
                total[dest] = total[dest] + product

    for b in range(blocks):
        out_ref[:, b * 128 : (b + 1) * 128] = total[b]


def fold_hubs(x_index, dest, hubs, steps, tiles, sizes, blocks, base):
    width = 2 * hubs[0].shape[1]
    bases = [] if base is None else [base]
    return call(
        partial(fold_kernel, steps, sizes, base is not None),
        jax.ShapeDtypeStruct((width, blocks * 128), F32),
        [SMEM, SMEM] + [VMEM] * (len(hubs) + 1 + len(bases)),
        [pltpu.VMEM((blocks + 1, width, 128), F32)],
        "hub_sums",
        tiles.size * width * len(hubs),
        4,
    )(x_index, dest, *hubs, tiles, *bases)


def hub_grad_kernel(k, sizes, x_ref, dest_ref, grad_ref, tile_ref, out_ref, blocked):
    blocks = blocked.shape[0] - 1
    for b in range(blocks):
        blocked[b] = grad_ref[:, b * 128 : (b + 1) * 128]
    blocked[blocks] = jnp.zeros_like(blocked[blocks])
    half = out_ref.shape[1]
    first = lax.broadcasted_iota(jnp.int32, (half, 128), 1) < 64
    z_size = sizes[1]

    @pl.loop(0, out_ref.shape[0] // z_size)
    def _(yh):
        for z in range(z_size):
            tile = tile_index(x_ref, k, sizes, yh, z, 1)
            weights = tile_ref[tile]
            product = mm(
                blocked[dest_ref[tile]],
                jnp.concatenate([weights, weights], axis=0),
                BOTH_COLS,
            )
            out_ref[yh * z_size + z] = jnp.where(first, product[:half], product[half:]).astype(BF)


def hub_grad_terms(x_index, dest, grad, tiles, k, sizes, blocks):
    width = grad.shape[0]
    return call(
        partial(hub_grad_kernel, k, sizes),
        jax.ShapeDtypeStruct((tiles.shape[0] // sizes[0], width // 2, 128), BF),
        [SMEM, SMEM, VMEM, VMEM],
        [pltpu.VMEM((blocks + 1, width, 128), BF)],
        "hub_grad_terms",
        tiles.size * width,
        4,
    )(x_index, dest, grad, tiles)


def local(
    features,
    hub_weight,
    hub_block,
    hub_mask,
    tail_rows,
    tail_count,
    tail_target,
    degree,
    w_self,
    w_neigh,
    out_bias,
    cotangent,
):
    width, nodes = features.shape
    tiles = hub_weight[0]
    parts, hubs, tile_len = tiles.shape
    slots = tail_rows.shape[2]
    half_width = width // 2
    blocks = nodes // tile_len
    full_width = w_self.shape[0]
    half_full = full_width // 2
    x_size, z_size = lax.axis_size("x"), lax.axis_size("z")
    sizes = (x_size, z_size)
    plane = parts // x_size
    x_index = lax.axis_index("x")[None]
    hub_dest = jnp.where(hub_mask[0] > 0, hub_block[0], blocks)
    degree = degree[None, :]

    hub_piece = jnp.concatenate([features[:half_width, :hubs], features[half_width:, :hubs]], axis=1)
    hub_plane = swap(jnp.broadcast_to(hub_piece[None], (plane, half_width, 128)), PLANE)

    slot_live = jnp.arange(slots, dtype=jnp.int32)[None, :] < tail_count[0][:, None]
    send_index = slot_rows(jnp.where(slot_live, tail_rows[0], -1))
    recv_index = slot_rows(tail_target[0])
    arrived = swap(gather_slots(send_index, features, parts, slots), DOM)

    own = jnp.concatenate([features, w_self.T, w_neigh.T], axis=1)
    hub_plane, own = lax.optimization_barrier((hub_plane, own))
    hub_all = [hub_plane] + [shift(hub_plane, "x", k) for k in range(1, x_size)]
    early = gather_rep(own)
    full_feat = early[:, :nodes]
    own_rows = lax.axis_index(REP) * width
    w_self_rows = lax.dynamic_slice_in_dim(early[:, nodes : nodes + full_width], own_rows, width, 1)
    w_neigh_rows = lax.dynamic_slice_in_dim(early[:, nodes + full_width :], own_rows, width, 1)
    pre_self = mm(w_self, full_feat, BOTH_ROWS) + out_bias[:, None]

    hub_sum = fold_hubs(x_index, hub_dest, hub_all[:2], (0, 1), tiles, sizes, blocks, None)
    hub_sum = fold_hubs(x_index, hub_dest, hub_all[2:], (2, 3), tiles, sizes, blocks, hub_sum)
    mixed = mixed_sums(recv_index, arrived, hub_sum, degree)

    full_mixed = lax.all_gather(mixed, REP, axis=0, tiled=True)
    pre = pre_self + mm(w_neigh, full_mixed, BOTH_ROWS)
    sigma = jax.nn.sigmoid(pre)
    output = (pre * sigma).astype(BF)
    d_pre = (cotangent.astype(F32) * (sigma * (1.0 + pre * (1.0 - sigma)))).astype(BF)

    full_d = lax.all_gather(d_pre, REP, axis=0, tiled=True)
    grad_rows = weight_rows(full_feat, full_mixed, d_pre, parts)
    mixed_grad, tail_send = back_gather(recv_index, w_neigh_rows.T, full_d, degree, parts, slots)
    tail_len = tail_send.shape[1]
    first = swap(jnp.concatenate([tail_send, grad_rows], axis=1), DOM)
    direct = mm(w_self_rows, full_d, BOTH_ROWS)

    hub_terms = [
        hub_grad_terms(x_index, hub_dest, mixed_grad, tiles, k, sizes, blocks)
        for k in range(x_size)
    ]
    hub_x = hub_terms[0].astype(F32)
    for k in range(1, x_size):
        hub_x = hub_x + shift(hub_terms[k], "x", k).astype(F32)

    sums = jnp.sum(first[:, tail_len:].astype(F32), axis=0)
    grad_bias = (sums[4] + sums[5])[:width]
    sums = sums[:2] + sums[2:4]
    far_sums = jnp.stack([sums] + [shift(sums, "x", k) for k in range(1, x_size)])
    order = lax.rem(x_index[0] + x_size - jnp.arange(x_size, dtype=jnp.int32), x_size)
    x_sums = jnp.take(far_sums, order, axis=0).reshape(2 * x_size, 128)
    sum_rows = jnp.broadcast_to(high_low(x_sums, 0)[None], (plane, 4 * x_size, 128))
    second = swap(jnp.concatenate([hub_x.astype(BF), sum_rows], axis=1), PLANE)

    tail_grad = tail_grads(send_index, first, direct, tail_len)
    all_sums = second[:, half_width:].astype(F32)
    all_sums = all_sums[:, : 2 * x_size] + all_sums[:, 2 * x_size :]
    all_sums = all_sums.reshape(-1, z_size, x_size, 2, 128).transpose(0, 2, 1, 3, 4)
    all_sums = all_sums.reshape(full_width, 128)
    grad_w_self, grad_w_neigh = [
        jnp.concatenate([rows[:, :width], rows[:, width:]], axis=0)
        for rows in (all_sums[:half_full], all_sums[half_full:])
    ]
    hub_back = jnp.sum(second[:, :half_width].astype(F32), axis=0)
    hub_grad = jnp.concatenate([hub_back[:, :hubs], hub_back[:, hubs:]], axis=0)
    grad_features = tail_grad.at[:, :hubs].add(hub_grad)
    return (output, grad_features, grad_w_self, grad_w_neigh, grad_bias)


def solution(mesh):
    grid = (4, 4, mesh.shape["dom"] // 16, 2, 2)
    parted = Mesh(mesh.devices.reshape(grid), DOM + REP)
    in_specs = (
        P(REP, DOM),
        P(DOM, None, None, None),
        P(DOM, None),
        P(DOM, None),
        P(DOM, None, None),
        P(DOM, None),
        P(DOM, None, None),
        P(DOM),
        P(None, REP),
        P(None, REP),
        P(REP),
        P(REP, DOM),
    )
    out_specs = (P(REP, DOM), P(REP, DOM), P(None, REP), P(None, REP), P(REP))
    return jax.shard_map(local, mesh=parted, in_specs=in_specs, out_specs=out_specs, check_vma=False)
```

```python
from functools import partial

import jax
import jax.numpy as jnp
from jax import lax
from jax.experimental import pallas as pl
from jax.experimental.pallas import tpu as pltpu
from jax.sharding import Mesh
from jax.sharding import PartitionSpec as P

BF = jnp.bfloat16
F32 = jnp.float32
BOTH_ROWS = (((0,), (0,)), ((), ()))
BOTH_COLS = (((1,), (1,)), ((), ()))
DOM = ("yh", "x", "z")
PLANE = ("yh", "z")
REP = ("yl", "core")
SMEM = pl.BlockSpec(memory_space=pltpu.SMEM)
VMEM = pl.BlockSpec(memory_space=pltpu.VMEM)
MIB = 1024 * 1024


def mm(a, b, dims):
    return lax.dot_general(a, b, dims, preferred_element_type=F32)


def swap(pieces, axis):
    return lax.all_to_all(pieces, axis, split_axis=0, concat_axis=0, tiled=True)


def shift(values, axis, step):
    size = lax.axis_size(axis)
    return lax.ppermute(values, axis, [(i, (i + step) % size) for i in range(size)])


def call(kernel, out_shape, in_specs, scratch, name, flops, mib):
    outs = VMEM if isinstance(out_shape, jax.ShapeDtypeStruct) else [VMEM] * len(out_shape)
    return pl.pallas_call(
        kernel,
        out_shape=out_shape,
        in_specs=in_specs,
        out_specs=outs,
        scratch_shapes=scratch,
        compiler_params=pltpu.CompilerParams(vmem_limit_bytes=32 * MIB),
        cost_estimate=pl.CostEstimate(flops=flops, bytes_accessed=mib * MIB, transcendentals=0),
        name=name,
    )


def slot_rows(index):
    parts, slots = index.shape
    return index.reshape(parts, 2, slots // 2).transpose(1, 0, 2).reshape(2, -1)


def pick_slots(index_ref, source, out_ref):
    width, nodes = source.shape
    low_size = 256
    high_size = nodes // low_size
    split = jnp.concatenate(
        [source[:, i * low_size : (i + 1) * low_size] for i in range(high_size)], axis=0
    )
    step = 256
    rows = out_ref.shape[1]
    low_ids = lax.broadcasted_iota(jnp.int32, (low_size, step), 0)
    for start in range(0, index_ref.shape[1], step):
        halves = []
        for h in range(2):
            index = index_ref[h : h + 1, start : start + step]
            hits = jnp.where(low_ids == (index & (low_size - 1)), 1.0, 0.0).astype(BF)
            found = jnp.dot(split, hits, preferred_element_type=F32)
            high = jnp.broadcast_to(index >> 8, (width, step))
            kept = jnp.zeros((width, step), F32)
            for i in range(high_size):
                kept = jnp.where(high == i, found[i * width : (i + 1) * width], kept)
            halves.append(kept)
        block = jnp.concatenate(halves, axis=0).T
        first = start // rows
        out_ref[first : first + step // rows] = block.reshape(step // rows, rows, 128).astype(BF)


def gather_kernel(index_ref, source_ref, out_ref):
    pick_slots(index_ref, source_ref[...], out_ref)


def gather_slots(index, source, parts, slots):
    return call(
        gather_kernel,
        jax.ShapeDtypeStruct((parts, slots // 2, 128), BF),
        [VMEM, VMEM],
        [],
        "tail_rows_out",
        2 * parts * slots * 256 * 256,
        2,
    )(index, source)


def back_kernel(index_ref, weight_ref, d_ref, degree_ref, grad_ref, out_ref):
    grad = jnp.dot(weight_ref[...], d_ref[...], preferred_element_type=F32).astype(BF)
    grad_ref[...] = grad
    scaled = (grad.astype(F32) / degree_ref[...].astype(F32)).astype(BF)
    pick_slots(index_ref, scaled, out_ref)


def back_gather(index, weight, d_full, degree, parts, slots):
    width, nodes = weight.shape[0], d_full.shape[1]
    return call(
        back_kernel,
        [
            jax.ShapeDtypeStruct((width, nodes), BF),
            jax.ShapeDtypeStruct((parts, slots // 2, 128), BF),
        ],
        [VMEM] * 4,
        [],
        "mixed_grad_rows_out",
        2 * parts * slots * 256 * 256,
        2,
    )(index, weight, d_full, degree)


def sum_slots(index_ref, arrived_ref, rows, start, size):
    parts = arrived_ref.shape[0]
    flat = arrived_ref[:, :rows, :].reshape(parts * rows, 128)
    ids = lax.broadcasted_iota(jnp.int32, (size, parts * rows), 0) + start
    sums = []
    for h in range(2):
        hits = jnp.where(ids == index_ref[h : h + 1, :], 1.0, 0.0).astype(BF)
        sums.append(jnp.dot(hits, flat, preferred_element_type=F32))
    return sums[0].T[:64] + sums[1].T[64:]


def mixed_kernel(rows, index_ref, arrived_ref, hub_ref, degree_ref, out_ref):
    size = 256
    for start in range(0, out_ref.shape[1], size):
        at = slice(start, start + size)
        tail = sum_slots(index_ref, arrived_ref, rows, start, size)
        out_ref[:, at] = (hub_ref[:, at] + tail / degree_ref[:, at].astype(F32)).astype(BF)


def mixed_sums(index, arrived, hub_sum, degree):
    parts, rows, _ = arrived.shape
    width, nodes = hub_sum.shape
    return call(
        partial(mixed_kernel, rows),
        jax.ShapeDtypeStruct((width, nodes), BF),
        [VMEM] * 4,
        [],
        "mixed",
        4 * parts * rows * nodes * 128,
        2,
    )(index, arrived, hub_sum, degree)


def tail_grad_kernel(rows, index_ref, arrived_ref, direct_ref, out_ref):
    size = 256
    for start in range(0, out_ref.shape[1], size):
        at = slice(start, start + size)
        tail = sum_slots(index_ref, arrived_ref, rows, start, size)
        out_ref[:, at] = direct_ref[:, at] + tail


def tail_grads(index, arrived, direct, rows):
    parts = arrived.shape[0]
    width, nodes = direct.shape
    return call(
        partial(tail_grad_kernel, rows),
        jax.ShapeDtypeStruct((width, nodes), F32),
        [VMEM] * 3,
        [],
        "tail_grads",
        4 * parts * rows * nodes * 128,
        2,
    )(index, arrived, direct)


def arrange_kernel(place_ref, near_ref, far_ref, w_ref, bias_ref, *refs):
    feat_ref, pre_ref, self_ref, neigh_ref, wide = refs
    width, nodes = pre_ref.shape
    full = feat_ref.shape[0]
    for i in range(4):
        block = (near_ref, far_ref)[i // 2].at[i % 2]
        at = pl.ds(pl.multiple_of(place_ref[i] * width, width), width)
        feat_ref[at, :] = block[:, :nodes]
        wide[at, :] = block[:, nodes:].astype(F32)
    pre_ref[...] = (
        jnp.dot(w_ref[...], feat_ref[...], preferred_element_type=F32) + bias_ref[...]
    )
    own = place_ref[0]
    for first, out_ref in ((0, self_ref), (full, neigh_ref)):
        rows = wide[:, first : first + width]
        for k in range(1, 4):
            at = first + k * width
            rows = jnp.where(own == k, wide[:, at : at + width], rows)
        out_ref[...] = rows.T.astype(BF)


def arrange(place, near, far, w_self, bias):
    width, full = w_self.shape
    nodes = near.shape[2] - 2 * full
    return call(
        arrange_kernel,
        [
            jax.ShapeDtypeStruct((full, nodes), BF),
            jax.ShapeDtypeStruct((width, nodes), F32),
            jax.ShapeDtypeStruct((width, full), BF),
            jax.ShapeDtypeStruct((width, full), BF),
        ],
        [SMEM] + [VMEM] * 4,
        [pltpu.VMEM((full, 2 * full), F32)],
        "own_columns",
        2 * width * full * nodes,
        2,
    )(place, near, far, w_self, bias)


def weight_kernel(feat_ref, mixed_ref, d_ref, out_ref, bias_ref):
    d_pre = d_ref[...]
    half = feat_ref.shape[0] // 2
    y_size, x_size, pairs = out_ref.shape[:3]
    for place, ref in enumerate((feat_ref, mixed_ref)):
        grad = mm(ref[...], d_pre, BOTH_COLS)
        grad = jnp.concatenate([grad[:half], grad[half:]], axis=1)
        grad = grad.reshape(y_size // 2, pairs, 16, 128).astype(BF)
        at = slice(place * (y_size // 2), (place + 1) * (y_size // 2))
        for x in range(x_size):
            out_ref[at, x] = grad
    rows = bias_ref.shape[0]
    bias = mm(jnp.ones((rows, d_pre.shape[1]), BF), d_pre, BOTH_COLS)
    bias = jnp.concatenate([bias, bias], axis=1)
    high = bias.astype(BF).astype(F32)
    row = lax.broadcasted_iota(jnp.int32, bias.shape, 0)
    kept = jnp.where(row == 0, high, jnp.where(row == 1, bias - high, 0.0))
    bias_ref[...] = kept.astype(BF)


def weight_rows(full_feat, full_mixed, d_pre, sizes, plane):
    x_size, z_size = sizes
    width = d_pre.shape[0]
    made, bias = call(
        weight_kernel,
        [
            jax.ShapeDtypeStruct((plane // z_size, x_size, z_size // 2, 16, 128), BF),
            jax.ShapeDtypeStruct((width // 2, 128), BF),
        ],
        [VMEM] * 3,
        [],
        "weight_grad_rows",
        4 * full_feat.size * width,
        2,
    )(full_feat, full_mixed, d_pre)
    return made.reshape(plane * x_size, 8, 128), bias


def quarter_call(kernel, out_shape, scalars, blocks, specs, out_spec, scratch, name, flops, steps):
    return pl.pallas_call(
        kernel,
        out_shape=out_shape,
        grid_spec=pltpu.PrefetchScalarGridSpec(
            num_scalar_prefetch=len(scalars),
            grid=(steps,),
            in_specs=specs,
            out_specs=out_spec,
            scratch_shapes=scratch,
        ),
        compiler_params=pltpu.CompilerParams(vmem_limit_bytes=32 * MIB),
        cost_estimate=pl.CostEstimate(flops=flops, bytes_accessed=2 * MIB, transcendentals=0),
        name=name,
    )(*scalars, *blocks)


def x_at(x_ref, step, x_size):
    return lax.rem(x_ref[0] + step % x_size, x_size)


def quarter_spec(tiles, step):
    _, x_size, z_size, hubs, tile_len = tiles.shape
    return pl.BlockSpec(
        (1, 1, z_size, hubs, tile_len),
        lambda y, x_ref, dest_ref: (y, x_at(x_ref, step, x_size), 0, 0, 0),
    )


def whole_spec(shape):
    return pl.BlockSpec(shape, lambda y, x_ref, dest_ref: (0,) * len(shape))


def fold_kernel(steps, sizes, has_base, x_ref, dest_ref, *refs):
    count = len(steps)
    hub_refs, tile_refs = refs[:count], refs[count : 2 * count]
    *base_ref, out_ref, total = refs[2 * count :]
    blocks = total.shape[0] - 1
    half = hub_refs[0].shape[1]
    x_size, z_size = sizes
    y = pl.program_id(0)

    @pl.when(y == 0)
    def _():
        for b in range(blocks):
            at = slice(b * 128, (b + 1) * 128)
            total[b] = base_ref[0][:, at] if has_base else jnp.zeros_like(total[b])
        total[blocks] = jnp.zeros_like(total[blocks])

    lanes = lax.broadcasted_iota(jnp.int32, (half, 128), 1)
    first = (lanes < 64).astype(F32).astype(BF)
    second = (lanes >= 64).astype(F32).astype(BF)
    for k, hub_ref, tile_ref in zip(steps, hub_refs, tile_refs):
        tile = (y * x_size + x_at(x_ref, -k, x_size)) * z_size
        for z in range(z_size):
            rows = hub_ref[z]
            weights = tile_ref[0, 0, z]
            product = jnp.dot(
                jnp.concatenate([rows * first, rows * second], axis=0),
                jnp.concatenate([weights, weights], axis=0),
                preferred_element_type=F32,
            )
            dest = dest_ref[tile + z]
            total[dest] = total[dest] + product

    @pl.when(y == pl.num_programs(0) - 1)
    def _():
        for b in range(blocks):
            out_ref[:, b * 128 : (b + 1) * 128] = total[b]


def fold_hubs(x_index, dest, hubs, steps, tiles, blocks, base):
    y_size, x_size, z_size = tiles.shape[:3]
    half = hubs[0].shape[1]
    shape = (2 * half, blocks * 128)
    bases = [] if base is None else [base]
    hub_spec = pl.BlockSpec((z_size, half, 128), lambda y, x_ref, dest_ref: (y, 0, 0))
    return quarter_call(
        partial(fold_kernel, steps, (x_size, z_size), base is not None),
        jax.ShapeDtypeStruct(shape, F32),
        (x_index, dest),
        (*hubs, *[tiles for _ in steps], *bases),
        [hub_spec for _ in hubs]
        + [quarter_spec(tiles, -k) for k in steps]
        + [whole_spec(shape) for _ in bases],
        whole_spec(shape),
        [pltpu.VMEM((blocks + 1, 2 * half, 128), F32)],
        "hub_sums",
        tiles.size * half * len(hubs),
        y_size,
    )


def hub_grad_kernel(k, sizes, x_ref, dest_ref, grad_ref, bias_ref, tile_ref, out_ref, blocked):
    blocks = blocked.shape[0] - 1
    x_size, z_size = sizes
    y = pl.program_id(0)

    @pl.when(y == 0)
    def _():
        for b in range(blocks):
            blocked[b] = grad_ref[:, b * 128 : (b + 1) * 128]
        blocked[blocks] = jnp.zeros_like(blocked[blocks])
        out_ref[out_ref.shape[0] - 1] = bias_ref[...]

    half = out_ref.shape[1]
    first = lax.broadcasted_iota(jnp.int32, (half, 128), 1) < 64
    tile = (y * x_size + x_at(x_ref, k, x_size)) * z_size
    for z in range(z_size):
        weights = tile_ref[0, 0, z]
        product = mm(
            blocked[dest_ref[tile + z]],
            jnp.concatenate([weights, weights], axis=0),
            BOTH_COLS,
        )
        out_ref[y * z_size + z] = jnp.where(first, product[:half], product[half:]).astype(BF)


def hub_grad_terms(x_index, dest, grad, bias, tiles, k, blocks):
    y_size, x_size, z_size = tiles.shape[:3]
    width = grad.shape[0]
    out = (y_size * z_size + 1, width // 2, 128)
    return quarter_call(
        partial(hub_grad_kernel, k, (x_size, z_size)),
        jax.ShapeDtypeStruct(out, BF),
        (x_index, dest),
        (grad, bias, tiles),
        [whole_spec(grad.shape), whole_spec(bias.shape), quarter_spec(tiles, k)],
        whole_spec(out),
        [pltpu.VMEM((blocks + 1, width, 128), BF)],
        "hub_grad_terms",
        tiles.size * width // 2,
        y_size,
    )


def pack_kernel(*refs):
    *term_refs, sum_ref, out_ref = refs
    count, half = out_ref.shape[0], term_refs[0].shape[1]
    total = term_refs[0][...].astype(F32)
    for ref in term_refs[1:]:
        total = total + ref[...].astype(F32)
    out_ref[:, :half] = total[:count].astype(BF)
    bias = total[count]
    bias = jnp.broadcast_to(bias[0:1] + bias[1:2], (8, 128))
    high = bias.astype(BF).astype(F32)
    row = lax.broadcasted_iota(jnp.int32, (8, 128), 0)
    bias = jnp.where(row == 0, high, jnp.where(row == 1, bias - high, 0.0))
    extra = jnp.concatenate([sum_ref[...], bias], axis=0).astype(BF)
    out_ref[:, half:] = jnp.broadcast_to(extra[None], (count, 16, 128))


def pack_rows(terms, sums):
    count, half, _ = terms[0].shape
    return call(
        pack_kernel,
        jax.ShapeDtypeStruct((count - 1, half + 16, 128), BF),
        [VMEM] * (len(terms) + 1),
        [],
        "hub_grads_over_x",
        MIB,
        2,
    )(*terms, sums)


def final_kernel(second_ref, base_ref, out_ref, self_ref, neigh_ref, bias_ref):
    half = out_ref.shape[0] // 2
    hub = jnp.sum(second_ref[:, :half].astype(F32), axis=0)
    hub = jnp.concatenate([hub, pltpu.roll(hub, 64, 1)], axis=0)
    lane = lax.broadcasted_iota(jnp.int32, hub.shape, 1)
    out_ref[...] = base_ref[...] + jnp.where(lane < 64, hub, 0.0)
    extra = second_ref[:, half:].astype(F32)
    grads = extra[:, :8].reshape(-1, 128)
    rows = grads.shape[0] // 2
    for place, ref in enumerate((self_ref, neigh_ref)):
        turned = grads[place * rows : (place + 1) * rows].T
        ref[...] = jnp.concatenate([turned[:64], turned[64:]], axis=1)
    bias = jnp.sum(extra[:, 8:], axis=0)
    bias_ref[...] = jnp.broadcast_to(bias[0:1] + bias[1:2], bias_ref.shape)


def finish(second, base, full):
    width, nodes = base.shape
    hub_part = pl.BlockSpec((width, 128), lambda i: (0, 0))
    return pl.pallas_call(
        final_kernel,
        out_shape=[
            jax.ShapeDtypeStruct((width, nodes), F32),
            jax.ShapeDtypeStruct((width, full), F32),
            jax.ShapeDtypeStruct((width, full), F32),
            jax.ShapeDtypeStruct((8, 128), F32),
        ],
        grid=(1,),
        in_specs=[pl.BlockSpec(second.shape, lambda i: (0, 0, 0)), hub_part],
        out_specs=[hub_part]
        + [pl.BlockSpec((width, full), lambda i: (0, 0))] * 2
        + [pl.BlockSpec((8, 128), lambda i: (0, 0))],
        input_output_aliases={1: 0},
        compiler_params=pltpu.CompilerParams(vmem_limit_bytes=32 * MIB),
        cost_estimate=pl.CostEstimate(flops=MIB, bytes_accessed=MIB, transcendentals=0),
        name="gradients",
    )(second, base)


def local(
    features,
    hub_weight,
    hub_block,
    hub_mask,
    tail_rows,
    tail_count,
    tail_target,
    degree,
    w_self,
    w_neigh,
    out_bias,
    cotangent,
):
    width, nodes = features.shape
    parts, hubs, tile_len = hub_weight.shape[1:]
    slots = tail_rows.shape[2]
    half_width = width // 2
    blocks = nodes // tile_len
    full_width = w_self.shape[0]
    x_size, z_size = lax.axis_size("x"), lax.axis_size("z")
    sizes = (x_size, z_size)
    plane = parts // x_size
    x_index = lax.axis_index("x")[None]
    tiles = hub_weight.reshape(-1, x_size, z_size, hubs, tile_len)
    hub_dest = jnp.where(hub_mask[0] > 0, hub_block[0], blocks)
    degree = degree[None, :]

    hub_piece = jnp.concatenate([features[:half_width, :hubs], features[half_width:, :hubs]], axis=1)
    hub_send = jnp.broadcast_to(hub_piece[None], (plane, half_width, 128))
    hub_plane = swap(hub_send, PLANE)

    slot_live = jnp.arange(slots, dtype=jnp.int32)[None, :] < tail_count[0][:, None]
    send_index = slot_rows(jnp.where(slot_live, tail_rows[0], -1))
    recv_index = slot_rows(tail_target[0])
    own = jnp.concatenate([features, w_self.T, w_neigh.T], axis=1)
    own, send_index, _ = lax.optimization_barrier((own, send_index, hub_send))
    near = jnp.stack([own, shift(own, "yl", 1)])
    tail_send = gather_slots(send_index, features, parts, slots)
    hub_plane, tail_send, recv_index, near = lax.optimization_barrier(
        (hub_plane, tail_send, recv_index, near)
    )
    arrived = swap(tail_send, DOM)
    hub_all = [hub_plane] + [shift(hub_plane, "x", k) for k in range(1, x_size)]
    far = shift(near, "core", 1)
    place = lax.axis_index(REP) ^ jnp.array([0, 2, 1, 3], jnp.int32)
    full_feat, pre_self, w_self_rows, w_neigh_rows = arrange(
        place, near, far, w_self.T, out_bias[:, None]
    )

    hub_sum = fold_hubs(x_index, hub_dest, hub_all[:2], (0, 1), tiles, blocks, None)
    hub_sum = fold_hubs(x_index, hub_dest, hub_all[2:], (2, 3), tiles, blocks, hub_sum)
    mixed = mixed_sums(recv_index, arrived, hub_sum, degree)

    full_mixed = lax.all_gather(mixed, REP, axis=0, tiled=True)
    pre = pre_self + mm(w_neigh, full_mixed, BOTH_ROWS)
    sigma = jax.nn.sigmoid(pre)
    output = (pre * sigma).astype(BF)
    d_pre = (cotangent.astype(F32) * (sigma * (1.0 + pre * (1.0 - sigma)))).astype(BF)

    full_d = lax.all_gather(d_pre, REP, axis=0, tiled=True)
    grad_rows, bias_rows = weight_rows(full_feat, full_mixed, d_pre, sizes, plane)
    mixed_grad, tail_back = back_gather(recv_index, w_neigh_rows, full_d, degree, parts, slots)
    tail_len = tail_back.shape[1]
    first = swap(jnp.concatenate([tail_back, grad_rows], axis=1), DOM)
    direct = jnp.dot(w_self_rows, full_d, preferred_element_type=F32)

    terms = [
        hub_grad_terms(x_index, hub_dest, mixed_grad, bias_rows, tiles, k, blocks)
        for k in range(x_size)
    ]
    terms = terms[:1] + [shift(terms[k], "x", k) for k in range(1, x_size)]
    sums = jnp.sum(first[:, tail_len:].astype(F32), axis=0)
    second = swap(pack_rows(terms, sums), PLANE)

    base = tail_grads(send_index, first, direct, tail_len)
    grad_features, grad_w_self, grad_w_neigh, grad_bias = finish(second, base, full_width)
    return (output, grad_features, grad_w_self.T, grad_w_neigh.T, grad_bias[0, :width])


def solution(mesh):
    grid = (4, 4, mesh.shape["dom"] // 16, 2, 2)
    parted = Mesh(mesh.devices.reshape(grid), DOM + REP)
    in_specs = (
        P(REP, DOM),
        P(DOM, None, None, None),
        P(DOM, None),
        P(DOM, None),
        P(DOM, None, None),
        P(DOM, None),
        P(DOM, None, None),
        P(DOM),
        P(None, REP),
        P(None, REP),
        P(REP),
        P(REP, DOM),
    )
    out_specs = (P(REP, DOM), P(REP, DOM), P(None, REP), P(None, REP), P(REP))
    return jax.shard_map(local, mesh=parted, in_specs=in_specs, out_specs=out_specs, check_vma=False)
```

```python
from functools import partial

import jax
import jax.numpy as jnp
from jax import lax
from jax.experimental import pallas as pl
from jax.experimental.pallas import tpu as pltpu
from jax.sharding import Mesh
from jax.sharding import PartitionSpec as P

BF = jnp.bfloat16
F32 = jnp.float32
BOTH_ROWS = (((0,), (0,)), ((), ()))
BOTH_COLS = (((1,), (1,)), ((), ()))
DOM = ("yh", "x", "z")
PLANE = ("yh", "z")
REP = ("yl", "core")
SMEM = pl.BlockSpec(memory_space=pltpu.SMEM)
VMEM = pl.BlockSpec(memory_space=pltpu.VMEM)
MIB = 1024 * 1024
VMEM_LIMIT = 16 * MIB


def mm(a, b, dims):
    return lax.dot_general(a, b, dims, preferred_element_type=F32)


def swap(pieces, axis):
    return lax.all_to_all(pieces, axis, split_axis=0, concat_axis=0, tiled=True)


def shift(values, axis, step):
    size = lax.axis_size(axis)
    return lax.ppermute(values, axis, [(i, (i + step) % size) for i in range(size)])


def call(kernel, out_shape, in_specs, scratch, name, flops, mib):
    outs = VMEM if isinstance(out_shape, jax.ShapeDtypeStruct) else [VMEM] * len(out_shape)
    return pl.pallas_call(
        kernel,
        out_shape=out_shape,
        in_specs=in_specs,
        out_specs=outs,
        scratch_shapes=scratch,
        compiler_params=pltpu.CompilerParams(vmem_limit_bytes=VMEM_LIMIT),
        cost_estimate=pl.CostEstimate(flops=flops, bytes_accessed=mib * MIB, transcendentals=0),
        name=name,
    )


def slot_rows(index):
    parts, slots = index.shape
    return index.reshape(parts, 2, slots // 2).transpose(1, 0, 2).reshape(2, -1)


def pick_slots(index_ref, source, step):
    width, nodes = source.shape
    low_size = 256
    high_size = nodes // low_size
    split = jnp.concatenate(
        [source[:, i * low_size : (i + 1) * low_size] for i in range(high_size)], axis=0
    )
    low_ids = lax.broadcasted_iota(jnp.int32, (low_size, step), 0)
    for start in range(0, index_ref.shape[1], step):
        halves = []
        for h in range(2):
            index = index_ref[h : h + 1, start : start + step]
            hits = jnp.where(low_ids == (index & (low_size - 1)), 1.0, 0.0).astype(BF)
            found = jnp.dot(split, hits, preferred_element_type=F32)
            high = jnp.broadcast_to(index >> 8, (width, step))
            kept = jnp.zeros((width, step), F32)
            for i in range(high_size):
                kept = jnp.where(high == i, found[i * width : (i + 1) * width], kept)
            halves.append(kept)
        yield start, jnp.concatenate(halves, axis=0).T


def gather_kernel(index_ref, source_ref, out_ref):
    rows, step = out_ref.shape[1], 256
    for start, block in pick_slots(index_ref, source_ref[...], step):
        first = start // rows
        out_ref[first : first + step // rows] = block.reshape(-1, rows, 128).astype(BF)


def gather_slots(index, source, parts, slots):
    return call(
        gather_kernel,
        jax.ShapeDtypeStruct((parts, slots // 2, 128), BF),
        [VMEM, VMEM],
        [],
        "tail_rows_out",
        2 * parts * slots * 256 * 256,
        2,
    )(index, source)


def layer_kernel(sizes, place_ref, index_ref, degree_ref, *refs):
    mixed_ref, feat_ref, pre_ref, cot_ref, w_ref, neigh_ref, *out_refs = refs
    output_ref, d_ref, grad_ref, send_ref, bias_ref, pre_full = out_refs
    x_size, z_size = sizes
    width = output_ref.shape[0]
    full = mixed_ref.shape[0]
    half = full // 2
    mixed = mixed_ref[...]
    for first in range(0, full, width):
        at = slice(first, first + width)
        pre = pre_ref[at] + jnp.dot(w_ref[at], mixed, preferred_element_type=F32)
        sigma = jax.nn.sigmoid(pre)
        pre_full[at] = pre * sigma
        slope = sigma * (1.0 + pre * (1.0 - sigma))
        d_ref[at] = (cot_ref[at].astype(F32) * slope).astype(BF)
    own = pl.ds(pl.multiple_of(place_ref[0] * width, width), width)
    output_ref[...] = pre_full[own].astype(BF)
    d_pre = d_ref[own]

    made = []
    for source in (feat_ref[...], mixed):
        grad = mm(source, d_pre, BOTH_COLS)
        grad = jnp.concatenate([grad[:half], grad[half:]], axis=1)
        made.append(grad.reshape(-1, z_size // 2, 16, 128))
    made = jnp.concatenate(made, axis=0)
    bias = mm(jnp.ones((bias_ref.shape[0], d_pre.shape[1]), BF), d_pre, BOTH_COLS)
    bias = jnp.concatenate([bias, bias], axis=1)
    high = bias.astype(BF).astype(F32)
    row = lax.broadcasted_iota(jnp.int32, bias.shape, 0)
    bias_ref[...] = jnp.where(row == 0, high, jnp.where(row == 1, bias - high, 0.0)).astype(BF)

    grad = jnp.dot(neigh_ref[...], d_ref[...], preferred_element_type=F32).astype(BF)
    grad_ref[...] = grad
    scaled = (grad.astype(F32) / degree_ref[...].astype(F32)).astype(BF)
    rows = (send_ref.shape[1] - 16) // 2
    step = 256
    for start, block in pick_slots(index_ref, scaled, step):
        block = block.reshape(-1, 2, rows, 128)
        count = block.shape[0]
        first = start // (2 * rows)
        weight = made[first // (x_size * z_size // 2)]
        weight = jnp.concatenate([weight] * (count // weight.shape[0]), axis=0)
        block = jnp.concatenate([block[:, 0], weight[:, :8], block[:, 1], weight[:, 8:]], axis=1)
        send_ref[first : first + count] = block.astype(BF)


def layer(place, index, degree, mixed, feat, pre, cot, w_all, neigh_rows, sizes, parts, slots):
    full, nodes = mixed.shape
    width = neigh_rows.shape[0]
    return call(
        partial(layer_kernel, sizes),
        [
            jax.ShapeDtypeStruct((width, nodes), BF),
            jax.ShapeDtypeStruct((full, nodes), BF),
            jax.ShapeDtypeStruct((width, nodes), BF),
            jax.ShapeDtypeStruct((parts // 2, slots + 16, 128), BF),
            jax.ShapeDtypeStruct((width // 2, 128), BF),
        ],
        [SMEM] + [VMEM] * 8,
        [pltpu.VMEM((full, nodes), F32)],
        "layer",
        2 * parts * slots * 256 * 256,
        4,
    )(place, index, degree, mixed, feat, pre, cot, w_all, neigh_rows)


def sum_slots(index_ref, arrived_ref, rows, start, size):
    parts = arrived_ref.shape[0]
    flat = arrived_ref[:, :rows, :].reshape(parts * rows, 128)
    ids = lax.broadcasted_iota(jnp.int32, (size, parts * rows), 0) + start
    sums = []
    for h in range(2):
        hits = jnp.where(ids == index_ref[h : h + 1, :], 1.0, 0.0).astype(BF)
        sums.append(jnp.dot(hits, flat, preferred_element_type=F32))
    return sums[0].T[:64] + sums[1].T[64:]


def mixed_kernel(rows, index_ref, arrived_ref, hub_ref, degree_ref, out_ref):
    size = 256
    for start in range(0, out_ref.shape[1], size):
        at = slice(start, start + size)
        tail = sum_slots(index_ref, arrived_ref, rows, start, size)
        out_ref[:, at] = (hub_ref[:, at] + tail / degree_ref[:, at].astype(F32)).astype(BF)


def mixed_sums(index, arrived, hub_sum, degree):
    parts, rows, _ = arrived.shape
    width, nodes = hub_sum.shape
    return call(
        partial(mixed_kernel, rows),
        jax.ShapeDtypeStruct((width, nodes), BF),
        [VMEM] * 4,
        [],
        "mixed",
        4 * parts * rows * nodes * 128,
        2,
    )(index, arrived, hub_sum, degree)


def tail_grad_kernel(rows, index_ref, arrived_ref, weight_ref, d_ref, out_ref):
    size = 256
    for start in range(0, out_ref.shape[1], size):
        at = slice(start, start + size)
        tail = sum_slots(index_ref, arrived_ref, rows, start, size)
        direct = jnp.dot(weight_ref[...], d_ref[:, at], preferred_element_type=F32)
        out_ref[:, at] = direct + tail


def tail_grads(index, arrived, weight, d_full, rows):
    parts = arrived.shape[0]
    width, nodes = weight.shape[0], d_full.shape[1]
    return call(
        partial(tail_grad_kernel, rows),
        jax.ShapeDtypeStruct((width, nodes), F32),
        [VMEM] * 4,
        [],
        "tail_grads",
        4 * parts * rows * nodes * 128,
        2,
    )(index, arrived, weight, d_full)


def arrange_kernel(place_ref, near_ref, far_ref, *refs):
    feat_ref, cot_ref, pre_ref, w_ref, self_ref, neigh_ref, wide = refs
    full, nodes = pre_ref.shape
    width = self_ref.shape[0]
    for i in range(4):
        block = (near_ref, far_ref)[i // 2].at[i % 2]
        at = pl.ds(pl.multiple_of(place_ref[i] * width, width), width)
        feat_ref[at, :] = block[:, :nodes]
        cot_ref[at, :] = block[:, nodes : 2 * nodes]
        wide[at, :] = block[:, 2 * nodes :].astype(F32)
    bias = jnp.sum(wide[:, 2 * full : 2 * full + 128], axis=1, keepdims=True)
    w_self = wide[:, :full].astype(BF)
    w_ref[...] = wide[:, full : 2 * full].astype(BF)
    pre_ref[...] = jnp.dot(w_self, feat_ref[...], preferred_element_type=F32) + bias
    own = place_ref[0]
    for first, out_ref in ((0, self_ref), (full, neigh_ref)):
        rows = wide[:, first : first + width]
        for k in range(1, 4):
            at = first + k * width
            rows = jnp.where(own == k, wide[:, at : at + width], rows)
        out_ref[...] = rows.T.astype(BF)


def arrange(place, near, far, nodes, full):
    width = near.shape[1]
    return call(
        arrange_kernel,
        [
            jax.ShapeDtypeStruct((full, nodes), BF),
            jax.ShapeDtypeStruct((full, nodes), BF),
            jax.ShapeDtypeStruct((full, nodes), F32),
            jax.ShapeDtypeStruct((full, full), BF),
            jax.ShapeDtypeStruct((width, full), BF),
            jax.ShapeDtypeStruct((width, full), BF),
        ],
        [SMEM] + [VMEM] * 2,
        [pltpu.VMEM((full, 2 * full + 128), F32)],
        "own_columns",
        2 * full * full * nodes,
        4,
    )(place, near, far)


def three_terms(values):
    high = lax.reduce_precision(values, 8, 7)
    rest = values - high
    middle = lax.reduce_precision(rest, 8, 7)
    return [high.astype(BF), middle.astype(BF), (rest - middle).astype(BF)]


def tile_index(x_ref, k, sizes, yh, z, sign):
    x_size, z_size = sizes
    x = lax.rem(x_ref[0] + (sign * k) % x_size, x_size)
    return (yh * x_size + x) * z_size + z


def fold_kernel(steps, sizes, has_base, x_ref, dest_ref, *refs):
    hub_refs, (tile_ref, *base_ref, out_ref, total) = refs[: len(steps)], refs[len(steps) :]
    blocks = total.shape[0] - 1
    half = hub_refs[0].shape[1]
    lanes = lax.broadcasted_iota(jnp.int32, (half, 128), 1)
    first = (lanes < 64).astype(F32).astype(BF)
    second = (lanes >= 64).astype(F32).astype(BF)
    for b in range(blocks):
        at = slice(b * 128, (b + 1) * 128)
        total[b] = base_ref[0][:, at] if has_base else jnp.zeros_like(total[b])
    total[blocks] = jnp.zeros_like(total[blocks])
    z_size = sizes[1]
    for k, hub_ref in zip(steps, hub_refs):

        @pl.loop(0, hub_ref.shape[0] // z_size)
        def _(yh):
            for z in range(z_size):
                tile = tile_index(x_ref, k, sizes, yh, z, -1)
                rows = hub_ref[yh * z_size + z]
                weights = tile_ref[tile]
                product = jnp.dot(
                    jnp.concatenate([rows * first, rows * second], axis=0),
                    jnp.concatenate([weights, weights], axis=0),
                    preferred_element_type=F32,
                )
                dest = dest_ref[tile]
                total[dest] = total[dest] + product

    for b in range(blocks):
        out_ref[:, b * 128 : (b + 1) * 128] = total[b]


def fold_hubs(x_index, dest, hubs, steps, tiles, sizes, blocks, base):
    width = 2 * hubs[0].shape[1]
    bases = [] if base is None else [base]
    return call(
        partial(fold_kernel, steps, sizes, base is not None),
        jax.ShapeDtypeStruct((width, blocks * 128), F32),
        [SMEM, SMEM] + [VMEM] * (len(hubs) + 1 + len(bases)),
        [pltpu.VMEM((blocks + 1, width, 128), F32)],
        "hub_sums",
        tiles.size * width * len(hubs),
        4,
    )(x_index, dest, *hubs, tiles, *bases)


def hub_grad_kernel(steps, sizes, x_ref, dest_ref, grad_ref, bias_ref, tile_ref, *refs):
    *out_refs, blocked = refs
    blocks = blocked.shape[0] - 1
    for b in range(blocks):
        blocked[b] = grad_ref[:, b * 128 : (b + 1) * 128]
    blocked[blocks] = jnp.zeros_like(blocked[blocks])
    count, half, _ = out_refs[0].shape
    first = lax.broadcasted_iota(jnp.int32, (half, 128), 1) < 64
    z_size = sizes[1]
    for k, out_ref in zip(steps, out_refs):
        out_ref[count - 1] = bias_ref[...]

        @pl.loop(0, count // z_size)
        def _(yh):
            for z in range(z_size):
                tile = tile_index(x_ref, k, sizes, yh, z, 1)
                weights = tile_ref[tile]
                product = mm(
                    blocked[dest_ref[tile]],
                    jnp.concatenate([weights, weights], axis=0),
                    BOTH_COLS,
                )
                out_ref[yh * z_size + z] = jnp.where(
                    first, product[:half], product[half:]
                ).astype(BF)


def hub_grad_terms(x_index, dest, grad, bias, tiles, steps, sizes, blocks):
    width = grad.shape[0]
    shape = (tiles.shape[0] // sizes[0] + 1, width // 2, 128)
    return call(
        partial(hub_grad_kernel, steps, sizes),
        [jax.ShapeDtypeStruct(shape, BF) for _ in steps],
        [SMEM, SMEM, VMEM, VMEM, VMEM],
        [pltpu.VMEM((blocks + 1, width, 128), BF)],
        "hub_grad_terms",
        tiles.size * width * len(steps),
        4,
    )(x_index, dest, grad, bias, tiles)


def pack_kernel(*refs):
    *term_refs, sum_ref, out_ref = refs
    count, half = out_ref.shape[0], term_refs[0].shape[1]
    total = term_refs[0][...].astype(F32)
    for ref in term_refs[1:]:
        total = total + ref[...].astype(F32)
    out_ref[:, :half] = total[:count].astype(BF)
    bias = total[count]
    bias = jnp.broadcast_to(bias[0:1] + bias[1:2], (8, 128))
    high = bias.astype(BF).astype(F32)
    row = lax.broadcasted_iota(jnp.int32, (8, 128), 0)
    bias = jnp.where(row == 0, high, jnp.where(row == 1, bias - high, 0.0))
    extra = jnp.concatenate([sum_ref[...], bias], axis=0).astype(BF)
    out_ref[:, half:] = jnp.broadcast_to(extra[None], (count, 16, 128))


def pack_rows(terms, sums):
    count, half, _ = terms[0].shape
    return call(
        pack_kernel,
        jax.ShapeDtypeStruct((count - 1, half + 16, 128), BF),
        [VMEM] * (len(terms) + 1),
        [],
        "hub_grads_over_x",
        MIB,
        2,
    )(*terms, sums)


def final_kernel(second_ref, base_ref, out_ref, self_ref, neigh_ref, bias_ref):
    half = out_ref.shape[0] // 2
    hub = jnp.sum(second_ref[:, :half].astype(F32), axis=0)
    hub = jnp.concatenate([hub, pltpu.roll(hub, 64, 1)], axis=0)
    lane = lax.broadcasted_iota(jnp.int32, hub.shape, 1)
    out_ref[...] = base_ref[...] + jnp.where(lane < 64, hub, 0.0)
    extra = second_ref[:, half:].astype(F32)
    grads = extra[:, :8].reshape(-1, 128)
    rows = grads.shape[0] // 2
    for place, ref in enumerate((self_ref, neigh_ref)):
        turned = grads[place * rows : (place + 1) * rows].T
        ref[...] = jnp.concatenate([turned[:64], turned[64:]], axis=1)
    bias = jnp.sum(extra[:, 8:], axis=0)
    bias_ref[...] = (bias[0:1] + bias[1:2])[:, : bias_ref.shape[1]]


def finish(second, base, full):
    width, nodes = base.shape
    hub_part = pl.BlockSpec((width, 128), lambda i: (0, 0))
    return pl.pallas_call(
        final_kernel,
        out_shape=[
            jax.ShapeDtypeStruct((width, nodes), F32),
            jax.ShapeDtypeStruct((width, full), F32),
            jax.ShapeDtypeStruct((width, full), F32),
            jax.ShapeDtypeStruct((1, width), F32),
        ],
        grid=(1,),
        in_specs=[pl.BlockSpec(second.shape, lambda i: (0, 0, 0)), hub_part],
        out_specs=[hub_part]
        + [pl.BlockSpec((width, full), lambda i: (0, 0))] * 2
        + [pl.BlockSpec((1, width), lambda i: (0, 0))],
        input_output_aliases={1: 0},
        compiler_params=pltpu.CompilerParams(vmem_limit_bytes=VMEM_LIMIT),
        cost_estimate=pl.CostEstimate(flops=MIB, bytes_accessed=MIB, transcendentals=0),
        name="gradients",
    )(second, base)


def local(
    features,
    hub_weight,
    hub_block,
    hub_mask,
    tail_rows,
    tail_count,
    tail_target,
    degree,
    w_self,
    w_neigh,
    out_bias,
    cotangent,
):
    width, nodes = features.shape
    parts, hubs, tile_len = hub_weight.shape[1:]
    slots = tail_rows.shape[2]
    half_width = width // 2
    blocks = nodes // tile_len
    full_width = w_self.shape[0]
    x_size, z_size = lax.axis_size("x"), lax.axis_size("z")
    sizes = (x_size, z_size)
    plane = parts // x_size
    x_index = lax.axis_index("x")[None]
    tiles = hub_weight[0]
    hub_dest = jnp.where(hub_mask[0] > 0, hub_block[0], blocks)
    degree = degree[None, :]

    hub_piece = jnp.concatenate([features[:half_width, :hubs], features[half_width:, :hubs]], axis=1)
    hub_send = jnp.broadcast_to(hub_piece[None], (plane, half_width, 128))
    hub_plane = swap(hub_send, PLANE)

    slot_live = jnp.arange(slots, dtype=jnp.int32)[None, :] < tail_count[0][:, None]
    send_index = slot_rows(jnp.where(slot_live, tail_rows[0], -1))
    recv_index = slot_rows(tail_target[0])
    bias_terms = jnp.stack(three_terms(out_bias), axis=1)
    bias_terms = jnp.pad(bias_terms, ((0, 0), (0, 128 - bias_terms.shape[1])))
    own = jnp.concatenate([features, cotangent, w_self.T, w_neigh.T, bias_terms], axis=1)
    own, send_index, _ = lax.optimization_barrier((own, send_index, hub_send))
    near = jnp.stack([own, shift(own, "yl", 1)])
    tail_send = gather_slots(send_index, features, parts, slots)
    hub_plane, tail_send, recv_index, near = lax.optimization_barrier(
        (hub_plane, tail_send, recv_index, near)
    )
    arrived = swap(tail_send, DOM)
    hub_all = [hub_plane] + [shift(hub_plane, "x", k) for k in range(1, x_size)]
    far = shift(near, "core", 1)
    place = lax.axis_index(REP) ^ jnp.array([0, 2, 1, 3], jnp.int32)
    own_columns = arrange(place, near, far, nodes, full_width)

    fold = partial(fold_hubs, x_index, hub_dest, tiles=tiles, sizes=sizes, blocks=blocks)
    hub_sum = fold(hub_all[:2], (0, 1), base=None)
    hub_sum, own_columns = lax.optimization_barrier((hub_sum, own_columns))
    full_feat, full_cot, pre_self, w_neigh_all, w_self_rows, w_neigh_rows = own_columns
    hub_sum = fold(hub_all[2:], (2, 3), base=hub_sum)
    mixed = mixed_sums(recv_index, arrived, hub_sum, degree)
    full_mixed = lax.all_gather(mixed, REP, axis=0, tiled=True)

    output, d_full, mixed_grad, tail_back, bias_rows = layer(
        place,
        recv_index,
        degree,
        full_mixed,
        full_feat,
        pre_self,
        full_cot,
        w_neigh_all,
        w_neigh_rows,
        sizes,
        parts,
        slots,
    )
    tail_len = slots // 2
    first = swap(tail_back.reshape(parts, tail_len + 8, 128), DOM)

    hub_terms = partial(
        hub_grad_terms, x_index, hub_dest, mixed_grad, bias_rows, tiles, sizes=sizes, blocks=blocks
    )
    far_steps = (2, 1, 3)
    terms = [shift(term, "x", k) for term, k in zip(hub_terms(far_steps), far_steps)]
    terms = list(hub_terms((0,))) + terms
    sums = jnp.sum(first[:, tail_len:].astype(F32), axis=0)
    second = swap(pack_rows(terms, sums), PLANE)

    base = tail_grads(send_index, first, w_self_rows, d_full, tail_len)
    grad_features, grad_w_self, grad_w_neigh, grad_bias = finish(second, base, full_width)
    return (output, grad_features, grad_w_self.T, grad_w_neigh.T, grad_bias[0])


def solution(mesh):
    grid = (4, 4, mesh.shape["dom"] // 16, 2, 2)
    parted = Mesh(mesh.devices.reshape(grid), DOM + REP)
    in_specs = (
        P(REP, DOM),
        P(DOM, None, None, None),
        P(DOM, None),
        P(DOM, None),
        P(DOM, None, None),
        P(DOM, None),
        P(DOM, None, None),
        P(DOM),
        P(None, REP),
        P(None, REP),
        P(REP),
        P(REP, DOM),
    )
    out_specs = (P(REP, DOM), P(REP, DOM), P(None, REP), P(None, REP), P(REP))
    return jax.shard_map(local, mesh=parted, in_specs=in_specs, out_specs=out_specs, check_vma=False)
```

```python
from functools import partial

import jax
import jax.numpy as jnp
from jax import lax
from jax.experimental import pallas as pl
from jax.experimental.pallas import tpu as pltpu
from jax.sharding import Mesh
from jax.sharding import PartitionSpec as P

BF = jnp.bfloat16
F32 = jnp.float32
BOTH_ROWS = (((0,), (0,)), ((), ()))
BOTH_COLS = (((1,), (1,)), ((), ()))
DOM = ("yh", "x", "z")
PLANE = ("yh", "z")
REP = ("yl", "core")
SMEM = pl.BlockSpec(memory_space=pltpu.SMEM)
VMEM = pl.BlockSpec(memory_space=pltpu.VMEM)
MIB = 1024 * 1024
VMEM_LIMIT = 16 * MIB


def mm(a, b, dims):
    return lax.dot_general(a, b, dims, preferred_element_type=F32)


def swap(pieces, axis):
    return lax.all_to_all(pieces, axis, split_axis=0, concat_axis=0, tiled=True)


def shift(values, axis, step):
    size = lax.axis_size(axis)
    return lax.ppermute(values, axis, [(i, (i + step) % size) for i in range(size)])


def call(kernel, out_shape, in_specs, scratch, name, flops, mib):
    outs = VMEM if isinstance(out_shape, jax.ShapeDtypeStruct) else [VMEM] * len(out_shape)
    return pl.pallas_call(
        kernel,
        out_shape=out_shape,
        in_specs=in_specs,
        out_specs=outs,
        scratch_shapes=scratch,
        compiler_params=pltpu.CompilerParams(vmem_limit_bytes=VMEM_LIMIT),
        cost_estimate=pl.CostEstimate(flops=flops, bytes_accessed=mib * MIB, transcendentals=0),
        name=name,
    )


def slot_rows(index):
    parts, slots = index.shape
    return index.reshape(parts, 2, slots // 2).transpose(1, 0, 2).reshape(2, -1)


def pick_slots(index_ref, source, step):
    width, nodes = source.shape
    low_size = 256
    high_size = nodes // low_size
    split = jnp.concatenate(
        [source[:, i * low_size : (i + 1) * low_size] for i in range(high_size)], axis=0
    )
    low_ids = lax.broadcasted_iota(jnp.int32, (low_size, step), 0)
    for start in range(0, index_ref.shape[1], step):
        halves = []
        for h in range(2):
            index = index_ref[h : h + 1, start : start + step]
            hits = jnp.where(low_ids == (index & (low_size - 1)), 1.0, 0.0).astype(BF)
            found = jnp.dot(split, hits, preferred_element_type=F32)
            high = jnp.broadcast_to(index >> 8, (width, step))
            kept = jnp.zeros((width, step), F32)
            for i in range(high_size):
                kept = jnp.where(high == i, found[i * width : (i + 1) * width], kept)
            halves.append(kept)
        yield start, jnp.concatenate(halves, axis=0).T


def gather_kernel(index_ref, source_ref, out_ref):
    rows, step = out_ref.shape[1], 256
    for start, block in pick_slots(index_ref, source_ref[...], step):
        first = start // rows
        out_ref[first : first + step // rows] = block.reshape(-1, rows, 128).astype(BF)


def gather_slots(index, source, parts, slots):
    return call(
        gather_kernel,
        jax.ShapeDtypeStruct((parts, slots // 2, 128), BF),
        [VMEM, VMEM],
        [],
        "tail_rows_out",
        2 * parts * slots * 256 * 256,
        2,
    )(index, source)


def layer_kernel(sizes, place_ref, index_ref, degree_ref, mixed_ref, *refs):
    block_refs, refs = refs[:4], refs[4:]
    outs, (bias_ref, *held), (feat, low_rows, sems) = refs[:5], refs[5:11], refs[11:]
    output_ref, d_ref, grad_ref, send_ref, self_ref = held
    x_size, z_size = sizes
    width, nodes = output_ref.shape
    full = mixed_ref.shape[0]
    half = full // 2
    copies = [pltpu.make_async_copy(h, o, sems.at[i]) for i, (h, o) in enumerate(zip(held, outs))]
    own = place_ref[0]
    rows_of = [pl.ds(pl.multiple_of(place_ref[i] * width, width), width) for i in range(4)]
    for at, ref in zip(rows_of, block_refs):
        feat[at, :] = ref[:, :nodes]
        low_rows[at, :] = ref[:, 2 * nodes : 2 * nodes + 2 * full].astype(F32)

    own_weights = []
    for first in (0, full):
        rows = low_rows[:, first : first + width]
        for k in range(1, 4):
            start = first + k * width
            rows = jnp.where(own == k, low_rows[:, start : start + width], rows)
        own_weights.append(rows.T.astype(BF))
    self_ref[...] = own_weights[0]
    copies[4].start()

    mixed, full_feat = mixed_ref[...], feat[...]
    for i, (at, ref) in enumerate(zip(rows_of, block_refs)):
        first = 2 * nodes
        bias = ref[:, first + 2 * full :].astype(F32)
        pre = jnp.dot(ref[:, first : first + full], full_feat, preferred_element_type=F32)
        pre = pre + jnp.dot(
            ref[:, first + full : first + 2 * full], mixed, preferred_element_type=F32
        )
        pre = pre + jnp.sum(bias, axis=1, keepdims=True)
        sigma = jax.nn.sigmoid(pre)
        slope = sigma * (1.0 + pre * (1.0 - sigma))
        d_part = (ref[:, nodes : 2 * nodes].astype(F32) * slope).astype(BF)
        d_ref[at, :] = d_part
        if i == 0:
            d_pre = d_part
            output_ref[...] = (pre * sigma).astype(BF)
            copies[0].start()
    copies[1].start()

    grad = jnp.dot(own_weights[1], d_ref[...], preferred_element_type=F32).astype(BF)
    grad_ref[...] = grad
    copies[2].start()
    scaled = (grad.astype(F32) / degree_ref[...].astype(F32)).astype(BF)

    made = []
    for source in (full_feat, mixed):
        total = mm(source, d_pre, BOTH_COLS)
        total = jnp.concatenate([total[:half], total[half:]], axis=1)
        made.append(total.reshape(-1, z_size // 2, 16, 128))
    made = jnp.concatenate(made, axis=0)
    bias = mm(jnp.ones((bias_ref.shape[0], nodes), BF), d_pre, BOTH_COLS)
    bias = jnp.concatenate([bias, bias], axis=1)
    high = bias.astype(BF).astype(F32)
    row = lax.broadcasted_iota(jnp.int32, bias.shape, 0)
    bias_ref[...] = jnp.where(row == 0, high, jnp.where(row == 1, bias - high, 0.0)).astype(BF)

    rows = (send_ref.shape[1] - 16) // 2
    step = 256
    for start, block in pick_slots(index_ref, scaled, step):
        block = block.reshape(-1, 2, rows, 128)
        count = block.shape[0]
        first = start // (2 * rows)
        weight = made[first // (x_size * z_size // 2)]
        weight = jnp.concatenate([weight] * (count // weight.shape[0]), axis=0)
        block = jnp.concatenate([block[:, 0], weight[:, :8], block[:, 1], weight[:, 8:]], axis=1)
        send_ref[first : first + count] = block.astype(BF)
    copies[3].start()
    for copy in copies:
        copy.wait()


def layer(place, index, degree, mixed, own_blocks, sizes, parts, slots):
    full, nodes = mixed.shape
    width = own_blocks[0].shape[0]
    held = [
        (width, nodes),
        (full, nodes),
        (width, nodes),
        (parts // 2, slots + 16, 128),
        (width, full),
    ]
    bias_shape = (width // 2, 128)
    return pl.pallas_call(
        partial(layer_kernel, sizes),
        out_shape=[jax.ShapeDtypeStruct(shape, BF) for shape in [*held, bias_shape]],
        in_specs=[SMEM] + [VMEM] * 7,
        out_specs=[pl.BlockSpec(memory_space=pl.ANY)] * len(held) + [VMEM],
        scratch_shapes=[pltpu.VMEM(shape, BF) for shape in held]
        + [
            pltpu.VMEM((full, nodes), BF),
            pltpu.VMEM((full, 2 * full), F32),
            pltpu.SemaphoreType.DMA((len(held),)),
        ],
        compiler_params=pltpu.CompilerParams(vmem_limit_bytes=VMEM_LIMIT),
        cost_estimate=pl.CostEstimate(flops=1000 * MIB, bytes_accessed=4 * MIB, transcendentals=0),
        name="layer",
    )(place, index, degree, mixed, *own_blocks)


def sum_slots(index_ref, arrived_ref, rows, start, size):
    parts = arrived_ref.shape[0]
    flat = arrived_ref[:, :rows, :].reshape(parts * rows, 128)
    ids = lax.broadcasted_iota(jnp.int32, (size, parts * rows), 0) + start
    sums = []
    for h in range(2):
        hits = jnp.where(ids == index_ref[h : h + 1, :], 1.0, 0.0).astype(BF)
        sums.append(jnp.dot(hits, flat, preferred_element_type=F32))
    return sums[0].T[:64] + sums[1].T[64:]


def mixed_kernel(rows, index_ref, arrived_ref, hub_ref, degree_ref, out_ref):
    size = 256
    for start in range(0, out_ref.shape[1], size):
        at = slice(start, start + size)
        tail = sum_slots(index_ref, arrived_ref, rows, start, size)
        out_ref[:, at] = (hub_ref[:, at] + tail / degree_ref[:, at].astype(F32)).astype(BF)


def mixed_sums(index, arrived, hub_sum, degree):
    parts, rows, _ = arrived.shape
    width, nodes = hub_sum.shape
    return call(
        partial(mixed_kernel, rows),
        jax.ShapeDtypeStruct((width, nodes), BF),
        [VMEM] * 4,
        [],
        "mixed",
        4 * parts * rows * nodes * 128,
        2,
    )(index, arrived, hub_sum, degree)


def tail_grad_kernel(rows, index_ref, arrived_ref, weight_ref, d_ref, out_ref):
    size = 256
    for start in range(0, out_ref.shape[1], size):
        at = slice(start, start + size)
        tail = sum_slots(index_ref, arrived_ref, rows, start, size)
        direct = jnp.dot(weight_ref[...], d_ref[:, at], preferred_element_type=F32)
        out_ref[:, at] = direct + tail


def tail_grads(index, arrived, weight, d_full, rows):
    parts = arrived.shape[0]
    width, nodes = weight.shape[0], d_full.shape[1]
    return call(
        partial(tail_grad_kernel, rows),
        jax.ShapeDtypeStruct((width, nodes), F32),
        [VMEM] * 4,
        [],
        "tail_grads",
        4 * parts * rows * nodes * 128,
        2,
    )(index, arrived, weight, d_full)


def own_kernel(feat_ref, cot_ref, self_ref, neigh_ref, bias_ref, out_ref):
    first = 0
    for ref in (feat_ref, cot_ref, self_ref, neigh_ref, bias_ref):
        out_ref[:, first : first + ref.shape[1]] = ref[...].astype(BF)
        first += ref.shape[1]


def own_block(*pieces):
    columns = sum(piece.shape[1] for piece in pieces)
    return call(
        own_kernel,
        jax.ShapeDtypeStruct((pieces[0].shape[0], columns), BF),
        [VMEM] * len(pieces),
        [],
        "own_block",
        0,
        0,
    )(*pieces)


def three_terms(values):
    high = lax.reduce_precision(values, 8, 7)
    rest = values - high
    middle = lax.reduce_precision(rest, 8, 7)
    return [high.astype(BF), middle.astype(BF), (rest - middle).astype(BF)]


def tile_index(x_ref, k, sizes, yh, z, sign):
    x_size, z_size = sizes
    x = lax.rem(x_ref[0] + (sign * k) % x_size, x_size)
    return (yh * x_size + x) * z_size + z


def fold_kernel(steps, sizes, has_base, x_ref, block_ref, mask_ref, *refs):
    hub_refs, (tile_ref, *base_ref, out_ref, total) = refs[: len(steps)], refs[len(steps) :]
    blocks = total.shape[0] - 1
    half = hub_refs[0].shape[1]
    lanes = lax.broadcasted_iota(jnp.int32, (half, 128), 1)
    first = (lanes < 64).astype(F32).astype(BF)
    second = (lanes >= 64).astype(F32).astype(BF)
    for b in range(blocks):
        at = slice(b * 128, (b + 1) * 128)
        total[b] = base_ref[0][:, at] if has_base else jnp.zeros_like(total[b])
    total[blocks] = jnp.zeros_like(total[blocks])
    z_size = sizes[1]
    for k, hub_ref in zip(steps, hub_refs):

        @pl.loop(0, hub_ref.shape[0] // z_size)
        def _(yh):
            for z in range(z_size):
                tile = tile_index(x_ref, k, sizes, yh, z, -1)
                rows = hub_ref[yh * z_size + z]
                weights = tile_ref[tile]
                product = jnp.dot(
                    jnp.concatenate([rows * first, rows * second], axis=0),
                    jnp.concatenate([weights, weights], axis=0),
                    preferred_element_type=F32,
                )
                dest = jnp.where(mask_ref[tile] > 0, block_ref[tile], blocks)
                total[dest] = total[dest] + product

    for b in range(blocks):
        out_ref[:, b * 128 : (b + 1) * 128] = total[b]


def fold_hubs(x_index, block, mask, hubs, steps, tiles, sizes, blocks, base):
    width = 2 * hubs[0].shape[1]
    bases = [] if base is None else [base]
    return call(
        partial(fold_kernel, steps, sizes, base is not None),
        jax.ShapeDtypeStruct((width, blocks * 128), F32),
        [SMEM, SMEM, SMEM] + [VMEM] * (len(hubs) + 1 + len(bases)),
        [pltpu.VMEM((blocks + 1, width, 128), F32)],
        "hub_sums",
        tiles.size * width * len(hubs),
        4,
    )(x_index, block, mask, *hubs, tiles, *bases)


def hub_grad_kernel(steps, sizes, x_ref, block_ref, mask_ref, grad_ref, bias_ref, tile_ref, *refs):
    *out_refs, blocked = refs
    blocks = blocked.shape[0] - 1
    for b in range(blocks):
        blocked[b] = grad_ref[:, b * 128 : (b + 1) * 128]
    blocked[blocks] = jnp.zeros_like(blocked[blocks])
    count, half, _ = out_refs[0].shape
    first = lax.broadcasted_iota(jnp.int32, (half, 128), 1) < 64
    z_size = sizes[1]
    for k, out_ref in zip(steps, out_refs):
        out_ref[count - 1] = bias_ref[...]

        @pl.loop(0, count // z_size)
        def _(yh):
            for z in range(z_size):
                tile = tile_index(x_ref, k, sizes, yh, z, 1)
                weights = tile_ref[tile]
                dest = jnp.where(mask_ref[tile] > 0, block_ref[tile], blocks)
                product = mm(
                    blocked[dest],
                    jnp.concatenate([weights, weights], axis=0),
                    BOTH_COLS,
                )
                out_ref[yh * z_size + z] = jnp.where(
                    first, product[:half], product[half:]
                ).astype(BF)


def hub_grad_terms(x_index, block, mask, grad, bias, tiles, steps, sizes, blocks):
    width = grad.shape[0]
    shape = (tiles.shape[0] // sizes[0] + 1, width // 2, 128)
    return call(
        partial(hub_grad_kernel, steps, sizes),
        [jax.ShapeDtypeStruct(shape, BF) for _ in steps],
        [SMEM, SMEM, SMEM, VMEM, VMEM, VMEM],
        [pltpu.VMEM((blocks + 1, width, 128), BF)],
        "hub_grad_terms",
        tiles.size * width * len(steps),
        4,
    )(x_index, block, mask, grad, bias, tiles)


def pack_kernel(*refs):
    *term_refs, sum_ref, out_ref = refs
    count, half = out_ref.shape[0], term_refs[0].shape[1]
    total = term_refs[0][...].astype(F32)
    for ref in term_refs[1:]:
        total = total + ref[...].astype(F32)
    out_ref[:, :half] = total[:count].astype(BF)
    bias = total[count]
    bias = jnp.broadcast_to(bias[0:1] + bias[1:2], (8, 128))
    high = bias.astype(BF).astype(F32)
    row = lax.broadcasted_iota(jnp.int32, (8, 128), 0)
    bias = jnp.where(row == 0, high, jnp.where(row == 1, bias - high, 0.0))
    extra = jnp.concatenate([sum_ref[...], bias], axis=0).astype(BF)
    out_ref[:, half:] = jnp.broadcast_to(extra[None], (count, 16, 128))


def pack_rows(terms, sums):
    count, half, _ = terms[0].shape
    return call(
        pack_kernel,
        jax.ShapeDtypeStruct((count - 1, half + 16, 128), BF),
        [VMEM] * (len(terms) + 1),
        [],
        "hub_grads_over_x",
        MIB,
        2,
    )(*terms, sums)


def final_kernel(second_ref, base_ref, out_ref, self_ref, neigh_ref, bias_ref):
    half = out_ref.shape[0] // 2
    hub = jnp.sum(second_ref[:, :half].astype(F32), axis=0)
    hub = jnp.concatenate([hub, pltpu.roll(hub, 64, 1)], axis=0)
    lane = lax.broadcasted_iota(jnp.int32, hub.shape, 1)
    out_ref[...] = base_ref[...] + jnp.where(lane < 64, hub, 0.0)
    extra = second_ref[:, half:].astype(F32)
    grads = extra[:, :8].reshape(-1, 128)
    rows = grads.shape[0] // 2
    for place, ref in enumerate((self_ref, neigh_ref)):
        turned = grads[place * rows : (place + 1) * rows].T
        ref[...] = jnp.concatenate([turned[:64], turned[64:]], axis=1)
    bias = jnp.sum(extra[:, 8:], axis=0)
    bias_ref[...] = (bias[0:1] + bias[1:2])[:, : bias_ref.shape[1]]


def finish(second, base, full):
    width, nodes = base.shape
    hub_part = pl.BlockSpec((width, 128), lambda i: (0, 0))
    return pl.pallas_call(
        final_kernel,
        out_shape=[
            jax.ShapeDtypeStruct((width, nodes), F32),
            jax.ShapeDtypeStruct((width, full), F32),
            jax.ShapeDtypeStruct((width, full), F32),
            jax.ShapeDtypeStruct((1, width), F32),
        ],
        grid=(1,),
        in_specs=[pl.BlockSpec(second.shape, lambda i: (0, 0, 0)), hub_part],
        out_specs=[hub_part]
        + [pl.BlockSpec((width, full), lambda i: (0, 0))] * 2
        + [pl.BlockSpec((1, width), lambda i: (0, 0))],
        input_output_aliases={1: 0},
        compiler_params=pltpu.CompilerParams(vmem_limit_bytes=VMEM_LIMIT),
        cost_estimate=pl.CostEstimate(flops=MIB, bytes_accessed=MIB, transcendentals=0),
        name="gradients",
    )(second, base)


def local(
    features,
    hub_weight,
    hub_block,
    hub_mask,
    tail_rows,
    tail_count,
    tail_target,
    degree,
    w_self,
    w_neigh,
    out_bias,
    cotangent,
):
    width, nodes = features.shape
    parts, hubs, tile_len = hub_weight.shape[1:]
    slots = tail_rows.shape[2]
    half_width = width // 2
    blocks = nodes // tile_len
    full_width = w_self.shape[0]
    x_size, z_size = lax.axis_size("x"), lax.axis_size("z")
    sizes = (x_size, z_size)
    plane = parts // x_size
    x_index = lax.axis_index("x")[None]
    tiles = hub_weight[0]
    hub_at = (x_index, hub_block[0], hub_mask[0])
    degree = degree[None, :]

    hub_piece = jnp.concatenate([features[:half_width, :hubs], features[half_width:, :hubs]], axis=1)
    hub_send = jnp.broadcast_to(hub_piece[None], (plane, half_width, 128))
    hub_plane = swap(hub_send, PLANE)

    slot_live = jnp.arange(slots, dtype=jnp.int32)[None, :] < tail_count[0][:, None]
    send_index = slot_rows(jnp.where(slot_live, tail_rows[0], -1))
    recv_index = slot_rows(tail_target[0])
    bias_terms = jnp.stack(three_terms(out_bias), axis=1)
    bias_terms = jnp.pad(bias_terms, ((0, 0), (0, 128 - bias_terms.shape[1])))
    feat_own, send_index, _ = lax.optimization_barrier((features, send_index, hub_send))
    own = own_block(feat_own, cotangent, w_self.T, w_neigh.T, bias_terms)
    near = (own, shift(own, "yl", 1), shift(own, "core", 1))
    tail_send = gather_slots(send_index, features, parts, slots)
    hub_plane, tail_send, recv_index, near = lax.optimization_barrier(
        (hub_plane, tail_send, recv_index, near)
    )
    arrived = swap(tail_send, DOM)
    hub_all = [hub_plane] + [shift(hub_plane, "x", k) for k in range(1, x_size)]
    own_blocks = [*near, shift(near[1], "core", 1)]
    place = lax.axis_index(REP) ^ jnp.array([0, 2, 1, 3], jnp.int32)

    fold = partial(fold_hubs, *hub_at, tiles=tiles, sizes=sizes, blocks=blocks)
    hub_sum = fold(hub_all[:2], (0, 1), base=None)
    hub_sum = fold(hub_all[2:], (2, 3), base=hub_sum)
    mixed = mixed_sums(recv_index, arrived, hub_sum, degree)
    full_mixed = lax.all_gather(mixed, REP, axis=0, tiled=True)

    output, d_full, mixed_grad, tail_back, w_self_rows, bias_rows = layer(
        place, recv_index, degree, full_mixed, own_blocks, sizes, parts, slots
    )
    tail_len = slots // 2
    first = swap(tail_back.reshape(parts, tail_len + 8, 128), DOM)

    hub_terms = partial(
        hub_grad_terms, *hub_at, mixed_grad, bias_rows, tiles, sizes=sizes, blocks=blocks
    )
    far_steps = (2, 1, 3)
    terms = [shift(term, "x", k) for term, k in zip(hub_terms(far_steps), far_steps)]
    terms = list(hub_terms((0,))) + terms
    sums = jnp.sum(first[:, tail_len:].astype(F32), axis=0)
    second = swap(pack_rows(terms, sums), PLANE)

    base = tail_grads(send_index, first, w_self_rows, d_full, tail_len)
    grad_features, grad_w_self, grad_w_neigh, grad_bias = finish(second, base, full_width)
    return (output, grad_features, grad_w_self.T, grad_w_neigh.T, grad_bias[0])


def solution(mesh):
    grid = (4, 4, mesh.shape["dom"] // 16, 2, 2)
    parted = Mesh(mesh.devices.reshape(grid), DOM + REP)
    in_specs = (
        P(REP, DOM),
        P(DOM, None, None, None),
        P(DOM, None),
        P(DOM, None),
        P(DOM, None, None),
        P(DOM, None),
        P(DOM, None, None),
        P(DOM),
        P(None, REP),
        P(None, REP),
        P(REP),
        P(REP, DOM),
    )
    out_specs = (P(REP, DOM), P(REP, DOM), P(None, REP), P(None, REP), P(REP))
    return jax.shard_map(local, mesh=parted, in_specs=in_specs, out_specs=out_specs, check_vma=False)
```

```python
from functools import partial

import jax
import jax.numpy as jnp
from jax import lax
from jax.experimental import pallas as pl
from jax.experimental.pallas import tpu as pltpu
from jax.sharding import Mesh
from jax.sharding import PartitionSpec as P

BF = jnp.bfloat16
F32 = jnp.float32
BOTH_ROWS = (((0,), (0,)), ((), ()))
BOTH_COLS = (((1,), (1,)), ((), ()))
DOM = ("yh", "x", "z")
PLANE = ("yh", "z")
REP = ("yl", "core")
SMEM = pl.BlockSpec(memory_space=pltpu.SMEM)
VMEM = pl.BlockSpec(memory_space=pltpu.VMEM)
MIB = 1024 * 1024
VMEM_LIMIT = 16 * MIB


def mm(a, b, dims):
    return lax.dot_general(a, b, dims, preferred_element_type=F32)


def swap(pieces, axis):
    return lax.all_to_all(pieces, axis, split_axis=0, concat_axis=0, tiled=True)


def shift(values, axis, step):
    size = lax.axis_size(axis)
    return lax.ppermute(values, axis, [(i, (i + step) % size) for i in range(size)])


def call(kernel, out_shape, in_specs, scratch, name, flops, mib):
    outs = VMEM if isinstance(out_shape, jax.ShapeDtypeStruct) else [VMEM] * len(out_shape)
    return pl.pallas_call(
        kernel,
        out_shape=out_shape,
        in_specs=in_specs,
        out_specs=outs,
        scratch_shapes=scratch,
        compiler_params=pltpu.CompilerParams(vmem_limit_bytes=VMEM_LIMIT),
        cost_estimate=pl.CostEstimate(flops=flops, bytes_accessed=mib * MIB, transcendentals=0),
        name=name,
    )


def slot_rows(index):
    parts, slots = index.shape
    return index.reshape(parts, 2, slots // 2).transpose(1, 0, 2).reshape(2, -1)


def pick_slots(index_ref, source, step):
    width, nodes = source.shape
    low_size = 256
    high_size = nodes // low_size
    split = jnp.concatenate(
        [source[:, i * low_size : (i + 1) * low_size] for i in range(high_size)], axis=0
    )
    low_ids = lax.broadcasted_iota(jnp.int32, (low_size, step), 0)
    for start in range(0, index_ref.shape[1], step):
        halves = []
        for h in range(2):
            index = index_ref[h : h + 1, start : start + step]
            hits = jnp.where(low_ids == (index & (low_size - 1)), 1.0, 0.0).astype(BF)
            found = jnp.dot(split, hits, preferred_element_type=F32)
            high = jnp.broadcast_to(index >> 8, (width, step))
            kept = jnp.zeros((width, step), F32)
            for i in range(high_size):
                kept = jnp.where(high == i, found[i * width : (i + 1) * width], kept)
            halves.append(kept)
        yield start, jnp.concatenate(halves, axis=0).T


def gather_kernel(index_ref, source_ref, out_ref):
    rows, step = out_ref.shape[1], 256
    for start, block in pick_slots(index_ref, source_ref[...], step):
        first = start // rows
        out_ref[first : first + step // rows] = block.reshape(-1, rows, 128).astype(BF)


def gather_slots(index, source, parts, slots):
    return call(
        gather_kernel,
        jax.ShapeDtypeStruct((parts, slots // 2, 128), BF),
        [VMEM, VMEM],
        [],
        "tail_rows_out",
        2 * parts * slots * 256 * 256,
        2,
    )(index, source)


def layer_kernel(sizes, place_ref, index_ref, degree_ref, mixed_ref, *refs):
    block_refs, refs = refs[:4], refs[4:]
    outs, (bias_ref, *held), (feat, low_rows, sems) = refs[:5], refs[5:11], refs[11:]
    output_ref, d_ref, grad_ref, send_ref, self_ref = held
    x_size, z_size = sizes
    width, nodes = output_ref.shape
    full = mixed_ref.shape[0]
    half = full // 2
    copies = [pltpu.make_async_copy(h, o, sems.at[i]) for i, (h, o) in enumerate(zip(held, outs))]
    own = place_ref[0]
    rows_of = [pl.ds(pl.multiple_of(place_ref[i] * width, width), width) for i in range(4)]
    for at, ref in zip(rows_of, block_refs):
        feat[at, :] = ref[:, :nodes]
        low_rows[at, :] = ref[:, 2 * nodes : 2 * nodes + 2 * full].astype(F32)

    own_weights = []
    for first in (0, full):
        rows = low_rows[:, first : first + width]
        for k in range(1, 4):
            start = first + k * width
            rows = jnp.where(own == k, low_rows[:, start : start + width], rows)
        own_weights.append(rows.T.astype(BF))
    self_ref[...] = own_weights[0]
    copies[4].start()

    mixed, full_feat = mixed_ref[...], feat[...]
    for i, (at, ref) in enumerate(zip(rows_of, block_refs)):
        first = 2 * nodes
        bias = ref[:, first + 2 * full :].astype(F32)
        pre = jnp.dot(ref[:, first : first + full], full_feat, preferred_element_type=F32)
        pre = pre + jnp.dot(
            ref[:, first + full : first + 2 * full], mixed, preferred_element_type=F32
        )
        pre = pre + jnp.sum(bias, axis=1, keepdims=True)
        sigma = jax.nn.sigmoid(pre)
        slope = sigma * (1.0 + pre * (1.0 - sigma))
        d_part = (ref[:, nodes : 2 * nodes].astype(F32) * slope).astype(BF)
        d_ref[at, :] = d_part
        if i == 0:
            d_pre = d_part
            output_ref[...] = (pre * sigma).astype(BF)
            copies[0].start()
    copies[1].start()

    grad = jnp.dot(own_weights[1], d_ref[...], preferred_element_type=F32).astype(BF)
    grad_ref[...] = grad
    copies[2].start()
    scaled = (grad.astype(F32) / degree_ref[...].astype(F32)).astype(BF)

    made = []
    for source in (full_feat, mixed):
        total = mm(source, d_pre, BOTH_COLS)
        total = jnp.concatenate([total[:half], total[half:]], axis=1)
        made.append(total.reshape(-1, z_size // 2, 16, 128))
    made = jnp.concatenate(made, axis=0)
    bias = mm(jnp.ones((bias_ref.shape[0], nodes), BF), d_pre, BOTH_COLS)
    bias = jnp.concatenate([bias, bias], axis=1)
    high = bias.astype(BF).astype(F32)
    row = lax.broadcasted_iota(jnp.int32, bias.shape, 0)
    bias_ref[...] = jnp.where(row == 0, high, jnp.where(row == 1, bias - high, 0.0)).astype(BF)

    rows = (send_ref.shape[1] - 16) // 2
    step = 256
    for start, block in pick_slots(index_ref, scaled, step):
        block = block.reshape(-1, 2, rows, 128)
        count = block.shape[0]
        first = start // (2 * rows)
        weight = made[first // (x_size * z_size // 2)]
        weight = jnp.concatenate([weight] * (count // weight.shape[0]), axis=0)
        block = jnp.concatenate([block[:, 0], weight[:, :8], block[:, 1], weight[:, 8:]], axis=1)
        send_ref[first : first + count] = block.astype(BF)
    copies[3].start()
    for copy in copies:
        copy.wait()


def layer(place, index, degree, mixed, own_blocks, sizes, parts, slots):
    full, nodes = mixed.shape
    width = own_blocks[0].shape[0]
    held = [
        (width, nodes),
        (full, nodes),
        (width, nodes),
        (parts // 2, slots + 16, 128),
        (width, full),
    ]
    bias_shape = (width // 2, 128)
    return pl.pallas_call(
        partial(layer_kernel, sizes),
        out_shape=[jax.ShapeDtypeStruct(shape, BF) for shape in [*held, bias_shape]],
        in_specs=[SMEM] + [VMEM] * 7,
        out_specs=[pl.BlockSpec(memory_space=pltpu.HBM)] * len(held) + [VMEM],
        scratch_shapes=[pltpu.VMEM(shape, BF) for shape in held]
        + [
            pltpu.VMEM((full, nodes), BF),
            pltpu.VMEM((full, 2 * full), F32),
            pltpu.SemaphoreType.DMA((len(held),)),
        ],
        compiler_params=pltpu.CompilerParams(vmem_limit_bytes=60 * MIB),
        cost_estimate=pl.CostEstimate(flops=1000 * MIB, bytes_accessed=4 * MIB, transcendentals=0),
        name="layer",
    )(place, index, degree, mixed, *own_blocks)


def sum_slots(index_ref, arrived_ref, rows, start, size):
    parts = arrived_ref.shape[0]
    flat = arrived_ref[:, :rows, :].reshape(parts * rows, 128)
    ids = lax.broadcasted_iota(jnp.int32, (size, parts * rows), 0) + start
    sums = []
    for h in range(2):
        hits = jnp.where(ids == index_ref[h : h + 1, :], 1.0, 0.0).astype(BF)
        sums.append(jnp.dot(hits, flat, preferred_element_type=F32))
    return sums[0].T[:64] + sums[1].T[64:]


def mixed_kernel(rows, index_ref, arrived_ref, hub_ref, degree_ref, out_ref):
    size = 256
    for start in range(0, out_ref.shape[1], size):
        at = slice(start, start + size)
        tail = sum_slots(index_ref, arrived_ref, rows, start, size)
        out_ref[:, at] = (hub_ref[:, at] + tail / degree_ref[:, at].astype(F32)).astype(BF)


def mixed_sums(index, arrived, hub_sum, degree):
    parts, rows, _ = arrived.shape
    width, nodes = hub_sum.shape
    return call(
        partial(mixed_kernel, rows),
        jax.ShapeDtypeStruct((width, nodes), BF),
        [VMEM] * 4,
        [],
        "mixed",
        4 * parts * rows * nodes * 128,
        2,
    )(index, arrived, hub_sum, degree)


def tail_grad_kernel(rows, index_ref, arrived_ref, weight_ref, d_ref, out_ref):
    size = 256
    for start in range(0, out_ref.shape[1], size):
        at = slice(start, start + size)
        tail = sum_slots(index_ref, arrived_ref, rows, start, size)
        direct = jnp.dot(weight_ref[...], d_ref[:, at], preferred_element_type=F32)
        out_ref[:, at] = direct + tail


def tail_grads(index, arrived, weight, d_full, rows):
    parts = arrived.shape[0]
    width, nodes = weight.shape[0], d_full.shape[1]
    return call(
        partial(tail_grad_kernel, rows),
        jax.ShapeDtypeStruct((width, nodes), F32),
        [VMEM] * 4,
        [],
        "tail_grads",
        4 * parts * rows * nodes * 128,
        2,
    )(index, arrived, weight, d_full)


def own_kernel(feat_ref, cot_ref, self_ref, neigh_ref, bias_ref, out_ref):
    first = 0
    for ref in (feat_ref, cot_ref, self_ref, neigh_ref, bias_ref):
        out_ref[:, first : first + ref.shape[1]] = ref[...].astype(BF)
        first += ref.shape[1]


def own_block(*pieces):
    columns = sum(piece.shape[1] for piece in pieces)
    return call(
        own_kernel,
        jax.ShapeDtypeStruct((pieces[0].shape[0], columns), BF),
        [VMEM] * len(pieces),
        [],
        "own_block",
        0,
        0,
    )(*pieces)


def three_terms(values):
    high = lax.reduce_precision(values, 8, 7)
    rest = values - high
    middle = lax.reduce_precision(rest, 8, 7)
    return [high.astype(BF), middle.astype(BF), (rest - middle).astype(BF)]


def tile_index(x_ref, k, sizes, yh, z, sign):
    x_size, z_size = sizes
    x = lax.rem(x_ref[0] + (sign * k) % x_size, x_size)
    return (yh * x_size + x) * z_size + z


def fold_kernel(steps, sizes, has_base, x_ref, block_ref, mask_ref, *refs):
    hub_refs, (tile_ref, *base_ref, out_ref, total) = refs[: len(steps)], refs[len(steps) :]
    blocks = total.shape[0] - 1
    half = hub_refs[0].shape[1]
    lanes = lax.broadcasted_iota(jnp.int32, (half, 128), 1)
    first = (lanes < 64).astype(F32).astype(BF)
    second = (lanes >= 64).astype(F32).astype(BF)
    for b in range(blocks):
        at = slice(b * 128, (b + 1) * 128)
        total[b] = base_ref[0][:, at] if has_base else jnp.zeros_like(total[b])
    total[blocks] = jnp.zeros_like(total[blocks])
    z_size = sizes[1]
    for k, hub_ref in zip(steps, hub_refs):

        @pl.loop(0, hub_ref.shape[0] // z_size)
        def _(yh):
            for z in range(z_size):
                tile = tile_index(x_ref, k, sizes, yh, z, -1)
                rows = hub_ref[yh * z_size + z]
                weights = tile_ref[tile]
                product = jnp.dot(
                    jnp.concatenate([rows * first, rows * second], axis=0),
                    jnp.concatenate([weights, weights], axis=0),
                    preferred_element_type=F32,
                )
                dest = jnp.where(mask_ref[tile] > 0, block_ref[tile], blocks)
                total[dest] = total[dest] + product

    for b in range(blocks):
        out_ref[:, b * 128 : (b + 1) * 128] = total[b]


def fold_hubs(x_index, block, mask, hubs, steps, tiles, sizes, blocks, base):
    width = 2 * hubs[0].shape[1]
    bases = [] if base is None else [base]
    return call(
        partial(fold_kernel, steps, sizes, base is not None),
        jax.ShapeDtypeStruct((width, blocks * 128), F32),
        [SMEM, SMEM, SMEM] + [VMEM] * (len(hubs) + 1 + len(bases)),
        [pltpu.VMEM((blocks + 1, width, 128), F32)],
        "hub_sums",
        tiles.size * width * len(hubs),
        4,
    )(x_index, block, mask, *hubs, tiles, *bases)


def hub_grad_kernel(steps, sizes, x_ref, block_ref, mask_ref, grad_ref, bias_ref, tile_ref, *refs):
    *out_refs, blocked = refs
    blocks = blocked.shape[0] - 1
    for b in range(blocks):
        blocked[b] = grad_ref[:, b * 128 : (b + 1) * 128]
    blocked[blocks] = jnp.zeros_like(blocked[blocks])
    count, half, _ = out_refs[0].shape
    first = lax.broadcasted_iota(jnp.int32, (half, 128), 1) < 64
    z_size = sizes[1]
    for k, out_ref in zip(steps, out_refs):
        out_ref[count - 1] = bias_ref[...]

        @pl.loop(0, count // z_size)
        def _(yh):
            for z in range(z_size):
                tile = tile_index(x_ref, k, sizes, yh, z, 1)
                weights = tile_ref[tile]
                dest = jnp.where(mask_ref[tile] > 0, block_ref[tile], blocks)
                product = mm(
                    blocked[dest],
                    jnp.concatenate([weights, weights], axis=0),
                    BOTH_COLS,
                )
                out_ref[yh * z_size + z] = jnp.where(
                    first, product[:half], product[half:]
                ).astype(BF)


def hub_grad_terms(x_index, block, mask, grad, bias, tiles, steps, sizes, blocks):
    width = grad.shape[0]
    shape = (tiles.shape[0] // sizes[0] + 1, width // 2, 128)
    return call(
        partial(hub_grad_kernel, steps, sizes),
        [jax.ShapeDtypeStruct(shape, BF) for _ in steps],
        [SMEM, SMEM, SMEM, VMEM, VMEM, VMEM],
        [pltpu.VMEM((blocks + 1, width, 128), BF)],
        "hub_grad_terms",
        tiles.size * width * len(steps),
        4,
    )(x_index, block, mask, grad, bias, tiles)


def pack_kernel(*refs):
    *term_refs, sum_ref, out_ref = refs
    count, half = out_ref.shape[0], term_refs[0].shape[1]
    total = term_refs[0][...].astype(F32)
    for ref in term_refs[1:]:
        total = total + ref[...].astype(F32)
    out_ref[:, :half] = total[:count].astype(BF)
    bias = total[count]
    bias = jnp.broadcast_to(bias[0:1] + bias[1:2], (8, 128))
    high = bias.astype(BF).astype(F32)
    row = lax.broadcasted_iota(jnp.int32, (8, 128), 0)
    bias = jnp.where(row == 0, high, jnp.where(row == 1, bias - high, 0.0))
    extra = jnp.concatenate([sum_ref[...], bias], axis=0).astype(BF)
    out_ref[:, half:] = jnp.broadcast_to(extra[None], (count, 16, 128))


def pack_rows(terms, sums):
    count, half, _ = terms[0].shape
    return call(
        pack_kernel,
        jax.ShapeDtypeStruct((count - 1, half + 16, 128), BF),
        [VMEM] * (len(terms) + 1),
        [],
        "hub_grads_over_x",
        MIB,
        2,
    )(*terms, sums)


def final_kernel(second_ref, base_ref, out_ref, self_ref, neigh_ref, bias_ref):
    half = out_ref.shape[0] // 2
    hub = jnp.sum(second_ref[:, :half].astype(F32), axis=0)
    hub = jnp.concatenate([hub, pltpu.roll(hub, 64, 1)], axis=0)
    lane = lax.broadcasted_iota(jnp.int32, hub.shape, 1)
    out_ref[...] = base_ref[...] + jnp.where(lane < 64, hub, 0.0)
    extra = second_ref[:, half:].astype(F32)
    grads = extra[:, :8].reshape(-1, 128)
    rows = grads.shape[0] // 2
    for place, ref in enumerate((self_ref, neigh_ref)):
        turned = grads[place * rows : (place + 1) * rows].T
        ref[...] = jnp.concatenate([turned[:64], turned[64:]], axis=1)
    bias = jnp.sum(extra[:, 8:], axis=0)
    bias_ref[...] = (bias[0:1] + bias[1:2])[:, : bias_ref.shape[1]]


def finish(second, base, full):
    width, nodes = base.shape
    hub_part = pl.BlockSpec((width, 128), lambda i: (0, 0))
    return pl.pallas_call(
        final_kernel,
        out_shape=[
            jax.ShapeDtypeStruct((width, nodes), F32),
            jax.ShapeDtypeStruct((width, full), F32),
            jax.ShapeDtypeStruct((width, full), F32),
            jax.ShapeDtypeStruct((1, width), F32),
        ],
        grid=(1,),
        in_specs=[pl.BlockSpec(second.shape, lambda i: (0, 0, 0)), hub_part],
        out_specs=[hub_part]
        + [pl.BlockSpec((width, full), lambda i: (0, 0))] * 2
        + [pl.BlockSpec((1, width), lambda i: (0, 0))],
        input_output_aliases={1: 0},
        compiler_params=pltpu.CompilerParams(vmem_limit_bytes=VMEM_LIMIT),
        cost_estimate=pl.CostEstimate(flops=MIB, bytes_accessed=MIB, transcendentals=0),
        name="gradients",
    )(second, base)


def local(
    features,
    hub_weight,
    hub_block,
    hub_mask,
    tail_rows,
    tail_count,
    tail_target,
    degree,
    w_self,
    w_neigh,
    out_bias,
    cotangent,
):
    width, nodes = features.shape
    parts, hubs, tile_len = hub_weight.shape[1:]
    slots = tail_rows.shape[2]
    half_width = width // 2
    blocks = nodes // tile_len
    full_width = w_self.shape[0]
    x_size, z_size = lax.axis_size("x"), lax.axis_size("z")
    sizes = (x_size, z_size)
    plane = parts // x_size
    x_index = lax.axis_index("x")[None]
    tiles = hub_weight[0]
    hub_at = (x_index, hub_block[0], hub_mask[0])
    degree = degree[None, :]

    hub_piece = jnp.concatenate([features[:half_width, :hubs], features[half_width:, :hubs]], axis=1)
    hub_send = jnp.broadcast_to(hub_piece[None], (plane, half_width, 128))
    hub_plane = swap(hub_send, PLANE)

    slot_live = jnp.arange(slots, dtype=jnp.int32)[None, :] < tail_count[0][:, None]
    send_index = slot_rows(jnp.where(slot_live, tail_rows[0], -1))
    recv_index = slot_rows(tail_target[0])
    bias_terms = jnp.stack(three_terms(out_bias), axis=1)
    bias_terms = jnp.pad(bias_terms, ((0, 0), (0, 128 - bias_terms.shape[1])))
    feat_own, send_index, _ = lax.optimization_barrier((features, send_index, hub_send))
    own = own_block(feat_own, cotangent, w_self.T, w_neigh.T, bias_terms)
    across = shift(own, "core", 1)
    tail_send = gather_slots(send_index, features, parts, slots)
    hub_plane, tail_send, recv_index, own, across = lax.optimization_barrier(
        (hub_plane, tail_send, recv_index, own, across)
    )
    arrived = swap(tail_send, DOM)
    hub_all = [hub_plane] + [shift(hub_plane, "x", k) for k in range(1, x_size)]
    near = shift(own, "yl", 1)
    own_blocks = [own, near, across, shift(near, "core", 1)]
    place = lax.axis_index(REP) ^ jnp.array([0, 2, 1, 3], jnp.int32)

    fold = partial(fold_hubs, *hub_at, tiles=tiles, sizes=sizes, blocks=blocks)
    hub_sum = fold(hub_all[:2], (0, 1), base=None)
    hub_sum = fold(hub_all[2:], (2, 3), base=hub_sum)
    mixed = mixed_sums(recv_index, arrived, hub_sum, degree)
    full_mixed = lax.all_gather(mixed, REP, axis=0, tiled=True)

    output, d_full, mixed_grad, tail_back, w_self_rows, bias_rows = layer(
        place, recv_index, degree, full_mixed, own_blocks, sizes, parts, slots
    )
    tail_len = slots // 2
    first = swap(tail_back.reshape(parts, tail_len + 8, 128), DOM)

    hub_terms = partial(
        hub_grad_terms, *hub_at, mixed_grad, bias_rows, tiles, sizes=sizes, blocks=blocks
    )
    far_steps = (2, 1, 3)
    terms = [shift(term, "x", k) for term, k in zip(hub_terms(far_steps), far_steps)]
    terms = list(hub_terms((0,))) + terms
    sums = jnp.sum(first[:, tail_len:].astype(F32), axis=0)
    second = swap(pack_rows(terms, sums), PLANE)

    base = tail_grads(send_index, first, w_self_rows, d_full, tail_len)
    grad_features, grad_w_self, grad_w_neigh, grad_bias = finish(second, base, full_width)
    return (output, grad_features, grad_w_self.T, grad_w_neigh.T, grad_bias[0])


def solution(mesh):
    grid = (4, 4, mesh.shape["dom"] // 16, 2, 2)
    parted = Mesh(mesh.devices.reshape(grid), DOM + REP)
    in_specs = (
        P(REP, DOM),
        P(DOM, None, None, None),
        P(DOM, None),
        P(DOM, None),
        P(DOM, None, None),
        P(DOM, None),
        P(DOM, None, None),
        P(DOM),
        P(None, REP),
        P(None, REP),
        P(REP),
        P(REP, DOM),
    )
    out_specs = (P(REP, DOM), P(REP, DOM), P(None, REP), P(None, REP), P(REP))
    return jax.shard_map(local, mesh=parted, in_specs=in_specs, out_specs=out_specs, check_vma=False)
```

```python
from functools import partial

import jax
import jax.numpy as jnp
from jax import lax
from jax.experimental import pallas as pl
from jax.experimental.pallas import tpu as pltpu
from jax.sharding import Mesh
from jax.sharding import PartitionSpec as P

BF = jnp.bfloat16
F32 = jnp.float32
BOTH_ROWS = (((0,), (0,)), ((), ()))
BOTH_COLS = (((1,), (1,)), ((), ()))
DOM = ("yh", "x", "z")
PLANE = ("yh", "z")
REP = ("yl", "core")
SMEM = pl.BlockSpec(memory_space=pltpu.SMEM)
VMEM = pl.BlockSpec(memory_space=pltpu.VMEM)
MIB = 1024 * 1024
VMEM_LIMIT = 16 * MIB


def mm(a, b, dims):
    return lax.dot_general(a, b, dims, preferred_element_type=F32)


def swap(pieces, axis):
    return lax.all_to_all(pieces, axis, split_axis=0, concat_axis=0, tiled=True)


def shift(values, axis, step):
    size = lax.axis_size(axis)
    return lax.ppermute(values, axis, [(i, (i + step) % size) for i in range(size)])


def call(kernel, out_shape, in_specs, scratch, name, flops, mib, limit=VMEM_LIMIT):
    outs = VMEM if isinstance(out_shape, jax.ShapeDtypeStruct) else [VMEM] * len(out_shape)
    return pl.pallas_call(
        kernel,
        out_shape=out_shape,
        in_specs=in_specs,
        out_specs=outs,
        scratch_shapes=scratch,
        compiler_params=pltpu.CompilerParams(vmem_limit_bytes=limit),
        cost_estimate=pl.CostEstimate(flops=flops, bytes_accessed=mib * MIB, transcendentals=0),
        name=name,
    )


def slot_rows(index):
    parts, slots = index.shape
    return index.reshape(parts, 2, slots // 2).transpose(1, 0, 2).reshape(2, -1)


def pick_slots(index_ref, source, step):
    width, nodes = source.shape
    low_size = 256
    high_size = nodes // low_size
    split = jnp.concatenate(
        [source[:, i * low_size : (i + 1) * low_size] for i in range(high_size)], axis=0
    )
    low_ids = lax.broadcasted_iota(jnp.int32, (low_size, step), 0)
    for start in range(0, index_ref.shape[1], step):
        halves = []
        for h in range(2):
            index = index_ref[h : h + 1, start : start + step]
            hits = jnp.where(low_ids == (index & (low_size - 1)), 1.0, 0.0).astype(BF)
            found = jnp.dot(split, hits, preferred_element_type=F32)
            high = jnp.broadcast_to(index >> 8, (width, step))
            kept = jnp.zeros((width, step), F32)
            for i in range(high_size):
                kept = jnp.where(high == i, found[i * width : (i + 1) * width], kept)
            halves.append(kept)
        yield start, jnp.concatenate(halves, axis=0).T


def gather_kernel(index_ref, source_ref, out_ref):
    rows, step = out_ref.shape[1], 256
    for start, block in pick_slots(index_ref, source_ref[...], step):
        first = start // rows
        out_ref[first : first + step // rows] = block.reshape(-1, rows, 128).astype(BF)


def gather_slots(index, source, parts, slots):
    return call(
        gather_kernel,
        jax.ShapeDtypeStruct((parts, slots // 2, 128), BF),
        [VMEM, VMEM],
        [],
        "tail_rows_out",
        2 * parts * slots * 256 * 256,
        2,
    )(index, source)


def layer_kernel(sizes, place_ref, index_ref, degree_ref, mixed_ref, *refs):
    block_refs, refs = refs[:4], refs[4:]
    outs, (bias_ref, *held), (feat, low_rows, sems) = refs[:5], refs[5:11], refs[11:]
    output_ref, d_ref, grad_ref, send_ref, self_ref = held
    x_size, z_size = sizes
    width, nodes = output_ref.shape
    full = mixed_ref.shape[0]
    half = full // 2
    copies = [pltpu.make_async_copy(h, o, sems.at[i]) for i, (h, o) in enumerate(zip(held, outs))]
    own = place_ref[0]
    rows_of = [pl.ds(pl.multiple_of(place_ref[i] * width, width), width) for i in range(4)]
    for at, ref in zip(rows_of, block_refs):
        feat[at, :] = ref[:, :nodes]
        low_rows[at, :] = ref[:, 2 * nodes : 2 * nodes + 2 * full].astype(F32)

    own_weights = []
    for first in (0, full):
        rows = low_rows[:, first : first + width]
        for k in range(1, 4):
            start = first + k * width
            rows = jnp.where(own == k, low_rows[:, start : start + width], rows)
        own_weights.append(rows.T.astype(BF))
    self_ref[...] = own_weights[0]
    copies[4].start()

    mixed, full_feat = mixed_ref[...], feat[...]
    for i, (at, ref) in enumerate(zip(rows_of, block_refs)):
        first = 2 * nodes
        bias = ref[:, first + 2 * full :].astype(F32)
        pre = jnp.dot(ref[:, first : first + full], full_feat, preferred_element_type=F32)
        pre = pre + jnp.dot(
            ref[:, first + full : first + 2 * full], mixed, preferred_element_type=F32
        )
        pre = pre + jnp.sum(bias, axis=1, keepdims=True)
        sigma = jax.nn.sigmoid(pre)
        slope = sigma * (1.0 + pre * (1.0 - sigma))
        d_part = (ref[:, nodes : 2 * nodes].astype(F32) * slope).astype(BF)
        d_ref[at, :] = d_part
        if i == 0:
            d_pre = d_part
            output_ref[...] = (pre * sigma).astype(BF)
            copies[0].start()
    copies[1].start()

    grad = jnp.dot(own_weights[1], d_ref[...], preferred_element_type=F32).astype(BF)
    grad_ref[...] = grad
    copies[2].start()
    scaled = (grad.astype(F32) / degree_ref[...].astype(F32)).astype(BF)

    made = []
    for source in (full_feat, mixed):
        total = mm(source, d_pre, BOTH_COLS)
        total = jnp.concatenate([total[:half], total[half:]], axis=1)
        made.append(total.reshape(-1, z_size // 2, 16, 128))
    made = jnp.concatenate(made, axis=0)
    bias = mm(jnp.ones((bias_ref.shape[0], nodes), BF), d_pre, BOTH_COLS)
    bias = jnp.concatenate([bias, bias], axis=1)
    high = bias.astype(BF).astype(F32)
    row = lax.broadcasted_iota(jnp.int32, bias.shape, 0)
    bias_ref[...] = jnp.where(row == 0, high, jnp.where(row == 1, bias - high, 0.0)).astype(BF)

    rows = (send_ref.shape[1] - 16) // 2
    step = 256
    for start, block in pick_slots(index_ref, scaled, step):
        block = block.reshape(-1, 2, rows, 128)
        count = block.shape[0]
        first = start // (2 * rows)
        weight = made[first // (x_size * z_size // 2)]
        weight = jnp.concatenate([weight] * (count // weight.shape[0]), axis=0)
        block = jnp.concatenate([block[:, 0], weight[:, :8], block[:, 1], weight[:, 8:]], axis=1)
        send_ref[first : first + count] = block.astype(BF)
    copies[3].start()
    for copy in copies:
        copy.wait()


def layer(place, index, degree, mixed, own_blocks, sizes, parts, slots):
    full, nodes = mixed.shape
    width = own_blocks[0].shape[0]
    held = [
        (width, nodes),
        (full, nodes),
        (width, nodes),
        (parts // 2, slots + 16, 128),
        (width, full),
    ]
    bias_shape = (width // 2, 128)
    return pl.pallas_call(
        partial(layer_kernel, sizes),
        out_shape=[jax.ShapeDtypeStruct(shape, BF) for shape in [*held, bias_shape]],
        in_specs=[SMEM] + [VMEM] * 7,
        out_specs=[pl.BlockSpec(memory_space=pltpu.HBM)] * len(held) + [VMEM],
        scratch_shapes=[pltpu.VMEM(shape, BF) for shape in held]
        + [
            pltpu.VMEM((full, nodes), BF),
            pltpu.VMEM((full, 2 * full), F32),
            pltpu.SemaphoreType.DMA((len(held),)),
        ],
        compiler_params=pltpu.CompilerParams(vmem_limit_bytes=60 * MIB),
        cost_estimate=pl.CostEstimate(flops=1000 * MIB, bytes_accessed=4 * MIB, transcendentals=0),
        name="layer",
    )(place, index, degree, mixed, *own_blocks)


def sum_slots(index_ref, arrived_ref, rows, start, size):
    parts = arrived_ref.shape[0]
    flat = arrived_ref[:, :rows, :].reshape(parts * rows, 128)
    ids = lax.broadcasted_iota(jnp.int32, (size, parts * rows), 0) + start
    sums = []
    for h in range(2):
        hits = jnp.where(ids == index_ref[h : h + 1, :], 1.0, 0.0).astype(BF)
        sums.append(jnp.dot(hits, flat, preferred_element_type=F32))
    return sums[0].T[:64] + sums[1].T[64:]


def mixed_kernel(rows, index_ref, arrived_ref, hub_ref, degree_ref, out_ref):
    size = 256
    for start in range(0, out_ref.shape[1], size):
        at = slice(start, start + size)
        tail = sum_slots(index_ref, arrived_ref, rows, start, size)
        out_ref[:, at] = (hub_ref[:, at] + tail / degree_ref[:, at].astype(F32)).astype(BF)


def mixed_sums(index, arrived, hub_sum, degree):
    parts, rows, _ = arrived.shape
    width, nodes = hub_sum.shape
    return call(
        partial(mixed_kernel, rows),
        jax.ShapeDtypeStruct((width, nodes), BF),
        [VMEM] * 4,
        [],
        "mixed",
        4 * parts * rows * nodes * 128,
        2,
    )(index, arrived, hub_sum, degree)


def tail_grad_kernel(rows, index_ref, arrived_ref, weight_ref, d_ref, out_ref):
    size = 256
    for start in range(0, out_ref.shape[1], size):
        at = slice(start, start + size)
        tail = sum_slots(index_ref, arrived_ref, rows, start, size)
        direct = jnp.dot(weight_ref[...], d_ref[:, at], preferred_element_type=F32)
        out_ref[:, at] = direct + tail


def tail_grads(index, arrived, weight, d_full, rows):
    parts = arrived.shape[0]
    width, nodes = weight.shape[0], d_full.shape[1]
    return call(
        partial(tail_grad_kernel, rows),
        jax.ShapeDtypeStruct((width, nodes), F32),
        [VMEM] * 4,
        [],
        "tail_grads",
        4 * parts * rows * nodes * 128,
        2,
    )(index, arrived, weight, d_full)


def own_kernel(feat_ref, cot_ref, self_ref, neigh_ref, bias_ref, out_ref):
    first = 0
    for ref in (feat_ref, cot_ref, self_ref, neigh_ref, bias_ref):
        out_ref[:, first : first + ref.shape[1]] = ref[...].astype(BF)
        first += ref.shape[1]


def own_block(*pieces):
    columns = sum(piece.shape[1] for piece in pieces)
    return call(
        own_kernel,
        jax.ShapeDtypeStruct((pieces[0].shape[0], columns), BF),
        [VMEM] * len(pieces),
        [],
        "own_block",
        0,
        0,
    )(*pieces)


def three_terms(values):
    high = lax.reduce_precision(values, 8, 7)
    rest = values - high
    middle = lax.reduce_precision(rest, 8, 7)
    return [high.astype(BF), middle.astype(BF), (rest - middle).astype(BF)]


def tile_index(x_ref, k, sizes, yh, z, sign):
    x_size, z_size = sizes
    x = lax.rem(x_ref[0] + (sign * k) % x_size, x_size)
    return (yh * x_size + x) * z_size + z


def fold_kernel(steps, sizes, has_base, x_ref, block_ref, mask_ref, *refs):
    hub_refs, (tile_ref, *base_ref, out_ref, total) = refs[: len(steps)], refs[len(steps) :]
    blocks = total.shape[0] - 1
    half = hub_refs[0].shape[1]
    lanes = lax.broadcasted_iota(jnp.int32, (half, 128), 1)
    first = (lanes < 64).astype(F32).astype(BF)
    second = (lanes >= 64).astype(F32).astype(BF)
    for b in range(blocks):
        at = slice(b * 128, (b + 1) * 128)
        total[b] = base_ref[0][:, at] if has_base else jnp.zeros_like(total[b])
    total[blocks] = jnp.zeros_like(total[blocks])
    z_size = sizes[1]
    for k, hub_ref in zip(steps, hub_refs):

        @pl.loop(0, hub_ref.shape[0] // z_size)
        def _(yh):
            for z in range(z_size):
                tile = tile_index(x_ref, k, sizes, yh, z, -1)
                rows = hub_ref[yh * z_size + z]
                weights = tile_ref[tile]
                product = jnp.dot(
                    jnp.concatenate([rows * first, rows * second], axis=0),
                    jnp.concatenate([weights, weights], axis=0),
                    preferred_element_type=F32,
                )
                dest = jnp.where(mask_ref[tile] > 0, block_ref[tile], blocks)
                total[dest] = total[dest] + product

    for b in range(blocks):
        out_ref[:, b * 128 : (b + 1) * 128] = total[b]


def fold_hubs(x_index, block, mask, hubs, steps, tiles, sizes, blocks, base):
    width = 2 * hubs[0].shape[1]
    bases = [] if base is None else [base]
    return call(
        partial(fold_kernel, steps, sizes, base is not None),
        jax.ShapeDtypeStruct((width, blocks * 128), F32),
        [SMEM, SMEM, SMEM] + [VMEM] * (len(hubs) + 1 + len(bases)),
        [pltpu.VMEM((blocks + 1, width, 128), F32)],
        "hub_sums",
        tiles.size * width * len(hubs),
        4,
    )(x_index, block, mask, *hubs, tiles, *bases)


def hub_grad_kernel(steps, sizes, x_ref, block_ref, mask_ref, grad_ref, bias_ref, tile_ref, *refs):
    *out_refs, blocked = refs
    blocks = blocked.shape[0] - 1
    for b in range(blocks):
        blocked[b] = grad_ref[:, b * 128 : (b + 1) * 128]
    blocked[blocks] = jnp.zeros_like(blocked[blocks])
    count, half, _ = out_refs[0].shape
    first = lax.broadcasted_iota(jnp.int32, (half, 128), 1) < 64
    z_size = sizes[1]
    for k, out_ref in zip(steps, out_refs):
        out_ref[count - 1] = bias_ref[...]

        @pl.loop(0, count // z_size)
        def _(yh):
            for z in range(0, z_size, 2):
                tile = tile_index(x_ref, k, sizes, yh, z, 1)
                dests = [
                    jnp.where(mask_ref[tile + i] > 0, block_ref[tile + i], blocks) for i in range(2)
                ]
                product = mm(
                    jnp.concatenate([blocked[dest] for dest in dests], axis=0),
                    jnp.concatenate([tile_ref[tile], tile_ref[tile + 1]], axis=0),
                    BOTH_COLS,
                )
                turned = pltpu.roll(product[half : 3 * half], 64, 1)
                place = yh * z_size + z
                out_ref[place] = jnp.where(first, product[:half], turned[:half]).astype(BF)
                out_ref[place + 1] = jnp.where(first, turned[half:], product[3 * half :]).astype(BF)


def hub_grad_terms(x_index, block, mask, grad, bias, tiles, steps, sizes, blocks):
    width = grad.shape[0]
    shape = (tiles.shape[0] // sizes[0] + 1, width // 2, 128)
    return call(
        partial(hub_grad_kernel, steps, sizes),
        [jax.ShapeDtypeStruct(shape, BF) for _ in steps],
        [SMEM, SMEM, SMEM, VMEM, VMEM, VMEM],
        [pltpu.VMEM((blocks + 1, width, 128), BF)],
        "hub_grad_terms",
        tiles.size * width * len(steps),
        4,
        60 * MIB,
    )(x_index, block, mask, grad, bias, tiles)


def pack_kernel(*refs):
    *term_refs, sum_ref, out_ref = refs
    count, half = out_ref.shape[0], term_refs[0].shape[1]
    total = term_refs[0][...].astype(F32)
    for ref in term_refs[1:]:
        total = total + ref[...].astype(F32)
    out_ref[:, :half] = total[:count].astype(BF)
    bias = total[count]
    bias = jnp.broadcast_to(bias[0:1] + bias[1:2], (8, 128))
    high = bias.astype(BF).astype(F32)
    row = lax.broadcasted_iota(jnp.int32, (8, 128), 0)
    bias = jnp.where(row == 0, high, jnp.where(row == 1, bias - high, 0.0))
    extra = jnp.concatenate([sum_ref[...], bias], axis=0).astype(BF)
    out_ref[:, half:] = jnp.broadcast_to(extra[None], (count, 16, 128))


def pack_rows(terms, sums):
    count, half, _ = terms[0].shape
    return call(
        pack_kernel,
        jax.ShapeDtypeStruct((count - 1, half + 16, 128), BF),
        [VMEM] * (len(terms) + 1),
        [],
        "hub_grads_over_x",
        MIB,
        2,
    )(*terms, sums)


def final_kernel(second_ref, base_ref, out_ref, self_ref, neigh_ref, bias_ref):
    half = out_ref.shape[0] // 2
    hub = jnp.sum(second_ref[:, :half].astype(F32), axis=0)
    hub = jnp.concatenate([hub, pltpu.roll(hub, 64, 1)], axis=0)
    lane = lax.broadcasted_iota(jnp.int32, hub.shape, 1)
    out_ref[...] = base_ref[...] + jnp.where(lane < 64, hub, 0.0)
    extra = second_ref[:, half:].astype(F32)
    grads = extra[:, :8].reshape(-1, 128)
    rows = grads.shape[0] // 2
    for place, ref in enumerate((self_ref, neigh_ref)):
        turned = grads[place * rows : (place + 1) * rows].T
        ref[...] = jnp.concatenate([turned[:64], turned[64:]], axis=1)
    bias = jnp.sum(extra[:, 8:], axis=0)
    bias_ref[...] = (bias[0:1] + bias[1:2])[:, : bias_ref.shape[1]]


def finish(second, base, full):
    width, nodes = base.shape
    hub_part = pl.BlockSpec((width, 128), lambda i: (0, 0))
    return pl.pallas_call(
        final_kernel,
        out_shape=[
            jax.ShapeDtypeStruct((width, nodes), F32),
            jax.ShapeDtypeStruct((width, full), F32),
            jax.ShapeDtypeStruct((width, full), F32),
            jax.ShapeDtypeStruct((1, width), F32),
        ],
        grid=(1,),
        in_specs=[pl.BlockSpec(second.shape, lambda i: (0, 0, 0)), hub_part],
        out_specs=[hub_part]
        + [pl.BlockSpec((width, full), lambda i: (0, 0))] * 2
        + [pl.BlockSpec((1, width), lambda i: (0, 0))],
        input_output_aliases={1: 0},
        compiler_params=pltpu.CompilerParams(vmem_limit_bytes=VMEM_LIMIT),
        cost_estimate=pl.CostEstimate(flops=MIB, bytes_accessed=MIB, transcendentals=0),
        name="gradients",
    )(second, base)


def local(
    features,
    hub_weight,
    hub_block,
    hub_mask,
    tail_rows,
    tail_count,
    tail_target,
    degree,
    w_self,
    w_neigh,
    out_bias,
    cotangent,
):
    width, nodes = features.shape
    parts, hubs, tile_len = hub_weight.shape[1:]
    slots = tail_rows.shape[2]
    half_width = width // 2
    blocks = nodes // tile_len
    full_width = w_self.shape[0]
    x_size, z_size = lax.axis_size("x"), lax.axis_size("z")
    sizes = (x_size, z_size)
    plane = parts // x_size
    x_index = lax.axis_index("x")[None]
    tiles = hub_weight[0]
    hub_at = (x_index, hub_block[0], hub_mask[0])
    degree = degree[None, :]

    hub_piece = jnp.concatenate([features[:half_width, :hubs], features[half_width:, :hubs]], axis=1)
    hub_send = jnp.broadcast_to(hub_piece[None], (plane, half_width, 128))
    hub_plane = swap(hub_send, PLANE)

    slot_live = jnp.arange(slots, dtype=jnp.int32)[None, :] < tail_count[0][:, None]
    send_index = slot_rows(jnp.where(slot_live, tail_rows[0], -1))
    recv_index = slot_rows(tail_target[0])
    bias_terms = jnp.stack(three_terms(out_bias), axis=1)
    bias_terms = jnp.pad(bias_terms, ((0, 0), (0, 128 - bias_terms.shape[1])))
    feat_own, send_index, _ = lax.optimization_barrier((features, send_index, hub_send))
    own = own_block(feat_own, cotangent, w_self.T, w_neigh.T, bias_terms)
    across = shift(own, "core", 1)
    tail_send = gather_slots(send_index, features, parts, slots)
    hub_plane, tail_send, recv_index, own, across = lax.optimization_barrier(
        (hub_plane, tail_send, recv_index, own, across)
    )
    arrived = swap(tail_send, DOM)
    hub_all = [hub_plane] + [shift(hub_plane, "x", k) for k in range(1, x_size)]
    near = shift(own, "yl", 1)
    place = lax.axis_index(REP) ^ jnp.array([0, 2, 1, 3], jnp.int32)

    fold = partial(fold_hubs, *hub_at, tiles=tiles, sizes=sizes, blocks=blocks)
    hub_sum = fold(hub_all[:2], (0, 1), base=None)
    hub_sum, near = lax.optimization_barrier((hub_sum, near))
    own_blocks = [own, near, across, shift(near, "core", 1)]
    hub_sum = fold(hub_all[2:], (2, 3), base=hub_sum)
    mixed = mixed_sums(recv_index, arrived, hub_sum, degree)
    full_mixed = lax.all_gather(mixed, REP, axis=0, tiled=True)

    output, d_full, mixed_grad, tail_back, w_self_rows, bias_rows = layer(
        place, recv_index, degree, full_mixed, own_blocks, sizes, parts, slots
    )
    tail_len = slots // 2
    first = swap(tail_back.reshape(parts, tail_len + 8, 128), DOM)

    hub_terms = partial(
        hub_grad_terms, *hub_at, mixed_grad, bias_rows, tiles, sizes=sizes, blocks=blocks
    )
    far_steps = (2, 1, 3)
    terms = [shift(term, "x", k) for term, k in zip(hub_terms(far_steps), far_steps)]
    terms = list(hub_terms((0,))) + terms
    sums = jnp.sum(first[:, tail_len:].astype(F32), axis=0)
    second = swap(pack_rows(terms, sums), PLANE)

    base = tail_grads(send_index, first, w_self_rows, d_full, tail_len)
    grad_features, grad_w_self, grad_w_neigh, grad_bias = finish(second, base, full_width)
    return (output, grad_features, grad_w_self.T, grad_w_neigh.T, grad_bias[0])


def solution(mesh):
    grid = (4, 4, mesh.shape["dom"] // 16, 2, 2)
    parted = Mesh(mesh.devices.reshape(grid), DOM + REP)
    in_specs = (
        P(REP, DOM),
        P(DOM, None, None, None),
        P(DOM, None),
        P(DOM, None),
        P(DOM, None, None),
        P(DOM, None),
        P(DOM, None, None),
        P(DOM),
        P(None, REP),
        P(None, REP),
        P(REP),
        P(REP, DOM),
    )
    out_specs = (P(REP, DOM), P(REP, DOM), P(None, REP), P(None, REP), P(REP))
    return jax.shard_map(local, mesh=parted, in_specs=in_specs, out_specs=out_specs, check_vma=False)
```

```python
from functools import partial

import jax
import jax.numpy as jnp
from jax import lax
from jax.experimental import pallas as pl
from jax.experimental.pallas import tpu as pltpu
from jax.sharding import Mesh
from jax.sharding import PartitionSpec as P

BF = jnp.bfloat16
F32 = jnp.float32
BOTH_ROWS = (((0,), (0,)), ((), ()))
BOTH_COLS = (((1,), (1,)), ((), ()))
DOM = ("yh", "x", "z")
PLANE = ("yh", "z")
REP = ("yl", "core")
SMEM = pl.BlockSpec(memory_space=pltpu.SMEM)
VMEM = pl.BlockSpec(memory_space=pltpu.VMEM)
MIB = 1024 * 1024
VMEM_LIMIT = 16 * MIB


def mm(a, b, dims):
    return lax.dot_general(a, b, dims, preferred_element_type=F32)


def swap(pieces, axis):
    return lax.all_to_all(pieces, axis, split_axis=0, concat_axis=0, tiled=True)


def shift(values, axis, step):
    size = lax.axis_size(axis)
    return lax.ppermute(values, axis, [(i, (i + step) % size) for i in range(size)])


def call(kernel, out_shape, in_specs, scratch, name, flops, mib):
    outs = VMEM if isinstance(out_shape, jax.ShapeDtypeStruct) else [VMEM] * len(out_shape)
    return pl.pallas_call(
        kernel,
        out_shape=out_shape,
        in_specs=in_specs,
        out_specs=outs,
        scratch_shapes=scratch,
        compiler_params=pltpu.CompilerParams(vmem_limit_bytes=VMEM_LIMIT),
        cost_estimate=pl.CostEstimate(flops=flops, bytes_accessed=mib * MIB, transcendentals=0),
        name=name,
    )


def slot_rows(index):
    parts, slots = index.shape
    return index.reshape(parts, 2, slots // 2).transpose(1, 0, 2).reshape(2, -1)


def pick_slots(index_ref, source, step):
    width, nodes = source.shape
    low_size = 256
    high_size = nodes // low_size
    split = jnp.concatenate(
        [source[:, i * low_size : (i + 1) * low_size] for i in range(high_size)], axis=0
    )
    low_ids = lax.broadcasted_iota(jnp.int32, (low_size, step), 0)
    for start in range(0, index_ref.shape[1], step):
        halves = []
        for h in range(2):
            index = index_ref[h : h + 1, start : start + step]
            hits = jnp.where(low_ids == (index & (low_size - 1)), 1.0, 0.0).astype(BF)
            found = jnp.dot(split, hits, preferred_element_type=F32)
            high = jnp.broadcast_to(index >> 8, (width, step))
            kept = jnp.zeros((width, step), F32)
            for i in range(high_size):
                kept = jnp.where(high == i, found[i * width : (i + 1) * width], kept)
            halves.append(kept)
        yield start, jnp.concatenate(halves, axis=0).T


def forward_kernel(index_ref, source_ref, hub_ref, out_ref):
    rows, step = out_ref.shape[1] - hub_ref.shape[0], 256
    hub = jnp.broadcast_to(hub_ref[...].astype(F32)[None], (step // rows, *hub_ref.shape))
    for start, block in pick_slots(index_ref, source_ref[...], step):
        first = start // rows
        block = jnp.concatenate([block.reshape(-1, rows, 128), hub], axis=1)
        out_ref[first : first + step // rows] = block.astype(BF)


def forward_rows(index, source, hub, parts, slots):
    return call(
        forward_kernel,
        jax.ShapeDtypeStruct((parts, slots // 2 + hub.shape[0], 128), BF),
        [VMEM, VMEM, VMEM],
        [],
        "forward_rows",
        2 * parts * slots * 256 * 256,
        2,
    )(index, source, hub)


def layer_kernel(sizes, place_ref, index_ref, degree_ref, mixed_ref, *refs):
    block_refs, refs = refs[:4], refs[4:]
    outs, (bias_ref, *held), (feat, low_rows, sems) = refs[:5], refs[5:11], refs[11:]
    output_ref, d_ref, grad_ref, send_ref, self_ref = held
    x_size, z_size = sizes
    width, nodes = output_ref.shape
    full = mixed_ref.shape[0]
    half = full // 2
    copies = [pltpu.make_async_copy(h, o, sems.at[i]) for i, (h, o) in enumerate(zip(held, outs))]
    own = place_ref[0]
    rows_of = [pl.ds(pl.multiple_of(place_ref[i] * width, width), width) for i in range(4)]
    for at, ref in zip(rows_of, block_refs):
        feat[at, :] = ref[:, :nodes]
        low_rows[at, :] = ref[:, 2 * nodes : 2 * nodes + 2 * full].astype(F32)

    own_weights = []
    for first in (0, full):
        rows = low_rows[:, first : first + width]
        for k in range(1, 4):
            start = first + k * width
            rows = jnp.where(own == k, low_rows[:, start : start + width], rows)
        own_weights.append(rows.T.astype(BF))
    self_ref[...] = own_weights[0]
    copies[4].start()

    mixed, full_feat = mixed_ref[...], feat[...]
    for i, (at, ref) in enumerate(zip(rows_of, block_refs)):
        first = 2 * nodes
        bias = ref[:, first + 2 * full :].astype(F32)
        pre = jnp.dot(ref[:, first : first + full], full_feat, preferred_element_type=F32)
        pre = pre + jnp.dot(
            ref[:, first + full : first + 2 * full], mixed, preferred_element_type=F32
        )
        pre = pre + jnp.sum(bias, axis=1, keepdims=True)
        sigma = jax.nn.sigmoid(pre)
        slope = sigma * (1.0 + pre * (1.0 - sigma))
        d_part = (ref[:, nodes : 2 * nodes].astype(F32) * slope).astype(BF)
        d_ref[at, :] = d_part
        if i == 0:
            d_pre = d_part
            output_ref[...] = (pre * sigma).astype(BF)
            copies[0].start()
    copies[1].start()

    grad = jnp.dot(own_weights[1], d_ref[...], preferred_element_type=F32).astype(BF)
    grad_ref[...] = grad
    copies[2].start()
    scaled = (grad.astype(F32) / degree_ref[...].astype(F32)).astype(BF)

    made = []
    for source in (full_feat, mixed):
        total = mm(source, d_pre, BOTH_COLS)
        total = jnp.concatenate([total[:half], total[half:]], axis=1)
        made.append(total.reshape(-1, z_size // 2, 16, 128))
    made = jnp.concatenate(made, axis=0)
    bias = mm(jnp.ones((bias_ref.shape[0], nodes), BF), d_pre, BOTH_COLS)
    bias = jnp.concatenate([bias, bias], axis=1)
    high = bias.astype(BF).astype(F32)
    row = lax.broadcasted_iota(jnp.int32, bias.shape, 0)
    bias_ref[...] = jnp.where(row == 0, high, jnp.where(row == 1, bias - high, 0.0)).astype(BF)

    rows = (send_ref.shape[1] - 16) // 2
    step = 256
    for start, block in pick_slots(index_ref, scaled, step):
        block = block.reshape(-1, 2, rows, 128)
        count = block.shape[0]
        first = start // (2 * rows)
        weight = made[first // (x_size * z_size // 2)]
        weight = jnp.concatenate([weight] * (count // weight.shape[0]), axis=0)
        block = jnp.concatenate([block[:, 0], weight[:, :8], block[:, 1], weight[:, 8:]], axis=1)
        send_ref[first : first + count] = block.astype(BF)
    copies[3].start()
    for copy in copies:
        copy.wait()


def layer(place, index, degree, mixed, own_blocks, sizes, parts, slots):
    full, nodes = mixed.shape
    width = own_blocks[0].shape[0]
    held = [
        (width, nodes),
        (full, nodes),
        (width, nodes),
        (parts // 2, slots + 16, 128),
        (width, full),
    ]
    bias_shape = (width // 2, 128)
    return pl.pallas_call(
        partial(layer_kernel, sizes),
        out_shape=[jax.ShapeDtypeStruct(shape, BF) for shape in [*held, bias_shape]],
        in_specs=[SMEM] + [VMEM] * 7,
        out_specs=[pl.BlockSpec(memory_space=pltpu.HBM)] * len(held) + [VMEM],
        scratch_shapes=[pltpu.VMEM(shape, BF) for shape in held]
        + [
            pltpu.VMEM((full, nodes), BF),
            pltpu.VMEM((full, 2 * full), F32),
            pltpu.SemaphoreType.DMA((len(held),)),
        ],
        compiler_params=pltpu.CompilerParams(vmem_limit_bytes=60 * MIB),
        cost_estimate=pl.CostEstimate(flops=1000 * MIB, bytes_accessed=4 * MIB, transcendentals=0),
        name="layer",
    )(place, index, degree, mixed, *own_blocks)


def sum_slots(index_ref, arrived_ref, rows, start, size):
    parts = arrived_ref.shape[0]
    flat = arrived_ref[:, :rows, :].reshape(parts * rows, 128)
    ids = lax.broadcasted_iota(jnp.int32, (size, parts * rows), 0) + start
    sums = []
    for h in range(2):
        hits = jnp.where(ids == index_ref[h : h + 1, :], 1.0, 0.0).astype(BF)
        sums.append(jnp.dot(hits, flat, preferred_element_type=F32))
    return sums[0].T[:64] + sums[1].T[64:]


def mixed_kernel(
    rows, block_ref, mask_ref, index_ref, arrived_ref, degree_ref, tile_ref, out_ref, total
):
    blocks = total.shape[0] - 1
    half = arrived_ref.shape[1] - rows
    lanes = lax.broadcasted_iota(jnp.int32, (half, 128), 1)
    first = (lanes < 64).astype(F32).astype(BF)
    second = (lanes >= 64).astype(F32).astype(BF)
    total[...] = jnp.zeros_like(total)
    group = 8

    @pl.loop(0, arrived_ref.shape[0] // group)
    def _(g):
        for i in range(group):
            tile = g * group + i
            hub = arrived_ref[tile, rows:, :]
            weights = tile_ref[tile]
            product = jnp.dot(
                jnp.concatenate([hub * first, hub * second], axis=0),
                jnp.concatenate([weights, weights], axis=0),
                preferred_element_type=F32,
            )
            dest = jnp.where(mask_ref[tile] > 0, block_ref[tile], blocks)
            total[dest] = total[dest] + product

    size = 256
    for start in range(0, out_ref.shape[1], size):
        at = slice(start, start + size)
        tail = sum_slots(index_ref, arrived_ref, rows, start, size)
        hub = jnp.concatenate([total[start // 128], total[start // 128 + 1]], axis=1)
        out_ref[:, at] = (hub + tail / degree_ref[:, at].astype(F32)).astype(BF)


def mixed_sums(block, mask, index, arrived, degree, tiles, rows, width):
    parts = arrived.shape[0]
    nodes = degree.shape[1]
    return call(
        partial(mixed_kernel, rows),
        jax.ShapeDtypeStruct((width, nodes), BF),
        [SMEM, SMEM] + [VMEM] * 4,
        [pltpu.VMEM((nodes // 128 + 1, width, 128), F32)],
        "mixed",
        4 * parts * rows * nodes * 128,
        2,
    )(block, mask, index, arrived, degree, tiles)


def tail_grad_kernel(rows, index_ref, arrived_ref, weight_ref, d_ref, out_ref):
    size = 256
    for start in range(0, out_ref.shape[1], size):
        at = slice(start, start + size)
        tail = sum_slots(index_ref, arrived_ref, rows, start, size)
        direct = jnp.dot(weight_ref[...], d_ref[:, at], preferred_element_type=F32)
        out_ref[:, at] = direct + tail


def tail_grads(index, arrived, weight, d_full, rows):
    parts = arrived.shape[0]
    width, nodes = weight.shape[0], d_full.shape[1]
    return call(
        partial(tail_grad_kernel, rows),
        jax.ShapeDtypeStruct((width, nodes), F32),
        [VMEM] * 4,
        [],
        "tail_grads",
        4 * parts * rows * nodes * 128,
        2,
    )(index, arrived, weight, d_full)


def own_kernel(feat_ref, cot_ref, self_ref, neigh_ref, bias_ref, out_ref):
    first = 0
    for ref in (feat_ref, cot_ref, self_ref, neigh_ref, bias_ref):
        out_ref[:, first : first + ref.shape[1]] = ref[...].astype(BF)
        first += ref.shape[1]


def own_block(*pieces):
    columns = sum(piece.shape[1] for piece in pieces)
    return call(
        own_kernel,
        jax.ShapeDtypeStruct((pieces[0].shape[0], columns), BF),
        [VMEM] * len(pieces),
        [],
        "own_block",
        0,
        0,
    )(*pieces)


def three_terms(values):
    high = lax.reduce_precision(values, 8, 7)
    rest = values - high
    middle = lax.reduce_precision(rest, 8, 7)
    return [high.astype(BF), middle.astype(BF), (rest - middle).astype(BF)]


def tile_index(x_ref, k, sizes, yh, z, sign):
    x_size, z_size = sizes
    x = lax.rem(x_ref[0] + (sign * k) % x_size, x_size)
    return (yh * x_size + x) * z_size + z


def hub_grad_kernel(steps, sizes, x_ref, block_ref, mask_ref, grad_ref, bias_ref, tile_ref, *refs):
    *out_refs, blocked = refs
    blocks = blocked.shape[0] - 1
    for b in range(blocks):
        blocked[b] = grad_ref[:, b * 128 : (b + 1) * 128]
    blocked[blocks] = jnp.zeros_like(blocked[blocks])
    count, half, _ = out_refs[0].shape
    first = lax.broadcasted_iota(jnp.int32, (half, 128), 1) < 64
    z_size = sizes[1]
    for k, out_ref in zip(steps, out_refs):
        out_ref[count - 1] = bias_ref[...]

        @pl.loop(0, count // z_size)
        def _(yh):
            for z in range(z_size):
                tile = tile_index(x_ref, k, sizes, yh, z, 1)
                weights = tile_ref[tile]
                dest = jnp.where(mask_ref[tile] > 0, block_ref[tile], blocks)
                product = mm(
                    blocked[dest],
                    jnp.concatenate([weights, weights], axis=0),
                    BOTH_COLS,
                )
                out_ref[yh * z_size + z] = jnp.where(
                    first, product[:half], product[half:]
                ).astype(BF)


def hub_grad_terms(x_index, block, mask, grad, bias, tiles, steps, sizes, blocks):
    width = grad.shape[0]
    shape = (tiles.shape[0] // sizes[0] + 1, width // 2, 128)
    return call(
        partial(hub_grad_kernel, steps, sizes),
        [jax.ShapeDtypeStruct(shape, BF) for _ in steps],
        [SMEM, SMEM, SMEM, VMEM, VMEM, VMEM],
        [pltpu.VMEM((blocks + 1, width, 128), BF)],
        "hub_grad_terms",
        tiles.size * width * len(steps),
        4,
    )(x_index, block, mask, grad, bias, tiles)


def pack_kernel(*refs):
    *term_refs, sum_ref, out_ref = refs
    count, half = out_ref.shape[0], term_refs[0].shape[1]
    total = term_refs[0][...].astype(F32)
    for ref in term_refs[1:]:
        total = total + ref[...].astype(F32)
    out_ref[:, :half] = total[:count].astype(BF)
    bias = total[count]
    bias = jnp.broadcast_to(bias[0:1] + bias[1:2], (8, 128))
    high = bias.astype(BF).astype(F32)
    row = lax.broadcasted_iota(jnp.int32, (8, 128), 0)
    bias = jnp.where(row == 0, high, jnp.where(row == 1, bias - high, 0.0))
    extra = jnp.concatenate([sum_ref[...], bias], axis=0).astype(BF)
    out_ref[:, half:] = jnp.broadcast_to(extra[None], (count, 16, 128))


def pack_rows(terms, sums):
    count, half, _ = terms[0].shape
    return call(
        pack_kernel,
        jax.ShapeDtypeStruct((count - 1, half + 16, 128), BF),
        [VMEM] * (len(terms) + 1),
        [],
        "hub_grads_over_x",
        MIB,
        2,
    )(*terms, sums)


def final_kernel(second_ref, base_ref, out_ref, self_ref, neigh_ref, bias_ref):
    half = out_ref.shape[0] // 2
    hub = jnp.sum(second_ref[:, :half].astype(F32), axis=0)
    hub = jnp.concatenate([hub, pltpu.roll(hub, 64, 1)], axis=0)
    lane = lax.broadcasted_iota(jnp.int32, hub.shape, 1)
    out_ref[...] = base_ref[...] + jnp.where(lane < 64, hub, 0.0)
    extra = second_ref[:, half:].astype(F32)
    grads = extra[:, :8].reshape(-1, 128)
    rows = grads.shape[0] // 2
    for place, ref in enumerate((self_ref, neigh_ref)):
        turned = grads[place * rows : (place + 1) * rows].T
        ref[...] = jnp.concatenate([turned[:64], turned[64:]], axis=1)
    bias = jnp.sum(extra[:, 8:], axis=0)
    bias_ref[...] = (bias[0:1] + bias[1:2])[:, : bias_ref.shape[1]]


def finish(second, base, full):
    width, nodes = base.shape
    hub_part = pl.BlockSpec((width, 128), lambda i: (0, 0))
    return pl.pallas_call(
        final_kernel,
        out_shape=[
            jax.ShapeDtypeStruct((width, nodes), F32),
            jax.ShapeDtypeStruct((width, full), F32),
            jax.ShapeDtypeStruct((width, full), F32),
            jax.ShapeDtypeStruct((1, width), F32),
        ],
        grid=(1,),
        in_specs=[pl.BlockSpec(second.shape, lambda i: (0, 0, 0)), hub_part],
        out_specs=[hub_part]
        + [pl.BlockSpec((width, full), lambda i: (0, 0))] * 2
        + [pl.BlockSpec((1, width), lambda i: (0, 0))],
        input_output_aliases={1: 0},
        compiler_params=pltpu.CompilerParams(vmem_limit_bytes=VMEM_LIMIT),
        cost_estimate=pl.CostEstimate(flops=MIB, bytes_accessed=MIB, transcendentals=0),
        name="gradients",
    )(second, base)


def local(
    features,
    hub_weight,
    hub_block,
    hub_mask,
    tail_rows,
    tail_count,
    tail_target,
    degree,
    w_self,
    w_neigh,
    out_bias,
    cotangent,
):
    width, nodes = features.shape
    parts, hubs, tile_len = hub_weight.shape[1:]
    slots = tail_rows.shape[2]
    half_width = width // 2
    blocks = nodes // tile_len
    full_width = w_self.shape[0]
    x_size, z_size = lax.axis_size("x"), lax.axis_size("z")
    sizes = (x_size, z_size)
    plane = parts // x_size
    x_index = lax.axis_index("x")[None]
    tiles = hub_weight[0]
    hub_at = (x_index, hub_block[0], hub_mask[0])
    degree = degree[None, :]

    hub_piece = jnp.concatenate([features[:half_width, :hubs], features[half_width:, :hubs]], axis=1)
    slot_live = jnp.arange(slots, dtype=jnp.int32)[None, :] < tail_count[0][:, None]
    send_index = slot_rows(jnp.where(slot_live, tail_rows[0], -1))
    send = forward_rows(send_index, features, hub_piece, parts, slots)
    arrived = swap(send, DOM)

    feat_own, targets, _ = lax.optimization_barrier((features, tail_target[0], send))
    recv_index = slot_rows(targets)
    bias_terms = jnp.stack(three_terms(out_bias), axis=1)
    bias_terms = jnp.pad(bias_terms, ((0, 0), (0, 128 - bias_terms.shape[1])))
    own = own_block(feat_own, cotangent, w_self.T, w_neigh.T, bias_terms)
    near = shift(own, "yl", 1)
    own_blocks = [own, near, shift(own, "core", 1), shift(near, "core", 1)]
    place = lax.axis_index(REP) ^ jnp.array([0, 2, 1, 3], jnp.int32)

    mixed = mixed_sums(*hub_at[1:], recv_index, arrived, degree, tiles, slots // 2, width)
    full_mixed = lax.all_gather(mixed, REP, axis=0, tiled=True)

    output, d_full, mixed_grad, tail_back, w_self_rows, bias_rows = layer(
        place, recv_index, degree, full_mixed, own_blocks, sizes, parts, slots
    )
    tail_len = slots // 2
    first = swap(tail_back.reshape(parts, tail_len + 8, 128), DOM)

    hub_terms = partial(
        hub_grad_terms, *hub_at, mixed_grad, bias_rows, tiles, sizes=sizes, blocks=blocks
    )
    far_steps = (2, 1, 3)
    terms = [shift(term, "x", k) for term, k in zip(hub_terms(far_steps), far_steps)]
    terms = list(hub_terms((0,))) + terms
    sums = jnp.sum(first[:, tail_len:].astype(F32), axis=0)
    second = swap(pack_rows(terms, sums), PLANE)

    base = tail_grads(send_index, first, w_self_rows, d_full, tail_len)
    grad_features, grad_w_self, grad_w_neigh, grad_bias = finish(second, base, full_width)
    return (output, grad_features, grad_w_self.T, grad_w_neigh.T, grad_bias[0])


def solution(mesh):
    grid = (4, 4, mesh.shape["dom"] // 16, 2, 2)
    parted = Mesh(mesh.devices.reshape(grid), DOM + REP)
    in_specs = (
        P(REP, DOM),
        P(DOM, None, None, None),
        P(DOM, None),
        P(DOM, None),
        P(DOM, None, None),
        P(DOM, None),
        P(DOM, None, None),
        P(DOM),
        P(None, REP),
        P(None, REP),
        P(REP),
        P(REP, DOM),
    )
    out_specs = (P(REP, DOM), P(REP, DOM), P(None, REP), P(None, REP), P(REP))
    return jax.shard_map(local, mesh=parted, in_specs=in_specs, out_specs=out_specs, check_vma=False)
```

```python
from functools import partial

import jax
import jax.numpy as jnp
from jax import lax
from jax.experimental import pallas as pl
from jax.experimental.pallas import tpu as pltpu
from jax.sharding import Mesh
from jax.sharding import PartitionSpec as P

BF = jnp.bfloat16
F32 = jnp.float32
BOTH_ROWS = (((0,), (0,)), ((), ()))
BOTH_COLS = (((1,), (1,)), ((), ()))
DOM = ("yh", "x", "z")
PLANE = ("yh", "z")
REP = ("yl", "core")
SMEM = pl.BlockSpec(memory_space=pltpu.SMEM)
VMEM = pl.BlockSpec(memory_space=pltpu.VMEM)
MIB = 1024 * 1024
VMEM_LIMIT = 16 * MIB


def mm(a, b, dims):
    return lax.dot_general(a, b, dims, preferred_element_type=F32)


def swap(pieces, axis):
    return lax.all_to_all(pieces, axis, split_axis=0, concat_axis=0, tiled=True)


def shift(values, axis, step):
    size = lax.axis_size(axis)
    return lax.ppermute(values, axis, [(i, (i + step) % size) for i in range(size)])


def call(kernel, out_shape, in_specs, scratch, name, flops, mib):
    outs = VMEM if isinstance(out_shape, jax.ShapeDtypeStruct) else [VMEM] * len(out_shape)
    return pl.pallas_call(
        kernel,
        out_shape=out_shape,
        in_specs=in_specs,
        out_specs=outs,
        scratch_shapes=scratch,
        compiler_params=pltpu.CompilerParams(vmem_limit_bytes=VMEM_LIMIT),
        cost_estimate=pl.CostEstimate(flops=flops, bytes_accessed=mib * MIB, transcendentals=0),
        name=name,
    )


def slot_rows(index):
    parts, slots = index.shape
    return index.reshape(parts, 2, slots // 2).transpose(1, 0, 2).reshape(2, -1)


def pick_slots(index_ref, source, step):
    width, nodes = source.shape
    low_size = 256
    high_size = nodes // low_size
    split = jnp.concatenate(
        [source[:, i * low_size : (i + 1) * low_size] for i in range(high_size)], axis=0
    )
    low_ids = lax.broadcasted_iota(jnp.int32, (low_size, step), 0)
    for start in range(0, index_ref.shape[1], step):
        halves = []
        for h in range(2):
            index = index_ref[h : h + 1, start : start + step]
            hits = jnp.where(low_ids == (index & (low_size - 1)), 1.0, 0.0).astype(BF)
            found = jnp.dot(split, hits, preferred_element_type=F32)
            high = jnp.broadcast_to(index >> 8, (width, step))
            kept = jnp.zeros((width, step), F32)
            for i in range(high_size):
                kept = jnp.where(high == i, found[i * width : (i + 1) * width], kept)
            halves.append(kept)
        yield start, jnp.concatenate(halves, axis=0).T


def gather_kernel(index_ref, source_ref, out_ref):
    rows, step = out_ref.shape[1], 256
    for start, block in pick_slots(index_ref, source_ref[...], step):
        first = start // rows
        out_ref[first : first + step // rows] = block.reshape(-1, rows, 128).astype(BF)


def gather_slots(index, source, parts, slots):
    return call(
        gather_kernel,
        jax.ShapeDtypeStruct((parts, slots // 2, 128), BF),
        [VMEM, VMEM],
        [],
        "tail_rows_out",
        2 * parts * slots * 256 * 256,
        2,
    )(index, source)


def layer_kernel(sizes, place_ref, index_ref, degree_ref, mixed_ref, *refs):
    block_refs, refs = refs[:4], refs[4:]
    outs, (bias_ref, *held), (feat, low_rows, sems) = refs[:5], refs[5:11], refs[11:]
    output_ref, d_ref, grad_ref, send_ref, self_ref = held
    x_size, z_size = sizes
    width, nodes = output_ref.shape
    full = mixed_ref.shape[0]
    half = full // 2
    copies = [pltpu.make_async_copy(h, o, sems.at[i]) for i, (h, o) in enumerate(zip(held, outs))]
    own = place_ref[0]
    rows_of = [pl.ds(pl.multiple_of(place_ref[i] * width, width), width) for i in range(4)]
    for at, ref in zip(rows_of, block_refs):
        feat[at, :] = ref[:, :nodes]
        low_rows[at, :] = ref[:, 2 * nodes : 2 * nodes + 2 * full].astype(F32)

    own_weights = []
    for first in (0, full):
        rows = low_rows[:, first : first + width]
        for k in range(1, 4):
            start = first + k * width
            rows = jnp.where(own == k, low_rows[:, start : start + width], rows)
        own_weights.append(rows.T.astype(BF))
    self_ref[...] = own_weights[0]
    copies[4].start()

    mixed, full_feat = mixed_ref[...], feat[...]
    for i, (at, ref) in enumerate(zip(rows_of, block_refs)):
        first = 2 * nodes
        bias = ref[:, first + 2 * full :].astype(F32)
        pre = jnp.dot(ref[:, first : first + full], full_feat, preferred_element_type=F32)
        pre = pre + jnp.dot(
            ref[:, first + full : first + 2 * full], mixed, preferred_element_type=F32
        )
        pre = pre + jnp.sum(bias, axis=1, keepdims=True)
        sigma = jax.nn.sigmoid(pre)
        slope = sigma * (1.0 + pre * (1.0 - sigma))
        d_part = (ref[:, nodes : 2 * nodes].astype(F32) * slope).astype(BF)
        d_ref[at, :] = d_part
        if i == 0:
            d_pre = d_part
            output_ref[...] = (pre * sigma).astype(BF)
            copies[0].start()
    copies[1].start()

    grad = jnp.dot(own_weights[1], d_ref[...], preferred_element_type=F32).astype(BF)
    grad_ref[...] = grad
    copies[2].start()
    scaled = (grad.astype(F32) / degree_ref[...].astype(F32)).astype(BF)

    made = []
    for source in (full_feat, mixed):
        total = mm(source, d_pre, BOTH_COLS)
        total = jnp.concatenate([total[:half], total[half:]], axis=1)
        made.append(total.reshape(-1, z_size // 2, 16, 128))
    made = jnp.concatenate(made, axis=0)
    bias = mm(jnp.ones((bias_ref.shape[0], nodes), BF), d_pre, BOTH_COLS)
    bias = jnp.concatenate([bias, bias], axis=1)
    high = bias.astype(BF).astype(F32)
    row = lax.broadcasted_iota(jnp.int32, bias.shape, 0)
    bias_ref[...] = jnp.where(row == 0, high, jnp.where(row == 1, bias - high, 0.0)).astype(BF)

    rows = (send_ref.shape[1] - 16) // 2
    step = 256
    for start, block in pick_slots(index_ref, scaled, step):
        block = block.reshape(-1, 2, rows, 128)
        count = block.shape[0]
        first = start // (2 * rows)
        weight = made[first // (x_size * z_size // 2)]
        weight = jnp.concatenate([weight] * (count // weight.shape[0]), axis=0)
        block = jnp.concatenate([block[:, 0], weight[:, :8], block[:, 1], weight[:, 8:]], axis=1)
        send_ref[first : first + count] = block.astype(BF)
    copies[3].start()
    for copy in copies:
        copy.wait()


def layer(place, index, degree, mixed, own_blocks, sizes, parts, slots):
    full, nodes = mixed.shape
    width = own_blocks[0].shape[0]
    held = [
        (width, nodes),
        (full, nodes),
        (width, nodes),
        (parts // 2, slots + 16, 128),
        (width, full),
    ]
    bias_shape = (width // 2, 128)
    return pl.pallas_call(
        partial(layer_kernel, sizes),
        out_shape=[jax.ShapeDtypeStruct(shape, BF) for shape in [*held, bias_shape]],
        in_specs=[SMEM] + [VMEM] * 7,
        out_specs=[pl.BlockSpec(memory_space=pltpu.HBM)] * len(held) + [VMEM],
        scratch_shapes=[pltpu.VMEM(shape, BF) for shape in held]
        + [
            pltpu.VMEM((full, nodes), BF),
            pltpu.VMEM((full, 2 * full), F32),
            pltpu.SemaphoreType.DMA((len(held),)),
        ],
        compiler_params=pltpu.CompilerParams(vmem_limit_bytes=60 * MIB),
        cost_estimate=pl.CostEstimate(flops=1000 * MIB, bytes_accessed=4 * MIB, transcendentals=0),
        name="layer",
    )(place, index, degree, mixed, *own_blocks)


def sum_slots(index_ref, arrived_ref, rows, start, size):
    parts = arrived_ref.shape[0]
    flat = arrived_ref[:, :rows, :].reshape(parts * rows, 128)
    ids = lax.broadcasted_iota(jnp.int32, (size, parts * rows), 0) + start
    sums = []
    for h in range(2):
        hits = jnp.where(ids == index_ref[h : h + 1, :], 1.0, 0.0).astype(BF)
        sums.append(jnp.dot(hits, flat, preferred_element_type=F32))
    return sums[0].T[:64] + sums[1].T[64:]


def mixed_kernel(rows, index_ref, arrived_ref, hub_ref, degree_ref, out_ref):
    size = 256
    for start in range(0, out_ref.shape[1], size):
        at = slice(start, start + size)
        tail = sum_slots(index_ref, arrived_ref, rows, start, size)
        out_ref[:, at] = (hub_ref[:, at] + tail / degree_ref[:, at].astype(F32)).astype(BF)


def mixed_sums(index, arrived, hub_sum, degree):
    parts, rows, _ = arrived.shape
    width, nodes = hub_sum.shape
    return call(
        partial(mixed_kernel, rows),
        jax.ShapeDtypeStruct((width, nodes), BF),
        [VMEM] * 4,
        [],
        "mixed",
        4 * parts * rows * nodes * 128,
        2,
    )(index, arrived, hub_sum, degree)


def tail_grad_kernel(rows, index_ref, arrived_ref, weight_ref, d_ref, out_ref):
    size = 256
    for start in range(0, out_ref.shape[1], size):
        at = slice(start, start + size)
        tail = sum_slots(index_ref, arrived_ref, rows, start, size)
        direct = jnp.dot(weight_ref[...], d_ref[:, at], preferred_element_type=F32)
        out_ref[:, at] = direct + tail


def tail_grads(index, arrived, weight, d_full, rows):
    parts = arrived.shape[0]
    width, nodes = weight.shape[0], d_full.shape[1]
    return call(
        partial(tail_grad_kernel, rows),
        jax.ShapeDtypeStruct((width, nodes), F32),
        [VMEM] * 4,
        [],
        "tail_grads",
        4 * parts * rows * nodes * 128,
        2,
    )(index, arrived, weight, d_full)


def own_kernel(feat_ref, cot_ref, self_ref, neigh_ref, bias_ref, out_ref):
    first = 0
    for ref in (feat_ref, cot_ref, self_ref, neigh_ref, bias_ref):
        out_ref[:, first : first + ref.shape[1]] = ref[...].astype(BF)
        first += ref.shape[1]


def own_block(*pieces):
    columns = sum(piece.shape[1] for piece in pieces)
    return call(
        own_kernel,
        jax.ShapeDtypeStruct((pieces[0].shape[0], columns), BF),
        [VMEM] * len(pieces),
        [],
        "own_block",
        0,
        0,
    )(*pieces)


def three_terms(values):
    high = lax.reduce_precision(values, 8, 7)
    rest = values - high
    middle = lax.reduce_precision(rest, 8, 7)
    return [high.astype(BF), middle.astype(BF), (rest - middle).astype(BF)]


def tile_index(x_ref, k, sizes, yh, z, sign):
    x_size, z_size = sizes
    x = lax.rem(x_ref[0] + (sign * k) % x_size, x_size)
    return (yh * x_size + x) * z_size + z


def fold_kernel(steps, sizes, has_base, x_ref, block_ref, mask_ref, *refs):
    hub_refs, (tile_ref, *base_ref, out_ref, total) = refs[: len(steps)], refs[len(steps) :]
    blocks = total.shape[0] - 1
    half = hub_refs[0].shape[1]
    lanes = lax.broadcasted_iota(jnp.int32, (half, 128), 1)
    first = (lanes < 64).astype(F32).astype(BF)
    second = (lanes >= 64).astype(F32).astype(BF)
    for b in range(blocks):
        at = slice(b * 128, (b + 1) * 128)
        total[b] = base_ref[0][:, at] if has_base else jnp.zeros_like(total[b])
    total[blocks] = jnp.zeros_like(total[blocks])
    z_size = sizes[1]
    for k, hub_ref in zip(steps, hub_refs):

        @pl.loop(0, hub_ref.shape[0] // z_size)
        def _(yh):
            for z in range(z_size):
                tile = tile_index(x_ref, k, sizes, yh, z, -1)
                rows = hub_ref[yh * z_size + z]
                weights = tile_ref[tile]
                product = jnp.dot(
                    jnp.concatenate([rows * first, rows * second], axis=0),
                    jnp.concatenate([weights, weights], axis=0),
                    preferred_element_type=F32,
                )
                dest = jnp.where(mask_ref[tile] > 0, block_ref[tile], blocks)
                total[dest] = total[dest] + product

    for b in range(blocks):
        out_ref[:, b * 128 : (b + 1) * 128] = total[b]


def fold_hubs(x_index, block, mask, hubs, steps, tiles, sizes, blocks, base):
    width = 2 * hubs[0].shape[1]
    bases = [] if base is None else [base]
    return call(
        partial(fold_kernel, steps, sizes, base is not None),
        jax.ShapeDtypeStruct((width, blocks * 128), F32),
        [SMEM, SMEM, SMEM] + [VMEM] * (len(hubs) + 1 + len(bases)),
        [pltpu.VMEM((blocks + 1, width, 128), F32)],
        "hub_sums",
        tiles.size * width * len(hubs),
        4,
    )(x_index, block, mask, *hubs, tiles, *bases)


def hub_grad_kernel(steps, sizes, x_ref, block_ref, mask_ref, grad_ref, bias_ref, tile_ref, *refs):
    *out_refs, blocked = refs
    blocks = blocked.shape[0] - 1
    for b in range(blocks):
        blocked[b] = grad_ref[:, b * 128 : (b + 1) * 128]
    blocked[blocks] = jnp.zeros_like(blocked[blocks])
    count, half, _ = out_refs[0].shape
    first = lax.broadcasted_iota(jnp.int32, (half, 128), 1) < 64
    z_size = sizes[1]
    for k, out_ref in zip(steps, out_refs):
        out_ref[count - 1] = bias_ref[...]

        @pl.loop(0, count // z_size)
        def _(yh):
            for z in range(0, z_size, 2):
                tile = tile_index(x_ref, k, sizes, yh, z, 1)
                dests = [
                    jnp.where(mask_ref[tile + i] > 0, block_ref[tile + i], blocks) for i in range(2)
                ]
                product = mm(
                    jnp.concatenate([blocked[dest] for dest in dests], axis=0),
                    jnp.concatenate([tile_ref[tile], tile_ref[tile + 1]], axis=0),
                    BOTH_COLS,
                )
                turned = pltpu.roll(product[half : 3 * half], 64, 1)
                place = yh * z_size + z
                out_ref[place] = jnp.where(first, product[:half], turned[:half]).astype(BF)
                out_ref[place + 1] = jnp.where(first, turned[half:], product[3 * half :]).astype(BF)


def hub_grad_terms(x_index, block, mask, grad, bias, tiles, steps, sizes, blocks):
    width = grad.shape[0]
    shape = (tiles.shape[0] // sizes[0] + 1, width // 2, 128)
    return call(
        partial(hub_grad_kernel, steps, sizes),
        [jax.ShapeDtypeStruct(shape, BF) for _ in steps],
        [SMEM, SMEM, SMEM, VMEM, VMEM, VMEM],
        [pltpu.VMEM((blocks + 1, width, 128), BF)],
        "hub_grad_terms",
        tiles.size * width * len(steps),
        4,
    )(x_index, block, mask, grad, bias, tiles)


def pack_kernel(*refs):
    *term_refs, sum_ref, out_ref = refs
    count, half = out_ref.shape[0], term_refs[0].shape[1]
    total = term_refs[0][...].astype(F32)
    for ref in term_refs[1:]:
        total = total + ref[...].astype(F32)
    out_ref[:, :half] = total[:count].astype(BF)
    bias = total[count]
    bias = jnp.broadcast_to(bias[0:1] + bias[1:2], (8, 128))
    high = bias.astype(BF).astype(F32)
    row = lax.broadcasted_iota(jnp.int32, (8, 128), 0)
    bias = jnp.where(row == 0, high, jnp.where(row == 1, bias - high, 0.0))
    extra = jnp.concatenate([sum_ref[...], bias], axis=0).astype(BF)
    out_ref[:, half:] = jnp.broadcast_to(extra[None], (count, 16, 128))


def pack_rows(terms, sums):
    count, half, _ = terms[0].shape
    return call(
        pack_kernel,
        jax.ShapeDtypeStruct((count - 1, half + 16, 128), BF),
        [VMEM] * (len(terms) + 1),
        [],
        "hub_grads_over_x",
        MIB,
        2,
    )(*terms, sums)


def final_kernel(second_ref, base_ref, out_ref, self_ref, neigh_ref, bias_ref):
    half = out_ref.shape[0] // 2
    hub = jnp.sum(second_ref[:, :half].astype(F32), axis=0)
    hub = jnp.concatenate([hub, pltpu.roll(hub, 64, 1)], axis=0)
    lane = lax.broadcasted_iota(jnp.int32, hub.shape, 1)
    out_ref[...] = base_ref[...] + jnp.where(lane < 64, hub, 0.0)
    extra = second_ref[:, half:].astype(F32)
    grads = extra[:, :8].reshape(-1, 128)
    rows = grads.shape[0] // 2
    for place, ref in enumerate((self_ref, neigh_ref)):
        turned = grads[place * rows : (place + 1) * rows].T
        ref[...] = jnp.concatenate([turned[:64], turned[64:]], axis=1)
    bias = jnp.sum(extra[:, 8:], axis=0)
    bias_ref[...] = (bias[0:1] + bias[1:2])[:, : bias_ref.shape[1]]


def finish(second, base, full):
    width, nodes = base.shape
    hub_part = pl.BlockSpec((width, 128), lambda i: (0, 0))
    return pl.pallas_call(
        final_kernel,
        out_shape=[
            jax.ShapeDtypeStruct((width, nodes), F32),
            jax.ShapeDtypeStruct((width, full), F32),
            jax.ShapeDtypeStruct((width, full), F32),
            jax.ShapeDtypeStruct((1, width), F32),
        ],
        grid=(1,),
        in_specs=[pl.BlockSpec(second.shape, lambda i: (0, 0, 0)), hub_part],
        out_specs=[hub_part]
        + [pl.BlockSpec((width, full), lambda i: (0, 0))] * 2
        + [pl.BlockSpec((1, width), lambda i: (0, 0))],
        input_output_aliases={1: 0},
        compiler_params=pltpu.CompilerParams(vmem_limit_bytes=VMEM_LIMIT),
        cost_estimate=pl.CostEstimate(flops=MIB, bytes_accessed=MIB, transcendentals=0),
        name="gradients",
    )(second, base)


def local(
    features,
    hub_weight,
    hub_block,
    hub_mask,
    tail_rows,
    tail_count,
    tail_target,
    degree,
    w_self,
    w_neigh,
    out_bias,
    cotangent,
):
    width, nodes = features.shape
    parts, hubs, tile_len = hub_weight.shape[1:]
    slots = tail_rows.shape[2]
    half_width = width // 2
    blocks = nodes // tile_len
    full_width = w_self.shape[0]
    x_size, z_size = lax.axis_size("x"), lax.axis_size("z")
    sizes = (x_size, z_size)
    plane = parts // x_size
    x_index = lax.axis_index("x")[None]
    tiles = hub_weight[0]
    hub_at = (x_index, hub_block[0], hub_mask[0])
    degree = degree[None, :]

    hub_piece = jnp.concatenate([features[:half_width, :hubs], features[half_width:, :hubs]], axis=1)
    hub_send = jnp.broadcast_to(hub_piece[None], (plane, half_width, 128))
    hub_plane = swap(hub_send, PLANE)

    slot_live = jnp.arange(slots, dtype=jnp.int32)[None, :] < tail_count[0][:, None]
    send_index = slot_rows(jnp.where(slot_live, tail_rows[0], -1))
    recv_index = slot_rows(tail_target[0])
    bias_terms = jnp.stack(three_terms(out_bias), axis=1)
    bias_terms = jnp.pad(bias_terms, ((0, 0), (0, 128 - bias_terms.shape[1])))
    feat_own, send_index, _ = lax.optimization_barrier((features, send_index, hub_send))
    own = own_block(feat_own, cotangent, w_self.T, w_neigh.T, bias_terms)
    across = shift(own, "core", 1)
    tail_send = gather_slots(send_index, features, parts, slots)
    hub_plane, tail_send, recv_index, own, across = lax.optimization_barrier(
        (hub_plane, tail_send, recv_index, own, across)
    )
    arrived = swap(tail_send, DOM)
    hub_all = [hub_plane] + [shift(hub_plane, "x", k) for k in range(1, x_size)]
    near = shift(own, "yl", 1)
    own_blocks = [own, near, across, shift(near, "core", 1)]
    place = lax.axis_index(REP) ^ jnp.array([0, 2, 1, 3], jnp.int32)

    fold = partial(fold_hubs, *hub_at, tiles=tiles, sizes=sizes, blocks=blocks)
    hub_sum = fold(hub_all, tuple(range(x_size)), base=None)
    mixed = mixed_sums(recv_index, arrived, hub_sum, degree)
    full_mixed = lax.all_gather(mixed, REP, axis=0, tiled=True)

    output, d_full, mixed_grad, tail_back, w_self_rows, bias_rows = layer(
        place, recv_index, degree, full_mixed, own_blocks, sizes, parts, slots
    )
    tail_len = slots // 2
    first = swap(tail_back.reshape(parts, tail_len + 8, 128), DOM)

    hub_terms = partial(
        hub_grad_terms, *hub_at, mixed_grad, bias_rows, tiles, sizes=sizes, blocks=blocks
    )
    far_steps = (2, 1, 3)
    terms = [shift(term, "x", k) for term, k in zip(hub_terms(far_steps), far_steps)]
    terms = list(hub_terms((0,))) + terms
    sums = jnp.sum(first[:, tail_len:].astype(F32), axis=0)
    second = swap(pack_rows(terms, sums), PLANE)

    base = tail_grads(send_index, first, w_self_rows, d_full, tail_len)
    grad_features, grad_w_self, grad_w_neigh, grad_bias = finish(second, base, full_width)
    return (output, grad_features, grad_w_self.T, grad_w_neigh.T, grad_bias[0])


def solution(mesh):
    grid = (4, 4, mesh.shape["dom"] // 16, 2, 2)
    parted = Mesh(mesh.devices.reshape(grid), DOM + REP)
    in_specs = (
        P(REP, DOM),
        P(DOM, None, None, None),
        P(DOM, None),
        P(DOM, None),
        P(DOM, None, None),
        P(DOM, None),
        P(DOM, None, None),
        P(DOM),
        P(None, REP),
        P(None, REP),
        P(REP),
        P(REP, DOM),
    )
    out_specs = (P(REP, DOM), P(REP, DOM), P(None, REP), P(None, REP), P(REP))
    return jax.shard_map(local, mesh=parted, in_specs=in_specs, out_specs=out_specs, check_vma=False)
```

```python
from functools import partial

import jax
import jax.numpy as jnp
from jax import lax
from jax.experimental import pallas as pl
from jax.experimental.pallas import tpu as pltpu
from jax.sharding import Mesh
from jax.sharding import PartitionSpec as P

BF = jnp.bfloat16
F32 = jnp.float32
BOTH_ROWS = (((0,), (0,)), ((), ()))
BOTH_COLS = (((1,), (1,)), ((), ()))
DOM = ("yh", "x", "z")
PLANE = ("yh", "z")
REP = ("yl", "core")
SMEM = pl.BlockSpec(memory_space=pltpu.SMEM)
VMEM = pl.BlockSpec(memory_space=pltpu.VMEM)
MIB = 1024 * 1024
VMEM_LIMIT = 16 * MIB


def mm(a, b, dims):
    return lax.dot_general(a, b, dims, preferred_element_type=F32)


def swap(pieces, axis):
    return lax.all_to_all(pieces, axis, split_axis=0, concat_axis=0, tiled=True)


def shift(values, axis, step):
    size = lax.axis_size(axis)
    return lax.ppermute(values, axis, [(i, (i + step) % size) for i in range(size)])


def call(kernel, out_shape, in_specs, scratch, name, flops, mib, limit=VMEM_LIMIT):
    outs = VMEM if isinstance(out_shape, jax.ShapeDtypeStruct) else [VMEM] * len(out_shape)
    return pl.pallas_call(
        kernel,
        out_shape=out_shape,
        in_specs=in_specs,
        out_specs=outs,
        scratch_shapes=scratch,
        compiler_params=pltpu.CompilerParams(vmem_limit_bytes=limit),
        cost_estimate=pl.CostEstimate(flops=flops, bytes_accessed=mib * MIB, transcendentals=0),
        name=name,
    )


def slot_rows(index):
    parts, slots = index.shape
    return index.reshape(parts, 2, slots // 2).transpose(1, 0, 2).reshape(2, -1)


def pick_slots(index_ref, source, step):
    width, nodes = source.shape
    low_size = 256
    high_size = nodes // low_size
    split = jnp.concatenate(
        [source[:, i * low_size : (i + 1) * low_size] for i in range(high_size)], axis=0
    )
    low_ids = lax.broadcasted_iota(jnp.int32, (low_size, step), 0)
    for start in range(0, index_ref.shape[1], step):
        halves = []
        for h in range(2):
            index = index_ref[h : h + 1, start : start + step]
            hits = jnp.where(low_ids == (index & (low_size - 1)), 1.0, 0.0).astype(BF)
            found = jnp.dot(split, hits, preferred_element_type=F32)
            high = jnp.broadcast_to(index >> 8, (width, step))
            kept = jnp.zeros((width, step), F32)
            for i in range(high_size):
                kept = jnp.where(high == i, found[i * width : (i + 1) * width], kept)
            halves.append(kept)
        yield start, jnp.concatenate(halves, axis=0).T


def gather_kernel(index_ref, source_ref, out_ref):
    rows, step = out_ref.shape[1], 256
    for start, block in pick_slots(index_ref, source_ref[...], step):
        first = start // rows
        out_ref[first : first + step // rows] = block.reshape(-1, rows, 128).astype(BF)


def gather_slots(index, source, parts, slots):
    return call(
        gather_kernel,
        jax.ShapeDtypeStruct((parts, slots // 2, 128), BF),
        [VMEM, VMEM],
        [],
        "tail_rows_out",
        2 * parts * slots * 256 * 256,
        2,
    )(index, source)


def layer_kernel(sizes, place_ref, index_ref, degree_ref, mixed_ref, *refs):
    block_refs, refs = refs[:4], refs[4:]
    outs, (bias_ref, *held), (feat, low_rows, sems) = refs[:5], refs[5:11], refs[11:]
    output_ref, d_ref, grad_ref, send_ref, self_ref = held
    x_size, z_size = sizes
    width, nodes = output_ref.shape
    full = mixed_ref.shape[0]
    half = full // 2
    copies = [pltpu.make_async_copy(h, o, sems.at[i]) for i, (h, o) in enumerate(zip(held, outs))]
    own = place_ref[0]
    rows_of = [pl.ds(pl.multiple_of(place_ref[i] * width, width), width) for i in range(4)]
    for at, ref in zip(rows_of, block_refs):
        feat[at, :] = ref[:, :nodes]
        low_rows[at, :] = ref[:, 2 * nodes : 2 * nodes + 2 * full].astype(F32)

    own_weights = []
    for first in (0, full):
        rows = low_rows[:, first : first + width]
        for k in range(1, 4):
            start = first + k * width
            rows = jnp.where(own == k, low_rows[:, start : start + width], rows)
        own_weights.append(rows.T.astype(BF))
    self_ref[...] = own_weights[0]
    copies[4].start()

    mixed, full_feat = mixed_ref[...], feat[...]
    for i, (at, ref) in enumerate(zip(rows_of, block_refs)):
        first = 2 * nodes
        bias = ref[:, first + 2 * full :].astype(F32)
        pre = jnp.dot(ref[:, first : first + full], full_feat, preferred_element_type=F32)
        pre = pre + jnp.dot(
            ref[:, first + full : first + 2 * full], mixed, preferred_element_type=F32
        )
        pre = pre + jnp.sum(bias, axis=1, keepdims=True)
        sigma = jax.nn.sigmoid(pre)
        slope = sigma * (1.0 + pre * (1.0 - sigma))
        d_part = (ref[:, nodes : 2 * nodes].astype(F32) * slope).astype(BF)
        d_ref[at, :] = d_part
        if i == 0:
            d_pre = d_part
            output_ref[...] = (pre * sigma).astype(BF)
            copies[0].start()
    copies[1].start()

    grad = jnp.dot(own_weights[1], d_ref[...], preferred_element_type=F32).astype(BF)
    grad_ref[...] = grad
    copies[2].start()
    scaled = (grad.astype(F32) / degree_ref[...].astype(F32)).astype(BF)

    made = []
    for source in (full_feat, mixed):
        total = mm(source, d_pre, BOTH_COLS)
        total = jnp.concatenate([total[:half], total[half:]], axis=1)
        made.append(total.reshape(-1, z_size // 2, 16, 128))
    made = jnp.concatenate(made, axis=0)
    bias = mm(jnp.ones((bias_ref.shape[0], nodes), BF), d_pre, BOTH_COLS)
    bias = jnp.concatenate([bias, bias], axis=1)
    high = bias.astype(BF).astype(F32)
    row = lax.broadcasted_iota(jnp.int32, bias.shape, 0)
    bias_ref[...] = jnp.where(row == 0, high, jnp.where(row == 1, bias - high, 0.0)).astype(BF)

    rows = (send_ref.shape[1] - 16) // 2
    step = 256
    for start, block in pick_slots(index_ref, scaled, step):
        block = block.reshape(-1, 2, rows, 128)
        count = block.shape[0]
        first = start // (2 * rows)
        weight = made[first // (x_size * z_size // 2)]
        weight = jnp.concatenate([weight] * (count // weight.shape[0]), axis=0)
        block = jnp.concatenate([block[:, 0], weight[:, :8], block[:, 1], weight[:, 8:]], axis=1)
        send_ref[first : first + count] = block.astype(BF)
    copies[3].start()
    for copy in copies:
        copy.wait()


def layer(place, index, degree, mixed, own_blocks, sizes, parts, slots):
    full, nodes = mixed.shape
    width = own_blocks[0].shape[0]
    held = [
        (width, nodes),
        (full, nodes),
        (width, nodes),
        (parts // 2, slots + 16, 128),
        (width, full),
    ]
    bias_shape = (width // 2, 128)
    return pl.pallas_call(
        partial(layer_kernel, sizes),
        out_shape=[jax.ShapeDtypeStruct(shape, BF) for shape in [*held, bias_shape]],
        in_specs=[SMEM] + [VMEM] * 7,
        out_specs=[pl.BlockSpec(memory_space=pltpu.HBM)] * len(held) + [VMEM],
        scratch_shapes=[pltpu.VMEM(shape, BF) for shape in held]
        + [
            pltpu.VMEM((full, nodes), BF),
            pltpu.VMEM((full, 2 * full), F32),
            pltpu.SemaphoreType.DMA((len(held),)),
        ],
        compiler_params=pltpu.CompilerParams(vmem_limit_bytes=60 * MIB),
        cost_estimate=pl.CostEstimate(flops=1000 * MIB, bytes_accessed=4 * MIB, transcendentals=0),
        name="layer",
    )(place, index, degree, mixed, *own_blocks)


def sum_slots(index_ref, arrived_ref, rows, start, size):
    parts = arrived_ref.shape[0]
    flat = arrived_ref[:, :rows, :].reshape(parts * rows, 128)
    ids = lax.broadcasted_iota(jnp.int32, (size, parts * rows), 0) + start
    sums = []
    for h in range(2):
        hits = jnp.where(ids == index_ref[h : h + 1, :], 1.0, 0.0).astype(BF)
        sums.append(jnp.dot(hits, flat, preferred_element_type=F32))
    return sums[0].T[:64] + sums[1].T[64:]


def mixed_kernel(rows, index_ref, arrived_ref, hub_ref, degree_ref, out_ref):
    size = 256
    for start in range(0, out_ref.shape[1], size):
        at = slice(start, start + size)
        tail = sum_slots(index_ref, arrived_ref, rows, start, size)
        out_ref[:, at] = (hub_ref[:, at] + tail / degree_ref[:, at].astype(F32)).astype(BF)


def mixed_sums(index, arrived, hub_sum, degree):
    parts, rows, _ = arrived.shape
    width, nodes = hub_sum.shape
    return call(
        partial(mixed_kernel, rows),
        jax.ShapeDtypeStruct((width, nodes), BF),
        [VMEM] * 4,
        [],
        "mixed",
        4 * parts * rows * nodes * 128,
        2,
    )(index, arrived, hub_sum, degree)


def tail_grad_kernel(rows, index_ref, arrived_ref, weight_ref, d_ref, out_ref):
    size = 256
    for start in range(0, out_ref.shape[1], size):
        at = slice(start, start + size)
        tail = sum_slots(index_ref, arrived_ref, rows, start, size)
        direct = jnp.dot(weight_ref[...], d_ref[:, at], preferred_element_type=F32)
        out_ref[:, at] = direct + tail


def tail_grads(index, arrived, weight, d_full, rows):
    parts = arrived.shape[0]
    width, nodes = weight.shape[0], d_full.shape[1]
    return call(
        partial(tail_grad_kernel, rows),
        jax.ShapeDtypeStruct((width, nodes), F32),
        [VMEM] * 4,
        [],
        "tail_grads",
        4 * parts * rows * nodes * 128,
        2,
    )(index, arrived, weight, d_full)


def own_kernel(feat_ref, cot_ref, self_ref, neigh_ref, bias_ref, out_ref):
    first = 0
    for ref in (feat_ref, cot_ref, self_ref, neigh_ref, bias_ref):
        out_ref[:, first : first + ref.shape[1]] = ref[...].astype(BF)
        first += ref.shape[1]


def own_block(*pieces):
    columns = sum(piece.shape[1] for piece in pieces)
    return call(
        own_kernel,
        jax.ShapeDtypeStruct((pieces[0].shape[0], columns), BF),
        [VMEM] * len(pieces),
        [],
        "own_block",
        0,
        0,
    )(*pieces)


def three_terms(values):
    high = lax.reduce_precision(values, 8, 7)
    rest = values - high
    middle = lax.reduce_precision(rest, 8, 7)
    return [high.astype(BF), middle.astype(BF), (rest - middle).astype(BF)]


def tile_index(x_ref, k, sizes, yh, z, sign):
    x_size, z_size = sizes
    x = lax.rem(x_ref[0] + (sign * k) % x_size, x_size)
    return (yh * x_size + x) * z_size + z


def fold_kernel(steps, sizes, has_base, x_ref, block_ref, mask_ref, *refs):
    hub_refs, (tile_ref, *base_ref, out_ref, total) = refs[: len(steps)], refs[len(steps) :]
    blocks = total.shape[0] - 1
    half = hub_refs[0].shape[1]
    lanes = lax.broadcasted_iota(jnp.int32, (half, 128), 1)
    first = (lanes < 64).astype(F32).astype(BF)
    second = (lanes >= 64).astype(F32).astype(BF)
    for b in range(blocks):
        at = slice(b * 128, (b + 1) * 128)
        total[b] = base_ref[0][:, at] if has_base else jnp.zeros_like(total[b])
    total[blocks] = jnp.zeros_like(total[blocks])
    z_size = sizes[1]
    for k, hub_ref in zip(steps, hub_refs):

        @pl.loop(0, hub_ref.shape[0] // z_size)
        def _(yh):
            for z in range(z_size):
                tile = tile_index(x_ref, k, sizes, yh, z, -1)
                rows = hub_ref[yh * z_size + z]
                weights = tile_ref[tile]
                product = jnp.dot(
                    jnp.concatenate([rows * first, rows * second], axis=0),
                    jnp.concatenate([weights, weights], axis=0),
                    preferred_element_type=F32,
                )
                dest = jnp.where(mask_ref[tile] > 0, block_ref[tile], blocks)
                total[dest] = total[dest] + product

    for b in range(blocks):
        out_ref[:, b * 128 : (b + 1) * 128] = total[b]


def fold_hubs(x_index, block, mask, hubs, steps, tiles, sizes, blocks, base):
    width = 2 * hubs[0].shape[1]
    bases = [] if base is None else [base]
    return call(
        partial(fold_kernel, steps, sizes, base is not None),
        jax.ShapeDtypeStruct((width, blocks * 128), F32),
        [SMEM, SMEM, SMEM] + [VMEM] * (len(hubs) + 1 + len(bases)),
        [pltpu.VMEM((blocks + 1, width, 128), F32)],
        "hub_sums",
        tiles.size * width * len(hubs),
        4,
    )(x_index, block, mask, *hubs, tiles, *bases)


def hub_grad_kernel(steps, sizes, x_ref, block_ref, mask_ref, grad_ref, bias_ref, tile_ref, *refs):
    *out_refs, blocked = refs
    blocks = blocked.shape[0] - 1
    for b in range(blocks):
        blocked[b] = grad_ref[:, b * 128 : (b + 1) * 128]
    blocked[blocks] = jnp.zeros_like(blocked[blocks])
    count, half, _ = out_refs[0].shape
    first = lax.broadcasted_iota(jnp.int32, (half, 128), 1) < 64
    z_size = sizes[1]
    for k, out_ref in zip(steps, out_refs):
        out_ref[count - 1] = bias_ref[...]

        @pl.loop(0, count // z_size)
        def _(yh):
            for z in range(0, z_size, 2):
                tile = tile_index(x_ref, k, sizes, yh, z, 1)
                dests = [
                    jnp.where(mask_ref[tile + i] > 0, block_ref[tile + i], blocks) for i in range(2)
                ]
                product = mm(
                    jnp.concatenate([blocked[dest] for dest in dests], axis=0),
                    jnp.concatenate([tile_ref[tile], tile_ref[tile + 1]], axis=0),
                    BOTH_COLS,
                )
                turned = pltpu.roll(product[half : 3 * half], 64, 1)
                place = yh * z_size + z
                out_ref[place] = jnp.where(first, product[:half], turned[:half]).astype(BF)
                out_ref[place + 1] = jnp.where(first, turned[half:], product[3 * half :]).astype(BF)


def hub_grad_terms(x_index, block, mask, grad, bias, tiles, steps, sizes, blocks):
    width = grad.shape[0]
    shape = (tiles.shape[0] // sizes[0] + 1, width // 2, 128)
    return call(
        partial(hub_grad_kernel, steps, sizes),
        [jax.ShapeDtypeStruct(shape, BF) for _ in steps],
        [SMEM, SMEM, SMEM, VMEM, VMEM, VMEM],
        [pltpu.VMEM((blocks + 1, width, 128), BF)],
        "hub_grad_terms",
        tiles.size * width * len(steps),
        4,
    )(x_index, block, mask, grad, bias, tiles)


def pack_kernel(*refs):
    *term_refs, sum_ref, out_ref = refs
    count, half = out_ref.shape[0], term_refs[0].shape[1]
    total = term_refs[0][...].astype(F32)
    for ref in term_refs[1:]:
        total = total + ref[...].astype(F32)
    out_ref[:, :half] = total[:count].astype(BF)
    bias = total[count]
    bias = jnp.broadcast_to(bias[0:1] + bias[1:2], (8, 128))
    high = bias.astype(BF).astype(F32)
    row = lax.broadcasted_iota(jnp.int32, (8, 128), 0)
    bias = jnp.where(row == 0, high, jnp.where(row == 1, bias - high, 0.0))
    extra = jnp.concatenate([sum_ref[...], bias], axis=0).astype(BF)
    out_ref[:, half:] = jnp.broadcast_to(extra[None], (count, 16, 128))


def pack_rows(terms, sums):
    count, half, _ = terms[0].shape
    return call(
        pack_kernel,
        jax.ShapeDtypeStruct((count - 1, half + 16, 128), BF),
        [VMEM] * (len(terms) + 1),
        [],
        "hub_grads_over_x",
        MIB,
        2,
    )(*terms, sums)


def final_kernel(second_ref, base_ref, out_ref, self_ref, neigh_ref, bias_ref):
    half = out_ref.shape[0] // 2
    hub = jnp.sum(second_ref[:, :half].astype(F32), axis=0)
    hub = jnp.concatenate([hub, pltpu.roll(hub, 64, 1)], axis=0)
    lane = lax.broadcasted_iota(jnp.int32, hub.shape, 1)
    out_ref[...] = base_ref[...] + jnp.where(lane < 64, hub, 0.0)
    extra = second_ref[:, half:].astype(F32)
    grads = extra[:, :8].reshape(-1, 128)
    rows = grads.shape[0] // 2
    for place, ref in enumerate((self_ref, neigh_ref)):
        turned = grads[place * rows : (place + 1) * rows].T
        ref[...] = jnp.concatenate([turned[:64], turned[64:]], axis=1)
    bias = jnp.sum(extra[:, 8:], axis=0)
    bias_ref[...] = (bias[0:1] + bias[1:2])[:, : bias_ref.shape[1]]


def finish(second, base, full):
    width, nodes = base.shape
    hub_part = pl.BlockSpec((width, 128), lambda i: (0, 0))
    return pl.pallas_call(
        final_kernel,
        out_shape=[
            jax.ShapeDtypeStruct((width, nodes), F32),
            jax.ShapeDtypeStruct((width, full), F32),
            jax.ShapeDtypeStruct((width, full), F32),
            jax.ShapeDtypeStruct((1, width), F32),
        ],
        grid=(1,),
        in_specs=[pl.BlockSpec(second.shape, lambda i: (0, 0, 0)), hub_part],
        out_specs=[hub_part]
        + [pl.BlockSpec((width, full), lambda i: (0, 0))] * 2
        + [pl.BlockSpec((1, width), lambda i: (0, 0))],
        input_output_aliases={1: 0},
        compiler_params=pltpu.CompilerParams(vmem_limit_bytes=VMEM_LIMIT),
        cost_estimate=pl.CostEstimate(flops=MIB, bytes_accessed=MIB, transcendentals=0),
        name="gradients",
    )(second, base)


def local(
    features,
    hub_weight,
    hub_block,
    hub_mask,
    tail_rows,
    tail_count,
    tail_target,
    degree,
    w_self,
    w_neigh,
    out_bias,
    cotangent,
):
    width, nodes = features.shape
    parts, hubs, tile_len = hub_weight.shape[1:]
    slots = tail_rows.shape[2]
    half_width = width // 2
    blocks = nodes // tile_len
    full_width = w_self.shape[0]
    x_size, z_size = lax.axis_size("x"), lax.axis_size("z")
    sizes = (x_size, z_size)
    plane = parts // x_size
    x_index = lax.axis_index("x")[None]
    tiles = hub_weight[0]
    hub_at = (x_index, hub_block[0], hub_mask[0])
    degree = degree[None, :]

    hub_piece = jnp.concatenate([features[:half_width, :hubs], features[half_width:, :hubs]], axis=1)
    hub_send = jnp.broadcast_to(hub_piece[None], (plane, half_width, 128))
    hub_plane = swap(hub_send, PLANE)

    slot_live = jnp.arange(slots, dtype=jnp.int32)[None, :] < tail_count[0][:, None]
    send_index = slot_rows(jnp.where(slot_live, tail_rows[0], -1))
    recv_index = slot_rows(tail_target[0])
    bias_terms = jnp.stack(three_terms(out_bias), axis=1)
    bias_terms = jnp.pad(bias_terms, ((0, 0), (0, 128 - bias_terms.shape[1])))
    feat_own, send_index, _ = lax.optimization_barrier((features, send_index, hub_send))
    own = own_block(feat_own, cotangent, w_self.T, w_neigh.T, bias_terms)
    across = shift(own, "core", 1)
    tail_send = gather_slots(send_index, features, parts, slots)
    hub_plane, tail_send, recv_index, own, across = lax.optimization_barrier(
        (hub_plane, tail_send, recv_index, own, across)
    )
    arrived = swap(tail_send, DOM)
    hub_all = [hub_plane] + [shift(hub_plane, "x", k) for k in range(1, x_size)]
    near = shift(own, "yl", 1)
    place = lax.axis_index(REP) ^ jnp.array([0, 2, 1, 3], jnp.int32)

    fold = partial(fold_hubs, *hub_at, tiles=tiles, sizes=sizes, blocks=blocks)
    hub_sum = fold(hub_all[:2], (0, 1), base=None)
    hub_sum, near = lax.optimization_barrier((hub_sum, near))
    own_blocks = [own, near, across, shift(near, "core", 1)]
    hub_sum = fold(hub_all[2:], (2, 3), base=hub_sum)
    mixed = mixed_sums(recv_index, arrived, hub_sum, degree)
    full_mixed = lax.all_gather(mixed, REP, axis=0, tiled=True)

    output, d_full, mixed_grad, tail_back, w_self_rows, bias_rows = layer(
        place, recv_index, degree, full_mixed, own_blocks, sizes, parts, slots
    )
    tail_len = slots // 2
    first = swap(tail_back.reshape(parts, tail_len + 8, 128), DOM)

    hub_terms = partial(
        hub_grad_terms, *hub_at, mixed_grad, bias_rows, tiles, sizes=sizes, blocks=blocks
    )
    far_steps = (2, 1, 3)
    terms = [shift(term, "x", k) for term, k in zip(hub_terms(far_steps), far_steps)]
    terms = list(hub_terms((0,))) + terms
    sums = jnp.sum(first[:, tail_len:].astype(F32), axis=0)
    second = swap(pack_rows(terms, sums), PLANE)

    base = tail_grads(send_index, first, w_self_rows, d_full, tail_len)
    grad_features, grad_w_self, grad_w_neigh, grad_bias = finish(second, base, full_width)
    return (output, grad_features, grad_w_self.T, grad_w_neigh.T, grad_bias[0])


def solution(mesh):
    grid = (4, 4, mesh.shape["dom"] // 16, 2, 2)
    parted = Mesh(mesh.devices.reshape(grid), DOM + REP)
    in_specs = (
        P(REP, DOM),
        P(DOM, None, None, None),
        P(DOM, None),
        P(DOM, None),
        P(DOM, None, None),
        P(DOM, None),
        P(DOM, None, None),
        P(DOM),
        P(None, REP),
        P(None, REP),
        P(REP),
        P(REP, DOM),
    )
    out_specs = (P(REP, DOM), P(REP, DOM), P(None, REP), P(None, REP), P(REP))
    return jax.shard_map(local, mesh=parted, in_specs=in_specs, out_specs=out_specs, check_vma=False)
```
